32 devices in a mesh: ens: 2 (over y), comp: 4 (over z), lat: 2 (over x), lon: 2 (over core).
Axes of the slice: x: 2, y: 2, z: 4, core: 2. Of those that a mesh axis runs over, the one named last changes fastest.
Arguments:
- spectrum: float32 [2304, 16, 256], P(('ens', 'comp'), 'lat', 'lon'), parts along dimension 0, may hold values from 0 to 2
- sea_mask: int32 [16, 256], P('lat', 'lon'), may hold values 0 or 1
- depth_class: int32 [16, 256], P('lat', 'lon'), may hold values from 0 to 15
- current_class: int32 [16, 256], P('lat', 'lon'), may hold values from 0 to 15
- speed_table: float32 [16, 32], replicated, may hold values from 0.1 to 0.5
- current_table: float32 [16, 2], replicated, may hold values from -0.14 to 0.14
- coupling: float32 [1152], replicated, may hold values from 0.05 to 0.5
- quad_index: int32 [2, 1152, 4], replicated, may hold values from 0 to 1151, as said below
- quad_weight: float32 [2, 1152, 4], replicated, may hold values from 0 to 1, as said below
Outputs:
- spectrum_out: float32 [2304, 16, 256], P(('ens', 'comp'), 'lat', 'lon'), parts along dimension 0
The draws below stay inside these ranges and needn't reach their ends.
There are 2 independent parts, one for each index of `ens`. The reference program is written for one: setup_inputs(seed, part) draws one part's arguments, and reference() takes and returns one part's arrays. A program takes and returns all parts, laid end to end along the dimension named above; an argument that names none is the same for every part. Nothing has to cross between parts.
Inputs may be any that keep to these rules, and one draw needn't show every extreme that they name: `quad_index`: for each side (0 plus, 1 minus) and component k the four entries are distinct components: two adjacent frequencies crossed with two adjacent directions, directions counted modulo 36; a component's number is its frequency times 36 plus its direction. `quad_weight`: the four weights of each side and component are non-negative and sum to one.
All inputs are finite; a program needn't handle non-finite values. No bound on the sum of `sea_mask` on one device may be relied on, other than what follows from the above.
Results may differ from the reference program's by a relative error of at most 0.002.
Values sent between devices are 32-bit elements; how exact they have to be, the bound alone decides.
No kernel may reach another device: no remote copies, remote signals or barrier semaphores. Data moves between devices by JAX's collectives and lax.ppermute only.
A program may use at most 64 MiB of HBM per device.

```python
import math
import jax
import jax.numpy as jnp
from jax import lax

NDIR = 36
NFREQ = 32
K = 1152
SUBSTEPS = 4
NDEPTH = 16
NCUR = 16
NLAT = 16
NLON = 256


def quad_corners(key):
    comp_total = NDIR * NFREQ
    comp_ids = jnp.arange(comp_total, dtype=jnp.int32)
    freq_ids = comp_ids // NDIR
    dir_ids = comp_ids % NDIR
    freq_key = jax.random.fold_in(key, 101)
    dir_key = jax.random.fold_in(key, 202)
    freq_step = jax.random.randint(freq_key, (2, NFREQ), 1, 3, dtype=jnp.int32)
    dir_step = jax.random.randint(dir_key, (2, NFREQ), 1, max(2, NDIR // 4), dtype=jnp.int32)
    signs = jnp.array([[1], [-1]], dtype=jnp.int32)
    base_freq = jnp.clip(freq_ids[None] + signs * freq_step[:, freq_ids], 0, NFREQ - 2)
    base_dir = jnp.mod(dir_ids[None] + signs * dir_step[:, freq_ids], NDIR)
    next_dir = jnp.mod(base_dir + 1, NDIR)
    corners = [base_freq * NDIR + base_dir, (base_freq + 1) * NDIR + base_dir, base_freq * NDIR + next_dir, (base_freq + 1) * NDIR + next_dir]
    return jnp.stack(corners, axis=-1).astype(jnp.int32)


def draw_quad_index(key, part):
    return quad_corners(key)


def draw_quad_weight(key, part):
    frac_key = jax.random.fold_in(key, 303)
    fracs = jax.random.uniform(frac_key, (2, NDIR * NFREQ, 2), dtype=jnp.float32)
    along_freq = fracs[..., 0]
    along_dir = fracs[..., 1]
    weights = [(1.0 - along_freq) * (1.0 - along_dir), along_freq * (1.0 - along_dir), (1.0 - along_freq) * along_dir, along_freq * along_dir]
    return jnp.stack(weights, axis=-1).astype(jnp.float32)


def plant(result, stream_key, smallest, largest):
    longest = result.shape.index(max(result.shape))
    spots = []
    for shift in (0, 1):
        where = [jax.random.randint(jax.random.fold_in(stream_key, axis), (), 0, length) for axis, length in enumerate(result.shape)]
        where[longest] = (where[longest] + shift) % result.shape[longest]
        spots.append(tuple(where))
    return result.at[spots[0]].set(smallest).at[spots[1]].set(largest)


def levels(rng, dims, shards, least, largest):
    factor_of, own = 1.0, jax.random.fold_in(rng, 6)
    for dim, parts in shards:
        heights = jnp.exp(jax.random.uniform(jax.random.fold_in(own, dim), (parts,), jnp.float32, least / len(shards), largest / len(shards)))
        factor_of = factor_of * jnp.repeat(heights, dims[dim] // parts).reshape([-1 if axis == dim else 1 for axis in range(len(dims))])
    return factor_of


def setup_inputs(seed: int = 0, part: int = 0) -> dict:
    arg_keys = jax.random.split(jax.random.key(seed), 10)
    part_splits = jax.random.split(jax.random.fold_in(arg_keys[9], part), 10)
    return {
        "spectrum": jnp.clip(2.0 * jax.random.uniform(part_splits[0], (K, NLAT, NLON), jnp.float32) ** levels(part_splits[0], (K, NLAT, NLON), ((0, 4), (1, 2), (2, 2)), -0.2, 0.2), 0.0, 2.0),
        "sea_mask": plant((jax.random.randint(arg_keys[1], (NLAT, NLON), 0, 4) < 3).astype(jnp.int32), jax.random.fold_in(arg_keys[1], 1), 0, 1),
        "depth_class": plant(jax.random.randint(arg_keys[2], (NLAT, NLON), 0, NDEPTH), jax.random.fold_in(arg_keys[2], 1), 0, NDEPTH - 1).astype(jnp.int32),
        "current_class": plant(jax.random.randint(arg_keys[3], (NLAT, NLON), 0, NCUR), jax.random.fold_in(arg_keys[3], 1), 0, NCUR - 1).astype(jnp.int32),
        "speed_table": jnp.clip(jax.random.uniform(arg_keys[4], (NDEPTH, NFREQ), jnp.float32, 0.1, 0.5), 0.1, 0.5),
        "current_table": jnp.clip(jax.random.uniform(arg_keys[5], (NCUR, 2), jnp.float32, -0.14, 0.14), -0.14, 0.14),
        "coupling": jnp.clip(jnp.exp(jax.random.uniform(arg_keys[6], (K,), jnp.float32, math.log(0.05), math.log(0.5))), 0.05, 0.5),
        "quad_index": draw_quad_index(jax.random.fold_in(arg_keys[9], 71), part),
        "quad_weight": draw_quad_weight(jax.random.fold_in(arg_keys[9], 71), part),
    }


plus_factor = 0.4096
minus_factor = 3.160494
cross_factor = 2.007843


def minmod(former, latter):
    return jnp.maximum(0.0, jnp.minimum(former, latter)) + jnp.minimum(0.0, jnp.maximum(former, latter))


def part_of(array, start, length, axis):
    return lax.slice_in_dim(array, start, start + length, axis=axis)


def face_flux(energy, cour, wet_cells, axis):
    length = energy.shape[axis]
    differences = part_of(energy, 1, length - 1, axis) - part_of(energy, 0, length - 1, axis)
    slopes = minmod(part_of(differences, 1, length - 2, axis), part_of(differences, 0, length - 2, axis))
    face_count = length - 3
    face_speed = 0.5 * (part_of(cour, 1, face_count, axis) + part_of(cour, 2, face_count, axis)) * (part_of(wet_cells, 1, face_count, axis) * part_of(wet_cells, 2, face_count, axis))
    upwind_left = part_of(energy, 1, face_count, axis) + 0.5 * (1.0 - face_speed) * part_of(slopes, 0, face_count, axis)
    upwind_right = part_of(energy, 2, face_count, axis) - 0.5 * (1.0 + face_speed) * part_of(slopes, 1, face_count, axis)
    return jnp.maximum(face_speed, 0.0) * upwind_left + jnp.minimum(face_speed, 0.0) * upwind_right


def advance(energy, cour_x, cour_y, wet_cells):
    flux_lon = face_flux(energy[:, 2:-2, :], cour_x[:, 2:-2, :], wet_cells[:, 2:-2, :], 2)
    flux_lat = face_flux(energy[:, :, 2:-2], cour_y[:, :, 2:-2], wet_cells[:, :, 2:-2], 1)
    return energy[:, 2:-2, 2:-2] - (flux_lon[:, :, 1:] - flux_lon[:, :, :-1]) - (flux_lat[:, 1:, :] - flux_lat[:, :-1, :])


def courant(comp_ids, depth_grid, current_grid, speed_table, current_table):
    n_depth, n_freq = speed_table.shape
    n_current = current_table.shape[0]
    depth_hot = (depth_grid[None] == jnp.arange(n_depth, dtype=jnp.int32)[:, None, None]).astype(jnp.float32)
    current_hot = (current_grid[None] == jnp.arange(n_current, dtype=jnp.int32)[:, None, None]).astype(jnp.float32)
    freq_hot = ((comp_ids // NDIR)[:, None] == jnp.arange(n_freq, dtype=jnp.int32)[None, :]).astype(jnp.float32)
    comp_speed = jnp.dot(freq_hot, speed_table.T, precision=lax.Precision.HIGHEST)
    speeds = jnp.einsum("kn,nhw->khw", comp_speed, depth_hot, precision=lax.Precision.HIGHEST)
    current_uv = jnp.einsum("nc,nhw->chw", current_table, current_hot, precision=lax.Precision.HIGHEST)
    angles = (2.0 * math.pi / NDIR) * (comp_ids % NDIR).astype(jnp.float32)
    cour_x = speeds * jnp.cos(angles)[:, None, None] + current_uv[0]
    cour_y = speeds * jnp.sin(angles)[:, None, None] + current_uv[1]
    return cour_x, cour_y


def dense_kernel(table_index, table_weight):
    comp_total = table_index.shape[0]
    columns = jnp.arange(comp_total, dtype=jnp.int32)[None, :]
    weights = table_weight.astype(jnp.bfloat16)
    kernel = jnp.where(columns == table_index[:, 3:4], weights[:, 3:4], jnp.zeros((), jnp.bfloat16))
    for corner in (2, 1, 0):
        kernel = jnp.where(columns == table_index[:, corner:corner + 1], weights[:, corner:corner + 1], kernel)
    return kernel


def interact(energy, kernel_plus, kernel_minus, coupling):
    energy_low = energy.astype(jnp.bfloat16)
    plus_side = jnp.dot(kernel_plus, energy_low, preferred_element_type=jnp.float32)
    minus_side = jnp.dot(kernel_minus, energy_low, preferred_element_type=jnp.float32)
    source = coupling[:, None] * (energy * energy * (plus_factor * plus_side + minus_factor * minus_side) - cross_factor * energy * plus_side * minus_side)
    source_low = source.astype(jnp.bfloat16)
    contract = (((0,), (0,)), ((), ()))
    net_gain = lax.dot_general(kernel_plus, source_low, contract, preferred_element_type=jnp.float32) + lax.dot_general(kernel_minus, source_low, contract, preferred_element_type=jnp.float32) - 2.0 * source
    return energy + net_gain / (1.0 + jnp.abs(net_gain))


def pad_grid(grid_field, rim_width):
    grid_field = jnp.pad(grid_field, ((0, 0), (rim_width, rim_width), (0, 0)))
    return jnp.concatenate([grid_field[:, :, -rim_width:], grid_field, grid_field[:, :, :rim_width]], axis=2)


def reference(spectrum, sea_mask, depth_class, current_class, speed_table, current_table, coupling, quad_index, quad_weight):
    comp_total = NDIR * NFREQ
    wet_cells = sea_mask.astype(jnp.float32)[None]
    wet_pad = pad_grid(wet_cells, 2)
    depth_pad = pad_grid(depth_class[None], 2)[0]
    current_pad = pad_grid(current_class[None], 2)[0]

    def propagate(freq_block):
        comp_ids = freq_block * NDIR + jnp.arange(NDIR, dtype=jnp.int32)
        energy = lax.dynamic_slice_in_dim(spectrum, freq_block * NDIR, NDIR, 0) * wet_cells
        cour_x, cour_y = courant(comp_ids, depth_pad, current_pad, speed_table, current_table)
        for substep in range(SUBSTEPS):
            energy = advance(pad_grid(energy, 2), cour_x, cour_y, wet_pad)
        return energy

    propagated = lax.map(propagate, jnp.arange(NFREQ, dtype=jnp.int32)).reshape(comp_total, NLAT * NLON)
    kernel_plus = dense_kernel(quad_index[0], quad_weight[0])
    kernel_minus = dense_kernel(quad_index[1], quad_weight[1])

    def interact_row(lat_row):
        energy = lax.dynamic_slice_in_dim(propagated, lat_row * NLON, NLON, 1)
        return interact(energy, kernel_plus, kernel_minus, coupling)

    rows_out = lax.map(interact_row, jnp.arange(NLAT, dtype=jnp.int32))
    return jnp.transpose(rows_out, (1, 0, 2))
```

```python
import functools
import math

import jax
import jax.numpy as jnp
from jax import lax
from jax.experimental import pallas as pl
from jax.experimental.pallas import tpu as pltpu
from jax.sharding import PartitionSpec as P

NDIR = 36
SUBSTEPS = 4
RIM = 2 * SUBSTEPS
GROUP = 16
CHUNKS = 3

plus_factor = 0.4096
minus_factor = 3.160494
cross_factor = 2.007843

VMEM_LIMIT = 16 * 1024 * 1024
whole = pl.BlockSpec(memory_space=pltpu.VMEM)
scalars = pl.BlockSpec(memory_space=pltpu.SMEM)


def params():
    return pltpu.CompilerParams(vmem_limit_bytes=VMEM_LIMIT)


def cost(micros):
    return pl.CostEstimate(flops=0, bytes_accessed=int(micros * 3.5e6), transcendentals=0)


def chunk_sizes(total):
    groups = total // GROUP
    count = min(CHUNKS, groups)
    return [GROUP * (groups // count + (i < groups % count)) for i in range(count)]


class Window:
    def __init__(self, n_lat, rows):
        self.pair = n_lat == 2
        self.rows = rows
        self.size = 2 * rows + 4 if self.pair else 3 * rows

    def own(self, lat):
        return jnp.where(lat == 0, 2, 2 + self.rows) if self.pair else self.rows

    def received(self, lat):
        if self.pair:
            return [jnp.where(lat == 0, 2 + self.rows, 2)]
        return [0, 2 * self.rows]

    def zeros(self, lat):
        if not self.pair:
            return []
        first = jnp.where(lat == 0, 0, 2 + 2 * self.rows)
        return [first, first + 1]

    def steps(self, lat, substep):
        shrink = 2 * (substep + 1)
        if self.pair:
            return jnp.where(lat == 0, 2, 2 + shrink), 2 * self.rows - shrink
        return shrink, 3 * self.rows - 2 * shrink


def faces_kernel(window, n_lon, place, own, lon_fields, lat_fields, out, fields):
    lat = place[0]
    rows, lanes = own.shape[1], own.shape[2]
    for row in window.zeros(lat):
        fields[row] = jnp.zeros((3, n_lon * lanes), jnp.float32)
    sources = [(window.own(lat), [own] + lon_fields)]
    for offset, blocks in zip(window.received(lat), lat_fields):
        sources.append((offset, blocks))
    for offset, blocks in sources:
        for d, block in enumerate(blocks):
            for f in range(3):
                for row in range(rows):
                    fields[offset + row, f : f + 1, d * lanes : (d + 1) * lanes] = block[f, row : row + 1, :]
    width = n_lon * lanes
    n_class = out.shape[2] // 6
    classes = lax.broadcasted_iota(jnp.int32, (n_class, width), 0).astype(jnp.float32)

    def hots(row):
        wet = fields[row, 0:1, :]
        hot_depth = (classes == fields[row, 1:2, :]).astype(jnp.float32)
        hot_current = (classes == fields[row, 2:3, :]).astype(jnp.float32)
        return wet, jnp.concatenate([hot_depth, hot_current], axis=0)

    def step(row, _):
        wet, hot = hots(row)
        wet_next, hot_next = hots(row + 1)
        east_wet = 0.5 * wet * pltpu.roll(wet, width - 1, 1)
        east = ((hot + pltpu.roll(hot, width - 1, 1)) * east_wet).astype(jnp.bfloat16)
        north = ((hot + hot_next) * (0.5 * wet * wet_next)).astype(jnp.bfloat16)
        span = 2 * n_class
        for copy in range(3):
            out[row, 0, copy * span : (copy + 1) * span, :] = east
            out[row, 1, copy * span : (copy + 1) * span, :] = north
        return 0

    lax.fori_loop(0, window.size - 1, step, 0)
    out[window.size - 1] = jnp.zeros(out.shape[1:], jnp.bfloat16)


def median_zero(a, b):
    return jnp.maximum(jnp.minimum(a, b), jnp.minimum(jnp.maximum(a, b), 0.0))


def flux(u, c, low, high, slope_low, slope_high):
    rising = u > 0.0
    return u * jnp.where(rising, low, high) + c * jnp.where(rising, slope_low, slope_high)


def prop_scratch(window, size, width):
    small = pltpu.VMEM((window.size, GROUP, width), jnp.float32)
    big = pltpu.VMEM((window.size, size, width), jnp.float32)
    return [small, small, big, big, big, big]


def propagate_kernel(
    window, n_lon, n_comp, split, start, head, place, tables, faces, wet, mine, lon_in, lat_in, *refs
):
    outs = refs[:-6]
    energy, other, east_u, east_c, north_u, north_c = refs[-6:]
    lat, comp = place[0], place[1]
    rows, lanes = window.rows, mine.shape[1]
    width = n_lon * lanes
    count = east_u.shape[1]

    def speeds(row, _):
        for which, u_ref, c_ref in ((0, east_u, east_c), (1, north_u, north_c)):
            u = jnp.dot(tables[which], faces[row, which], preferred_element_type=jnp.float32)
            size = jnp.abs(u)
            u_ref[row] = u
            c_ref[row] = 0.5 * size * (1.0 - size)
        return 0

    lax.fori_loop(0, window.size, speeds, 0, unroll=True)

    own = window.own(lat)

    def group(g, _):
        first = pl.multiple_of(g * GROUP, GROUP)
        here = pl.ds(first, GROUP)
        for row in window.zeros(lat):
            energy[row] = jnp.zeros((GROUP, width), jnp.float32)
            other[row] = jnp.zeros((GROUP, width), jnp.float32)
        sources = [(own, [(mine, start)] + [(ref, 3 + start) for ref in lon_in])]
        for offset, blocks in zip(window.received(lat), lat_in):
            sources.append((offset, [(ref, head) for ref in blocks]))
        for offset, blocks in sources:
            for d, (ref, lead) in enumerate(blocks):
                for row in range(rows):
                    at = pl.ds((lead + first) * rows + row, GROUP, stride=rows)
                    sea = wet[offset + row, 0:1, d * lanes : (d + 1) * lanes]
                    energy[offset + row, :, d * lanes : (d + 1) * lanes] = ref[at, :] * sea

        for substep in range(SUBSTEPS):
            base, length = window.steps(lat, substep)
            old, new = (energy, other) if substep % 2 == 0 else (other, energy)
            prior = [old[base + i] for i in (-2, -1, 0, 1)]
            gap = [b - a for a, b in zip(prior, prior[1:])]
            slope_prior, slope_here = median_zero(gap[1], gap[0]), median_zero(gap[2], gap[1])
            south = flux(
                north_u[base - 1, here], north_c[base - 1, here], prior[1], prior[2], slope_prior, slope_here
            )

            def row_step(i, carry):
                south, this, after, gap_after, slope_this = carry
                row = base + i
                beyond = old[row + 2]
                gap_beyond = beyond - after
                slope_after = median_zero(gap_beyond, gap_after)
                north = flux(north_u[row, here], north_c[row, here], this, after, slope_this, slope_after)
                east_cell = pltpu.roll(this, width - 1, 1)
                gap_east = east_cell - this
                gap_west = pltpu.roll(gap_east, 1, 1)
                slope = median_zero(gap_east, gap_west)
                slope_east = pltpu.roll(slope, width - 1, 1)
                east = flux(east_u[row, here], east_c[row, here], this, east_cell, slope, slope_east)
                west = pltpu.roll(east, 1, 1)
                new[row] = this - (east - west) - (north - south)
                return north, after, beyond, gap_beyond, slope_after

            lax.fori_loop(0, length, row_step, (south, prior[2], prior[3], gap[2], slope_here), unroll=True)

        if split:
            share = rows // n_comp
            for r in range(n_comp):
                base = own + lax.rem(comp + r, n_comp) * share
                for d in range(n_lon):
                    for k in range(share):
                        outs[r][d, k, here, :] = energy[base + k, :, d * lanes : (d + 1) * lanes]
        else:
            for row in range(rows):
                for d in range(n_lon):
                    outs[0][row, d, here, :] = energy[own + row, :, d * lanes : (d + 1) * lanes]
        return 0

    lax.fori_loop(0, count // GROUP, group, 0)


def matrix_kernel(index_cols, weight_cols, index_rows, weight_rows, out, out_t):
    height, total = out.shape[1], out.shape[2]
    base = pl.program_id(1) * height

    def step(i, _):
        at = pl.ds(pl.multiple_of(i * GROUP, GROUP), GROUP)
        cols = lax.broadcasted_iota(jnp.int32, (GROUP, total), 1)
        index, weight = index_cols[0, at, :], weight_cols[0, at, :]
        made = jnp.zeros((GROUP, total), jnp.float32)
        for corner in range(4):
            made = jnp.where(cols == index[:, corner : corner + 1], weight[:, corner : corner + 1], made)
        out[0, at, :] = made.astype(jnp.bfloat16)
        rows = base + i * GROUP + lax.broadcasted_iota(jnp.int32, (GROUP, total), 0)
        made = jnp.zeros((GROUP, total), jnp.float32)
        for corner in range(4):
            made = jnp.where(
                rows == index_rows[0, corner : corner + 1, :], weight_rows[0, corner : corner + 1, :], made
            )
        out_t[0, at, :] = made.astype(jnp.bfloat16)
        return 0

    lax.fori_loop(0, height // GROUP, step, 0, unroll=3)


def forward_kernel(sizes, n_lon, matrix, coupling, *refs):
    pieces = refs[:-4]
    energy_out, source_out, source_low_out, low = refs[-4:]
    step = pl.program_id(0)
    block = matrix.shape[1]
    half = block // n_lon
    per_chunk = len(pieces) // len(sizes)
    share, lanes = pieces[0].shape[1], pieces[0].shape[3]

    @pl.when(step == 0)
    def _():
        for s in range(per_chunk - n_lon + 1):
            for d in range(n_lon):
                at = (s * n_lon + d) * half
                for i, size in enumerate(sizes):
                    group = pieces[i * per_chunk : (i + 1) * per_chunk]
                    for k in range(share):
                        part = group[s][0, k] if d == 0 else group[d - n_lon][s, k]
                        energy_out[at : at + size, k * lanes : (k + 1) * lanes] = part
                        low[at : at + size, k * lanes : (k + 1) * lanes] = part.astype(jnp.bfloat16)
                    at += size

    here = pl.ds(pl.multiple_of(step * block, GROUP), block)
    energy = energy_out[here, :]
    plus_side = jnp.dot(matrix[0], low[...], preferred_element_type=jnp.float32)
    minus_side = jnp.dot(matrix[1], low[...], preferred_element_type=jnp.float32)
    source = coupling[...] * (
        energy * energy * (plus_factor * plus_side + minus_factor * minus_side)
        - cross_factor * energy * plus_side * minus_side
    )
    source_out[...] = source
    source_low_out[...] = source.astype(jnp.bfloat16)


def backward_kernel(matrix_t, source_low, energy, source, out):
    gain = (
        jnp.dot(matrix_t[0], source_low[...], preferred_element_type=jnp.float32)
        + jnp.dot(matrix_t[1], source_low[...], preferred_element_type=jnp.float32)
        - 2.0 * source[...]
    )
    result = energy[...] + gain / (1.0 + jnp.abs(gain))
    lanes = out.shape[2]
    for k in range(out.shape[0]):
        out[k] = result[:, k * lanes : (k + 1) * lanes]


def gather_kernel(n_lon, rows, place, *refs):
    pieces, out = refs[:-1], refs[-1]
    comp, lon = place[1], place[2]
    n_comp = len(pieces)
    share = rows // n_comp
    half = pieces[0].shape[1] // n_lon
    for r, piece in enumerate(pieces):
        for k in range(share):
            row = lax.rem(comp + r, n_comp) * share + k
            for d in range(n_lon):
                first = lax.rem(lon + n_lon - d, n_lon) * half
                for i in range(0, half, GROUP):
                    at = pl.ds((first + i) * rows + row, GROUP, stride=rows)
                    out[at, :] = piece[k, d * half + i : d * half + i + GROUP, :]


def turned(array, axis, position):
    return jnp.roll(jnp.flip(array, axis), position + 1, axis)


def local(
    spectrum,
    sea_mask,
    depth_class,
    current_class,
    speed_table,
    current_table,
    coupling,
    quad_index,
    quad_weight,
):
    comps_local, rows, lanes = spectrum.shape
    n_comp, n_lat, n_lon = (lax.axis_size(a) for a in ("comp", "lat", "lon"))
    comp, lat, lon = (lax.axis_index(a) for a in ("comp", "lat", "lon"))
    place = jnp.stack([lat, comp, lon]).astype(jnp.int32)
    half_own = comps_local // n_lon
    half = -(-half_own // GROUP) * GROUP
    sizes = chunk_sizes(half)
    starts = [sum(sizes[:i]) for i in range(len(sizes))]
    window = Window(n_lat, rows)
    width = n_lon * lanes
    split = rows % n_comp == 0

    flat = spectrum.reshape(comps_local * rows, lanes)
    fields = jnp.stack([sea_mask, depth_class, current_class]).astype(jnp.float32)
    fields_flat = fields.reshape(3 * rows, lanes)
    parts = []
    for d in range(n_lon):
        owner = lax.rem(lon + d, n_lon)
        part = lax.dynamic_slice_in_dim(flat, owner * half_own * rows, half_own * rows, 0)
        parts.append(jnp.pad(part, ((0, (half - half_own) * rows), (0, 0))))
    lon_in = []
    for d in range(n_lon - 1, 0, -1):
        lon_in.append(
            lax.ppermute(
                jnp.concatenate([fields_flat, parts[d]]), "lon", [(i, (i + d) % n_lon) for i in range(n_lon)]
            )
        )
    if window.pair:
        moves = [[(0, 1), (1, 0)]]
    else:
        moves = [[(i, i + 1) for i in range(n_lat - 1)], [(i + 1, i) for i in range(n_lat - 1)]]
    lat_in = []
    for i, (start, size) in enumerate(zip(starts, sizes)):
        of_chunk = []
        for move in moves:
            blocks = []
            for d in [0] + list(range(n_lon - 1, 0, -1)):
                block = lax.slice_in_dim(parts[d], start * rows, (start + size) * rows, axis=0)
                if i == 0:
                    block = jnp.concatenate([fields_flat, block])
                pairs = [
                    (a * n_lon + b, to * n_lon + (b + d) % n_lon) for a, to in move for b in range(n_lon)
                ]
                blocks.append(lax.ppermute(block, ("lat", "lon"), pairs))
            of_chunk.append(blocks)
        lat_in.append(of_chunk)

    n_class = speed_table.shape[0]
    head_block = pl.BlockSpec((3, rows, lanes), lambda i: (0, 0, 0))
    lon_heads = [a.reshape(-1, rows, lanes) for a in lon_in]
    lat_heads = [[a.reshape(-1, rows, lanes) for a in blocks] for blocks in lat_in[0]]
    faces, window_fields = pl.pallas_call(
        functools.partial(faces_kernel, window, n_lon),
        grid=(1,),
        out_shape=(
            jax.ShapeDtypeStruct((window.size, 2, 6 * n_class, width), jnp.bfloat16),
            jax.ShapeDtypeStruct((window.size, 3, width), jnp.float32),
        ),
        in_specs=[
            scalars,
            head_block,
            [head_block] * len(lon_heads),
            [[head_block] * len(blocks) for blocks in lat_heads],
        ],
        out_specs=(whole, whole),
        compiler_params=params(),
        cost_estimate=cost(2),
    )(place, fields, lon_heads, lat_heads)

    ids = comp * comps_local + lon * half_own + jnp.arange(half, dtype=jnp.int32)
    freq_hot = ((ids // NDIR)[:, None] == jnp.arange(speed_table.shape[1], dtype=jnp.int32)[None, :]).astype(
        jnp.float32
    )
    speed = jnp.dot(freq_hot, speed_table.T, precision=lax.Precision.HIGHEST)
    angles = 2.0 * math.pi / NDIR * (ids % NDIR).astype(jnp.float32)
    tables = []
    for which, turn in ((0, jnp.cos(angles)), (1, jnp.sin(angles))):
        currents = jnp.broadcast_to(current_table[:, which][None], (half, n_class))
        left = jnp.concatenate([speed * turn[:, None], currents], axis=1)
        levels = []
        for _ in range(3):
            level = lax.reduce_precision(left, 8, 7)
            levels.append(level)
            left = left - level
        tables.append(jnp.concatenate(levels, axis=1).astype(jnp.bfloat16))
    tables = jnp.stack(tables)

    def arranged(array):
        array = array.reshape(array.shape[0], n_comp, n_lon, half_own, array.shape[-1])
        if split:
            array = turned(array, 1, comp)
        return turned(array, 2, lon)

    def position(index):
        of_comp, rest = index // comps_local, index % comps_local
        if split:
            of_comp = lax.rem(comp + n_comp - of_comp, n_comp)
        of_lon = lax.rem(lon + n_lon - rest // half_own, n_lon)
        return (of_comp * n_lon + of_lon) * half + rest % half_own

    padding = ((0, 0), (0, 0), (0, 0), (0, half - half_own), (0, 0))
    total = n_comp * n_lon * half
    block = n_lon * half
    index = jnp.pad(arranged(position(quad_index)), padding, constant_values=-1).reshape(2, total, 4)
    weight = jnp.pad(arranged(quad_weight), padding).reshape(2, total, 4)
    strength = jnp.pad(arranged(coupling[None, :, None]), padding).reshape(total, 1)
    by_rows = pl.BlockSpec((1, block, 4), lambda s, i: (s, i, 0))
    by_cols = pl.BlockSpec((1, 4, total), lambda s, i: (s, 0, 0))
    by_block = pl.BlockSpec((1, block, total), lambda s, i: (s, i, 0))
    matrix, matrix_t = pl.pallas_call(
        matrix_kernel,
        grid=(2, n_comp),
        out_shape=(jax.ShapeDtypeStruct((2, total, total), jnp.bfloat16),) * 2,
        in_specs=[by_rows, by_rows, by_cols, by_cols],
        out_specs=(by_block, by_block),
        compiler_params=params(),
        cost_estimate=cost(10),
    )(index, weight, jnp.swapaxes(index, 1, 2), jnp.swapaxes(weight, 1, 2))

    if split:
        share, span = rows // n_comp, lanes
    else:
        groups = n_comp // rows
        share, span = 1, lanes // groups
    arrived = []
    for i, (start, size) in enumerate(zip(starts, sizes)):
        table = lax.slice_in_dim(tables, start, start + size, axis=1)
        if split:
            shapes = [jax.ShapeDtypeStruct((n_lon, share, size, lanes), jnp.float32)] * n_comp
        else:
            shapes = [jax.ShapeDtypeStruct((rows, n_lon, size, lanes), jnp.float32)]
        big = pltpu.VMEM((window.size, size, width), jnp.float32)
        pieces = pl.pallas_call(
            functools.partial(
                propagate_kernel, window, n_lon, n_comp, split, start, 3 if i == 0 else 0
            ),
            out_shape=shapes,
            in_specs=[
                scalars,
                whole,
                whole,
                whole,
                whole,
                [whole] * len(lon_in),
                [[whole] * len(blocks) for blocks in lat_in[i]],
            ],
            out_specs=[whole] * len(shapes),
            scratch_shapes=prop_scratch(window, size, width),
            compiler_params=params(),
            cost_estimate=cost(7),
        )(
            place,
            table,
            faces,
            window_fields,
            parts[0],
            lon_in,
            lat_in[i],
        )
        if split:
            moved = [pieces[0]]
            for r in range(1, n_comp):
                moved.append(lax.ppermute(pieces[r], "comp", [(a, (a + r) % n_comp) for a in range(n_comp)]))
        else:
            energy = pieces[0].reshape(rows, n_lon, size, groups, span)
            energy = jnp.transpose(energy, (0, 3, 1, 2, 4)).reshape(n_comp, n_lon, 1, size, span)
            energy = lax.all_to_all(energy, "comp", split_axis=0, concat_axis=0, tiled=True)
            moved = [energy[s] for s in range(n_comp)]
        crossed = []
        for d in range(1, n_lon):
            pairs = [(b, (b + d) % n_lon) for b in range(n_lon)]
            crossed.append(lax.ppermute(jnp.stack([piece[d] for piece in moved]), "lon", pairs))
        arrived += moved + crossed

    cells = share * span
    energy, source, source_low = pl.pallas_call(
        functools.partial(forward_kernel, sizes, n_lon),
        grid=(n_comp,),
        out_shape=(
            jax.ShapeDtypeStruct((total, cells), jnp.float32),
            jax.ShapeDtypeStruct((total, cells), jnp.float32),
            jax.ShapeDtypeStruct((total, cells), jnp.bfloat16),
        ),
        in_specs=[
            pl.BlockSpec((2, block, total), lambda s: (0, s, 0)),
            pl.BlockSpec((block, 1), lambda s: (s, 0)),
        ]
        + [whole] * len(arrived),
        out_specs=(
            pl.BlockSpec((total, cells), lambda s: (0, 0)),
            pl.BlockSpec((block, cells), lambda s: (s, 0)),
            pl.BlockSpec((block, cells), lambda s: (s, 0)),
        ),
        scratch_shapes=[pltpu.VMEM((total, cells), jnp.bfloat16)],
        compiler_params=params(),
        cost_estimate=cost(4),
    )(matrix, strength, *arrived)

    back = []
    for s in range(n_comp):
        back.append(
            pl.pallas_call(
                backward_kernel,
                grid=(1,),
                out_shape=jax.ShapeDtypeStruct((share, block, span), jnp.float32),
                in_specs=[
                    pl.BlockSpec((2, block, total), lambda i, s=s: (0, s, 0)),
                    pl.BlockSpec((total, cells), lambda i: (0, 0)),
                    pl.BlockSpec((block, cells), lambda i, s=s: (s, 0)),
                    pl.BlockSpec((block, cells), lambda i, s=s: (s, 0)),
                ],
                out_specs=pl.BlockSpec((share, block, span), lambda i: (0, 0, 0)),
                compiler_params=params(),
                cost_estimate=cost(0.6),
            )(matrix_t, source_low, energy, source)
        )

    if split:
        home = [back[0]]
        for r in range(1, n_comp):
            home.append(lax.ppermute(back[r], "comp", [(a, (a - r) % n_comp) for a in range(n_comp)]))
        if half == half_own:
            out = pl.pallas_call(
                functools.partial(gather_kernel, n_lon, rows),
                out_shape=jax.ShapeDtypeStruct((comps_local * rows, lanes), jnp.float32),
                in_specs=[scalars] + [whole] * n_comp,
                out_specs=whole,
                compiler_params=params(),
                cost_estimate=cost(2),
            )(place, *home)
            return out.reshape(comps_local, rows, lanes)
        home = jnp.stack(home).reshape(n_comp, share, n_lon, half, lanes)[:, :, :, :half_own]
        home = jnp.roll(home, comp, 0)
        home = turned(home, 2, lon)
        return jnp.transpose(home, (2, 3, 0, 1, 4)).reshape(comps_local, rows, lanes)
    home = lax.all_to_all(jnp.concatenate(back), "comp", split_axis=0, concat_axis=0, tiled=True)
    home = home.reshape(rows, groups, n_lon, half, span)[:, :, :, :half_own]
    home = turned(home, 2, lon)
    return jnp.transpose(home, (2, 3, 0, 1, 4)).reshape(comps_local, rows, lanes)


def solution(mesh):
    placed = (
        P(("ens", "comp"), "lat", "lon"),
        P("lat", "lon"),
        P("lat", "lon"),
        P("lat", "lon"),
        P(),
        P(),
        P(),
        P(),
        P(),
    )
    return jax.shard_map(
        local,
        mesh=mesh,
        in_specs=placed,
        out_specs=P(("ens", "comp"), "lat", "lon"),
        check_vma=False,
    )
```

```python
import functools
import math

import jax
import jax.numpy as jnp
from jax import lax
from jax.experimental import pallas as pl
from jax.experimental.pallas import tpu as pltpu
from jax.sharding import PartitionSpec as P

NDIR = 36
SUBSTEPS = 4
RIM = 2 * SUBSTEPS
GROUP = 16
CHUNKS = 3

plus_factor = 0.4096
minus_factor = 3.160494
cross_factor = 2.007843

VMEM_LIMIT = 16 * 1024 * 1024
whole = pl.BlockSpec(memory_space=pltpu.VMEM)
anywhere = pl.BlockSpec(memory_space=pl.ANY)
scalars = pl.BlockSpec(memory_space=pltpu.SMEM)


def params():
    return pltpu.CompilerParams(vmem_limit_bytes=VMEM_LIMIT)


def cost(micros):
    return pl.CostEstimate(flops=0, bytes_accessed=int(micros * 3.5e6), transcendentals=0)


def chunk_sizes(total):
    groups = total // GROUP
    count = min(CHUNKS, groups)
    return [GROUP * (groups // count + (i < groups % count)) for i in range(count)]


class Window:
    def __init__(self, n_lat, rows):
        self.pair = n_lat == 2
        self.rows = rows
        self.size = 2 * rows + 4 if self.pair else 3 * rows

    def own(self, lat):
        return jnp.where(lat == 0, 2, 2 + self.rows) if self.pair else self.rows

    def received(self, lat):
        if self.pair:
            return [jnp.where(lat == 0, 2 + self.rows, 2)]
        return [0, 2 * self.rows]

    def zeros(self, lat):
        if not self.pair:
            return []
        first = jnp.where(lat == 0, 0, 2 + 2 * self.rows)
        return [first, first + 1]

    def steps(self, lat, substep):
        shrink = 2 * (substep + 1)
        if self.pair:
            return jnp.where(lat == 0, 2, 2 + shrink), 2 * self.rows - shrink
        return shrink, 3 * self.rows - 2 * shrink


def faces_kernel(window, n_lon, place, own, received, after, out, fields):
    lat = place[0]
    rows, lanes = own[0].shape[0] // 3, own[0].shape[1]
    for row in window.zeros(lat):
        fields[row] = jnp.zeros((3, n_lon * lanes), jnp.float32)
    sources = [(window.own(lat), [(ref, 0) for ref in own])]
    for offset, ref in zip(window.received(lat), received):
        sources.append((offset, [(ref, 3 * d) for d in range(n_lon)]))
    for offset, blocks in sources:
        for d, (ref, lead) in enumerate(blocks):
            for f in range(3):
                for row in range(rows):
                    at = (lead + f) * rows + row
                    fields[offset + row, f : f + 1, d * lanes : (d + 1) * lanes] = ref[at : at + 1, :]
    width = n_lon * lanes
    n_class = out.shape[2] // 6
    classes = lax.broadcasted_iota(jnp.int32, (n_class, width), 0).astype(jnp.float32)

    def hots(row):
        wet = fields[row, 0:1, :]
        hot_depth = (classes == fields[row, 1:2, :]).astype(jnp.float32)
        hot_current = (classes == fields[row, 2:3, :]).astype(jnp.float32)
        return wet, jnp.concatenate([hot_depth, hot_current], axis=0)

    def step(row, _):
        wet, hot = hots(row)
        wet_next, hot_next = hots(row + 1)
        east_wet = 0.5 * wet * pltpu.roll(wet, width - 1, 1)
        east = ((hot + pltpu.roll(hot, width - 1, 1)) * east_wet).astype(jnp.bfloat16)
        north = ((hot + hot_next) * (0.5 * wet * wet_next)).astype(jnp.bfloat16)
        span = 2 * n_class
        for copy in range(3):
            out[row, 0, copy * span : (copy + 1) * span, :] = east
            out[row, 1, copy * span : (copy + 1) * span, :] = north
        return 0

    lax.fori_loop(0, window.size - 1, step, 0)
    out[window.size - 1] = jnp.zeros(out.shape[1:], jnp.bfloat16)


def pack_kernel(start, half, rows, place, own_in, head, after, out, sems):
    lead = sum(ref.shape[0] for ref in head)
    length = (out.shape[0] - lead) // len(own_in)
    first = pl.multiple_of((place[2] * half + start) * rows, 8)
    copies = []
    for d, ref in enumerate(own_in):
        to = out.at[pl.ds(lead + d * length, length)]
        copies.append(pltpu.make_async_copy(ref.at[pl.ds(first, length)], to, sems.at[d]))
        copies[-1].start()
    for i, ref in enumerate(head):
        out[i * ref.shape[0] : (i + 1) * ref.shape[0], :] = ref[...]
    for copy in copies:
        copy.wait()


def cross_pack_kernel(d, pieces, after, out, sems):
    copies = []
    for s, ref in enumerate(pieces):
        copies.append(pltpu.make_async_copy(ref.at[d], out.at[s], sems.at[s]))
        copies[-1].start()
    for copy in copies:
        copy.wait()


def gate_kernel(*refs):
    pass


def median_zero(a, b):
    return jnp.maximum(jnp.minimum(a, b), jnp.minimum(jnp.maximum(a, b), 0.0))


def flux(u, c, low, high, slope_low, slope_high):
    rising = u > 0.0
    return u * jnp.where(rising, low, high) + c * jnp.where(rising, slope_low, slope_high)


def propagate_scratch(window, size, lanes, n_lon):
    width = n_lon * lanes
    energy = pltpu.VMEM((window.size, GROUP, width), jnp.float32)
    speed = pltpu.VMEM((window.size, size, width), jnp.float32)
    block = pltpu.VMEM((size * window.rows, lanes), jnp.float32)
    return [energy, energy, speed, speed, speed, speed] + [block] * n_lon + [pltpu.SemaphoreType.DMA((n_lon,))]


def propagate_kernel(
    window, n_lon, n_comp, split, start, half, head, place, tables, faces, wet, own_in, lat_in, after, *refs
):
    outs, scratch = refs[: -7 - n_lon], refs[-7 - n_lon :]
    energy, other, east_u, east_c, north_u, north_c = scratch[:6]
    own_blocks, sems = scratch[6:-1], scratch[-1]
    lat, comp, lon = place[0], place[1], place[2]
    rows, lanes = window.rows, wet.shape[2] // n_lon
    width = n_lon * lanes
    count = east_u.shape[1]
    copies = []
    for d in range(n_lon):
        first = pl.multiple_of((lon * half + start) * rows, 8)
        copies.append(pltpu.make_async_copy(own_in[d].at[pl.ds(first, count * rows)], own_blocks[d], sems.at[d]))
        copies[-1].start()

    def speeds(row, _):
        for which, u_ref, c_ref in ((0, east_u, east_c), (1, north_u, north_c)):
            u = jnp.dot(tables[which], faces[row, which], preferred_element_type=jnp.float32)
            size = jnp.abs(u)
            u_ref[row] = u
            c_ref[row] = 0.5 * size * (1.0 - size)
        return 0

    lax.fori_loop(0, window.size, speeds, 0, unroll=True)

    for copy in copies:
        copy.wait()
    own = window.own(lat)

    def group(g, _):
        first = pl.multiple_of(g * GROUP, GROUP)
        here = pl.ds(first, GROUP)
        for row in window.zeros(lat):
            energy[row] = jnp.zeros((GROUP, width), jnp.float32)
            other[row] = jnp.zeros((GROUP, width), jnp.float32)
        sources = [(own, [(ref, 0) for ref in own_blocks])]
        for offset, ref in zip(window.received(lat), lat_in):
            sources.append((offset, [(ref, head + d * count) for d in range(n_lon)]))
        for offset, blocks in sources:
            for d, (ref, lead) in enumerate(blocks):
                for row in range(rows):
                    at = pl.ds((lead + first) * rows + row, GROUP, stride=rows)
                    sea = wet[offset + row, 0:1, d * lanes : (d + 1) * lanes]
                    energy[offset + row, :, d * lanes : (d + 1) * lanes] = ref[at, :] * sea

        for substep in range(SUBSTEPS):
            base, length = window.steps(lat, substep)
            old, new = (energy, other) if substep % 2 == 0 else (other, energy)
            prior = [old[base + i] for i in (-2, -1, 0, 1)]
            gap = [b - a for a, b in zip(prior, prior[1:])]
            slope_prior, slope_here = median_zero(gap[1], gap[0]), median_zero(gap[2], gap[1])
            south = flux(
                north_u[base - 1, here], north_c[base - 1, here], prior[1], prior[2], slope_prior, slope_here
            )

            def row_step(i, carry):
                south, this, after, gap_after, slope_this = carry
                row = base + i
                beyond = old[row + 2]
                gap_beyond = beyond - after
                slope_after = median_zero(gap_beyond, gap_after)
                north = flux(north_u[row, here], north_c[row, here], this, after, slope_this, slope_after)
                east_cell = pltpu.roll(this, width - 1, 1)
                gap_east = east_cell - this
                gap_west = pltpu.roll(gap_east, 1, 1)
                slope = median_zero(gap_east, gap_west)
                slope_east = pltpu.roll(slope, width - 1, 1)
                east = flux(east_u[row, here], east_c[row, here], this, east_cell, slope, slope_east)
                west = pltpu.roll(east, 1, 1)
                new[row] = this - (east - west) - (north - south)
                return north, after, beyond, gap_beyond, slope_after

            lax.fori_loop(0, length, row_step, (south, prior[2], prior[3], gap[2], slope_here), unroll=True)

        if split:
            share = rows // n_comp
            for r in range(n_comp):
                base = own + lax.rem(comp + r, n_comp) * share
                for d in range(n_lon):
                    for k in range(share):
                        outs[r][d, k, here, :] = energy[base + k, :, d * lanes : (d + 1) * lanes]
        else:
            for row in range(rows):
                for d in range(n_lon):
                    outs[0][row, d, here, :] = energy[own + row, :, d * lanes : (d + 1) * lanes]
        return 0

    lax.fori_loop(0, count // GROUP, group, 0)


def matrix_kernel(names, index, weight, after, out, columns):
    height = out.shape[1]

    @pl.when(pl.program_id(1) == 0)
    def _():
        columns[...] = jnp.transpose(jnp.concatenate([index[0], weight[0]], axis=0))

    base = pl.program_id(1) * height

    def step(i, _):
        at = pl.multiple_of(i * GROUP, GROUP)
        column = columns[pl.ds(base + at, GROUP), :]
        name = names[...]
        made = jnp.zeros((GROUP, name.shape[1]), jnp.float32)
        for corner in range(4):
            made = jnp.where(name == column[:, corner : corner + 1], column[:, corner + 4 : corner + 5], made)
        out[0, pl.ds(at, GROUP), :] = made.astype(jnp.bfloat16)
        return 0

    lax.fori_loop(0, height // GROUP, step, 0, unroll=3)


def transposed_kernel(half, half_own, index, weight, after, out):
    height, total = out.shape[1], out.shape[2]
    base = pl.program_id(1) * height

    def step(i, _):
        at = pl.multiple_of(i * GROUP, GROUP)
        row = base + at + lax.broadcasted_iota(jnp.int32, (GROUP, 1), 0)
        if half != half_own:
            row = jnp.where(row % half < half_own, row // half * half_own + row % half, -1)
        row = jnp.broadcast_to(row.astype(jnp.float32), (GROUP, total))
        made = jnp.zeros((GROUP, total), jnp.float32)
        for corner in range(4):
            made = jnp.where(row == index[0, corner : corner + 1, :], weight[0, corner : corner + 1, :], made)
        out[0, pl.ds(at, GROUP), :] = made.astype(jnp.bfloat16)
        return 0

    lax.fori_loop(0, height // GROUP, step, 0, unroll=3)


def forward_kernel(sizes, n_lon, split, place, matrix, coupling, *refs):
    pieces = refs[:-4]
    energy_out, source_out, source_low_out, low = refs[-4:]
    step = pl.program_id(0)
    block = coupling.shape[0]
    half = block // n_lon
    per_chunk = len(pieces) // len(sizes)
    share, lanes = pieces[0].shape[1], pieces[0].shape[3]

    n_comp = per_chunk - n_lon + 1

    @pl.when(step == 0)
    def _():
        for s in range(n_comp):
            of_comp = lax.rem(place[1] + n_comp - s, n_comp) if split else s
            for d in range(n_lon):
                of_lon = lax.rem(place[2] + n_lon - d, n_lon)
                first = (of_comp * n_lon + of_lon) * half
                for i, size in enumerate(sizes):
                    at = pl.ds(pl.multiple_of(first + sum(sizes[:i]), GROUP), size)
                    group = pieces[i * per_chunk : (i + 1) * per_chunk]
                    for k in range(share):
                        part = group[s][0, k] if d == 0 else group[d - n_lon][s, k]
                        energy_out[at, k * lanes : (k + 1) * lanes] = part
                        low[at, k * lanes : (k + 1) * lanes] = part.astype(jnp.bfloat16)

    here = pl.ds(pl.multiple_of(step * block, GROUP), block)
    energy = energy_out[here, :]
    plus_side = jnp.dot(matrix[0, here, :], low[...], preferred_element_type=jnp.float32)
    minus_side = jnp.dot(matrix[1, here, :], low[...], preferred_element_type=jnp.float32)
    source = coupling[...] * (
        energy * energy * (plus_factor * plus_side + minus_factor * minus_side)
        - cross_factor * energy * plus_side * minus_side
    )
    source_out[...] = source
    source_low_out[...] = source.astype(jnp.bfloat16)


def backward_kernel(s, n_comp, split, place, matrix_t, source_low, energy, source, out):
    block, lanes = out.shape[1], out.shape[2]
    home = lax.rem(place[1] + n_comp - s, n_comp) if split else s
    here = pl.ds(pl.multiple_of(home * block, GROUP), block)
    gain = (
        jnp.dot(matrix_t[0, here, :], source_low[...], preferred_element_type=jnp.float32)
        + jnp.dot(matrix_t[1, here, :], source_low[...], preferred_element_type=jnp.float32)
        - 2.0 * source[here, :]
    )
    result = energy[here, :] + gain / (1.0 + jnp.abs(gain))
    for k in range(out.shape[0]):
        out[k] = result[:, k * lanes : (k + 1) * lanes]


def gather_kernel(rows, place, *refs):
    pieces, out = refs[:-1], refs[-1]
    comp = place[1]
    n_comp = len(pieces)
    share = rows // n_comp
    for r, piece in enumerate(pieces):
        for k in range(share):
            row = lax.rem(comp + r, n_comp) * share + k
            for i in range(0, piece.shape[1], GROUP):
                out[pl.ds(i * rows + row, GROUP, stride=rows), :] = piece[k, i : i + GROUP, :]


def local(
    spectrum,
    sea_mask,
    depth_class,
    current_class,
    speed_table,
    current_table,
    coupling,
    quad_index,
    quad_weight,
):
    comps_local, rows, lanes = spectrum.shape
    n_comp, n_lat, n_lon = (lax.axis_size(a) for a in ("comp", "lat", "lon"))
    comp, lat, lon = (lax.axis_index(a) for a in ("comp", "lat", "lon"))
    place = jnp.stack([lat, comp, lon]).astype(jnp.int32)
    half_own = comps_local // n_lon
    half = -(-half_own // GROUP) * GROUP
    sizes = chunk_sizes(half)
    starts = [sum(sizes[:i]) for i in range(len(sizes))]
    window = Window(n_lat, rows)
    width = n_lon * lanes
    split = rows % n_comp == 0

    if half == half_own:
        flat = spectrum.reshape(comps_local * rows, lanes)
    else:
        flat = spectrum.reshape(n_lon, half_own, rows, lanes)
        flat = jnp.pad(flat, ((0, 0), (0, half - half_own), (0, 0), (0, 0))).reshape(-1, lanes)
    fields = jnp.concatenate([sea_mask, depth_class, current_class]).astype(jnp.float32)
    own_in, own_fields = [flat], [fields]
    for d in range(n_lon - 1, 0, -1):
        pairs = [(i, (i + d) % n_lon) for i in range(n_lon)]
        own_in.append(lax.ppermute(flat, "lon", pairs))
        own_fields.append(lax.ppermute(fields, "lon", pairs))
    if window.pair:
        moves = [[(0, 1), (1, 0)]]
    else:
        moves = [[(i, i + 1) for i in range(n_lat - 1)], [(i + 1, i) for i in range(n_lat - 1)]]
    lat_in, packed = [], []
    for i, (start, size) in enumerate(zip(starts, sizes)):
        head = own_fields if i == 0 else []
        length = n_lon * (size + (0 if i else 3)) * rows
        packed.append(
            pl.pallas_call(
                functools.partial(pack_kernel, start, half, rows),
                out_shape=jax.ShapeDtypeStruct((length, lanes), jnp.float32),
                in_specs=[scalars, [anywhere] * n_lon, [whole] * len(head), [anywhere] * (i > 0)],
                out_specs=whole,
                scratch_shapes=[pltpu.SemaphoreType.DMA((n_lon,))],
                compiler_params=params(),
                cost_estimate=cost(1),
            )(place, own_in, head, packed[-1:])
        )
        lat_in.append([lax.ppermute(packed[i], "lat", move) for move in moves])

    total = n_comp * n_lon * half
    block = n_lon * half

    def spread(array):
        if half == half_own:
            return array
        array = array.reshape(array.shape[:-1] + (n_comp * n_lon, half_own))
        array = jnp.pad(array, ((0, 0),) * (array.ndim - 1) + ((0, half - half_own),), constant_values=-1)
        return array.reshape(array.shape[:-2] + (total,))

    names = spread(jnp.arange(n_comp * comps_local, dtype=jnp.float32)[None])
    index = spread(jnp.swapaxes(quad_index, 1, 2).astype(jnp.float32))
    weight = jnp.maximum(spread(jnp.swapaxes(quad_weight, 1, 2)), 0.0)
    strength = spread(coupling[None]).reshape(total, 1)
    by_cols = pl.BlockSpec((1, 4, total), lambda s, i: (s, 0, 0))
    by_block = pl.BlockSpec((1, block, total), lambda s, i: (s, i, 0))
    matrix = pl.pallas_call(
        matrix_kernel,
        grid=(2, n_comp),
        out_shape=pltpu.VMEM((2, total, total), jnp.bfloat16),
        in_specs=[whole, by_cols, by_cols, anywhere],
        out_specs=by_block,
        scratch_shapes=[pltpu.VMEM((total, 8), jnp.float32)],
        compiler_params=params(),
        cost_estimate=cost(6),
    )(names, index, weight, packed[-1])

    n_class = speed_table.shape[0]
    head_block = pl.BlockSpec((3 * n_lon * rows, lanes), lambda i: (0, 0))
    faces, window_fields = pl.pallas_call(
        functools.partial(faces_kernel, window, n_lon),
        grid=(1,),
        out_shape=(
            jax.ShapeDtypeStruct((window.size, 2, 6 * n_class, width), jnp.bfloat16),
            jax.ShapeDtypeStruct((window.size, 3, width), jnp.float32),
        ),
        in_specs=[scalars, [whole] * n_lon, [head_block] * len(moves), anywhere],
        out_specs=(whole, whole),
        compiler_params=params(),
        cost_estimate=cost(2),
    )(place, own_fields, lat_in[0], matrix)

    ids = comp * comps_local + lon * half_own + jnp.arange(half, dtype=jnp.int32)
    freq_hot = ((ids // NDIR)[:, None] == jnp.arange(speed_table.shape[1], dtype=jnp.int32)[None, :]).astype(
        jnp.float32
    )
    speed = jnp.dot(freq_hot, speed_table.T, precision=lax.Precision.HIGHEST)
    angles = 2.0 * math.pi / NDIR * (ids % NDIR).astype(jnp.float32)
    tables = []
    for which, turn in ((0, jnp.cos(angles)), (1, jnp.sin(angles))):
        currents = jnp.broadcast_to(current_table[:, which][None], (half, n_class))
        left = jnp.concatenate([speed * turn[:, None], currents], axis=1)
        levels = []
        for _ in range(3):
            level = lax.reduce_precision(left, 8, 7)
            levels.append(level)
            left = left - level
        tables.append(jnp.concatenate(levels, axis=1).astype(jnp.bfloat16))
    tables = jnp.stack(tables)

    if split:
        share, span = rows // n_comp, lanes
    else:
        groups = n_comp // rows
        share, span = 1, lanes // groups
    arrived = []
    for i, (start, size) in enumerate(zip(starts, sizes)):
        table = lax.slice_in_dim(tables, start, start + size, axis=1)
        if split:
            shapes = [jax.ShapeDtypeStruct((n_lon, share, size, lanes), jnp.float32)] * n_comp
        else:
            shapes = [jax.ShapeDtypeStruct((rows, n_lon, size, lanes), jnp.float32)]
        pieces = pl.pallas_call(
            functools.partial(
                propagate_kernel, window, n_lon, n_comp, split, start, half, 0 if i else 3 * n_lon
            ),
            out_shape=shapes,
            in_specs=[
                scalars,
                whole,
                whole,
                whole,
                [anywhere] * n_lon,
                [whole] * len(moves),
                anywhere,
            ],
            out_specs=[whole] * len(shapes),
            scratch_shapes=propagate_scratch(window, size, lanes, n_lon),
            compiler_params=params(),
            cost_estimate=cost(1.5 + 0.11 * size),
        )(
            place,
            table,
            faces,
            window_fields,
            own_in,
            lat_in[i],
            matrix if i == 0 else pieces[0],
        )
        if split:
            sent = pieces[1:]
            if i > 0:
                sent = pl.pallas_call(
                    gate_kernel,
                    out_shape=shapes[1:],
                    in_specs=[anywhere] * (2 * len(sent)),
                    out_specs=[anywhere] * len(sent),
                    input_output_aliases={j: j for j in range(len(sent))},
                    compiler_params=params(),
                    cost_estimate=cost(0.1),
                )(*sent, *moved[1:])
            moved = [pieces[0]]
            for r in range(1, n_comp):
                pairs = [(a, (a + r) % n_comp) for a in range(n_comp)]
                moved.append(lax.ppermute(sent[r - 1], "comp", pairs))
        else:
            energy = pieces[0].reshape(rows, n_lon, size, groups, span)
            energy = jnp.transpose(energy, (0, 3, 1, 2, 4)).reshape(n_comp, n_lon, 1, size, span)
            energy = lax.all_to_all(energy, "comp", split_axis=0, concat_axis=0, tiled=True)
            moved = [energy[s] for s in range(n_comp)]
        after = []
        if i == len(sizes) - 1:
            matrix_t = pl.pallas_call(
                functools.partial(transposed_kernel, half, half_own),
                grid=(2, n_comp),
                out_shape=pltpu.VMEM((2, total, total), jnp.bfloat16),
                in_specs=[by_cols, by_cols, anywhere],
                out_specs=by_block,
                compiler_params=params(),
                cost_estimate=cost(4),
            )(index, weight, pieces[0])
            after = [matrix_t]
        crossed = []
        for d in range(1, n_lon):
            pairs = [(b, (b + d) % n_lon) for b in range(n_lon)]
            packed = pl.pallas_call(
                functools.partial(cross_pack_kernel, d),
                out_shape=jax.ShapeDtypeStruct((n_comp, share, size, span), jnp.float32),
                in_specs=[[anywhere] * n_comp, [anywhere] * len(after)],
                out_specs=whole,
                scratch_shapes=[pltpu.SemaphoreType.DMA((n_comp,))],
                compiler_params=params(),
                cost_estimate=cost(1),
            )(moved, after)
            crossed.append(lax.ppermute(packed, "lon", pairs))
        arrived += moved + crossed

    cells = share * span
    energy, source, source_low = pl.pallas_call(
        functools.partial(forward_kernel, sizes, n_lon, split),
        grid=(n_comp,),
        out_shape=(
            jax.ShapeDtypeStruct((total, cells), jnp.float32),
            jax.ShapeDtypeStruct((total, cells), jnp.float32),
            jax.ShapeDtypeStruct((total, cells), jnp.bfloat16),
        ),
        in_specs=[
            scalars,
            whole,
            pl.BlockSpec((block, 1), lambda s: (s, 0)),
        ]
        + [whole] * len(arrived),
        out_specs=(
            pl.BlockSpec((total, cells), lambda s: (0, 0)),
            pl.BlockSpec((block, cells), lambda s: (s, 0)),
            pl.BlockSpec((block, cells), lambda s: (s, 0)),
        ),
        scratch_shapes=[pltpu.VMEM((total, cells), jnp.bfloat16)],
        compiler_params=params(),
        cost_estimate=cost(4),
    )(place, matrix, strength, *arrived)

    back = []
    for s in range(n_comp):
        back.append(
            pl.pallas_call(
                functools.partial(backward_kernel, s, n_comp, split),
                out_shape=jax.ShapeDtypeStruct((share, block, span), jnp.float32),
                in_specs=[scalars] + [whole] * 4,
                out_specs=whole,
                compiler_params=params(),
                cost_estimate=cost(0.6),
            )(place, matrix_t, source_low, energy, source)
        )

    if split:
        home = [back[0]]
        for r in range(1, n_comp):
            home.append(lax.ppermute(back[r], "comp", [(a, (a - r) % n_comp) for a in range(n_comp)]))
        if half == half_own:
            out = pl.pallas_call(
                functools.partial(gather_kernel, rows),
                out_shape=jax.ShapeDtypeStruct((comps_local * rows, lanes), jnp.float32),
                in_specs=[scalars] + [whole] * n_comp,
                out_specs=whole,
                compiler_params=params(),
                cost_estimate=cost(2),
            )(place, *home)
            return out.reshape(comps_local, rows, lanes)
        home = jnp.stack(home).reshape(n_comp, share, n_lon, half, lanes)[:, :, :, :half_own]
        home = jnp.roll(home, comp, 0)
        return jnp.transpose(home, (2, 3, 0, 1, 4)).reshape(comps_local, rows, lanes)
    home = lax.all_to_all(jnp.concatenate(back), "comp", split_axis=0, concat_axis=0, tiled=True)
    home = home.reshape(rows, groups, n_lon, half, span)[:, :, :, :half_own]
    return jnp.transpose(home, (2, 3, 0, 1, 4)).reshape(comps_local, rows, lanes)


def solution(mesh):
    placed = (
        P(("ens", "comp"), "lat", "lon"),
        P("lat", "lon"),
        P("lat", "lon"),
        P("lat", "lon"),
        P(),
        P(),
        P(),
        P(),
        P(),
    )
    return jax.shard_map(
        local,
        mesh=mesh,
        in_specs=placed,
        out_specs=P(("ens", "comp"), "lat", "lon"),
        check_vma=False,
    )
```

```python
import functools
import math

import jax
import jax.numpy as jnp
from jax import lax
from jax.experimental import pallas as pl
from jax.experimental.pallas import tpu as pltpu
from jax.sharding import PartitionSpec as P

NDIR = 36
SUBSTEPS = 4
RIM = 2 * SUBSTEPS
GROUP = 16
CHUNKS = 3

plus_factor = 0.4096
minus_factor = 3.160494
cross_factor = 2.007843

VMEM_LIMIT = 16 * 1024 * 1024
whole = pl.BlockSpec(memory_space=pltpu.VMEM)
anywhere = pl.BlockSpec(memory_space=pl.ANY)
scalars = pl.BlockSpec(memory_space=pltpu.SMEM)


def params():
    return pltpu.CompilerParams(vmem_limit_bytes=VMEM_LIMIT)


def cost(micros):
    return pl.CostEstimate(flops=0, bytes_accessed=int(micros * 3.5e6), transcendentals=0)


def chunk_sizes(total):
    groups = total // GROUP
    count = min(CHUNKS, groups)
    return [GROUP * (groups // count + (i < groups % count)) for i in range(count)]


class Window:
    def __init__(self, n_lat, rows):
        self.pair = n_lat == 2
        self.rows = rows
        self.size = 2 * rows + 4 if self.pair else 3 * rows

    def own(self, lat):
        return jnp.where(lat == 0, 2, 2 + self.rows) if self.pair else self.rows

    def received(self, lat):
        if self.pair:
            return [jnp.where(lat == 0, 2 + self.rows, 2)]
        return [0, 2 * self.rows]

    def zeros(self, lat):
        if not self.pair:
            return []
        first = jnp.where(lat == 0, 0, 2 + 2 * self.rows)
        return [first, first + 1]

    def steps(self, lat, substep):
        shrink = 2 * (substep + 1)
        if self.pair:
            return jnp.where(lat == 0, 2, 2 + shrink), 2 * self.rows - shrink
        return shrink, 3 * self.rows - 2 * shrink


def faces_kernel(window, n_lon, place, own, received, after, out, fields):
    lat = place[0]
    rows, lanes = window.rows, own[0].shape[1]
    for row in window.zeros(lat):
        fields[row] = jnp.zeros((3, n_lon * lanes), jnp.float32)
    for offset, blocks in [(window.own(lat), own)] + list(zip(window.received(lat), received)):
        for d, ref in enumerate(blocks):
            for f in range(3):
                for row in range(rows):
                    at = f * rows + row
                    fields[offset + row, f : f + 1, d * lanes : (d + 1) * lanes] = ref[at : at + 1, :]
    width = n_lon * lanes
    n_class = out.shape[2] // 6
    classes = lax.broadcasted_iota(jnp.int32, (n_class, width), 0).astype(jnp.float32)

    def hots(row):
        wet = fields[row, 0:1, :]
        hot_depth = (classes == fields[row, 1:2, :]).astype(jnp.float32)
        hot_current = (classes == fields[row, 2:3, :]).astype(jnp.float32)
        return wet, jnp.concatenate([hot_depth, hot_current], axis=0)

    def step(row, _):
        wet, hot = hots(row)
        wet_next, hot_next = hots(row + 1)
        east_wet = 0.5 * wet * pltpu.roll(wet, width - 1, 1)
        east = ((hot + pltpu.roll(hot, width - 1, 1)) * east_wet).astype(jnp.bfloat16)
        north = ((hot + hot_next) * (0.5 * wet * wet_next)).astype(jnp.bfloat16)
        span = 2 * n_class
        for copy in range(3):
            out[row, 0, copy * span : (copy + 1) * span, :] = east
            out[row, 1, copy * span : (copy + 1) * span, :] = north
        return 0

    lax.fori_loop(0, window.size - 1, step, 0, unroll=4)
    out[window.size - 1] = jnp.zeros(out.shape[1:], jnp.bfloat16)


def pack_raw_kernel(half, rows, flat, sea, depth, current, out, fields_out, held, sems):
    fields = [sea, depth, current]
    lead = len(fields) * rows
    parts = flat.shape[0] // (half * rows)
    length = (out.shape[0] - lead) // parts
    copies = []
    for i in range(parts):
        to = out.at[pl.ds(lead + i * length, length)]
        copies.append(pltpu.make_async_copy(flat.at[pl.ds(i * half * rows, length)], to, sems.at[0, i]))
    for i, ref in enumerate(fields):
        copies.append(pltpu.make_async_copy(ref, held.at[i], sems.at[1, i]))
    for copy in copies:
        copy.start()
    for copy in copies:
        copy.wait()
    for i in range(len(fields)):
        at = slice(i * rows, (i + 1) * rows)
        out[at, :] = held[i].astype(jnp.float32)
        fields_out[at, :] = held[i].astype(jnp.float32)


def pack_kernel(starts, half, rows, place, own_in, after, *refs):
    outs, sems = refs[:-1], refs[-1]
    copies = []
    for i, (start, out) in enumerate(zip(starts, outs)):
        length = out.shape[0] // len(own_in)
        first = pl.multiple_of((place[2] * half + start) * rows, 8)
        for d, ref in enumerate(own_in):
            there = ref.at[pl.ds(first, length)]
            copies.append(pltpu.make_async_copy(there, out.at[pl.ds(d * length, length)], sems.at[i, d]))
    for copy in copies:
        copy.start()
    for copy in copies:
        copy.wait()


def cross_pack_kernel(d, pieces, after, out, sems):
    copies = []
    for s, ref in enumerate(pieces):
        copies.append(pltpu.make_async_copy(ref.at[d], out.at[s], sems.at[s]))
        copies[-1].start()
    for copy in copies:
        copy.wait()


def gate_kernel(*refs):
    pass


def gated(arrays, after):
    return pl.pallas_call(
        gate_kernel,
        out_shape=[jax.ShapeDtypeStruct(a.shape, a.dtype) for a in arrays],
        in_specs=[anywhere] * (len(arrays) + len(after)),
        out_specs=[anywhere] * len(arrays),
        input_output_aliases={i: i for i in range(len(arrays))},
        compiler_params=params(),
        cost_estimate=cost(0.1),
    )(*arrays, *after)


def median_zero(a, b):
    return jnp.maximum(jnp.minimum(a, b), jnp.minimum(jnp.maximum(a, b), 0.0))


def flux(u, c, low, high, slope_low, slope_high):
    rising = u > 0.0
    return u * jnp.where(rising, low, high) + c * jnp.where(rising, slope_low, slope_high)


def propagate_scratch(window, size, lanes, n_lon):
    width = n_lon * lanes
    energy = pltpu.VMEM((window.size, GROUP, width), jnp.float32)
    speed = pltpu.VMEM((window.size, size, width), jnp.float32)
    block = pltpu.VMEM((size * window.rows, lanes), jnp.float32)
    return [energy, energy, speed, speed, speed, speed] + [block] * n_lon + [pltpu.SemaphoreType.DMA((n_lon,))]


def propagate_kernel(
    window, n_lon, n_comp, split, start, half, head, place, tables, faces, wet, own_in, lat_in, after, *refs
):
    outs, scratch = refs[: -7 - n_lon], refs[-7 - n_lon :]
    energy, other, east_u, east_c, north_u, north_c = scratch[:6]
    own_blocks, sems = scratch[6:-1], scratch[-1]
    lat, comp, lon = place[0], place[1], place[2]
    rows, lanes = window.rows, wet.shape[2] // n_lon
    width = n_lon * lanes
    count = east_u.shape[1]
    copies = []
    for d in range(n_lon):
        first = pl.multiple_of((lon * half + start) * rows, 8)
        copies.append(pltpu.make_async_copy(own_in[d].at[pl.ds(first, count * rows)], own_blocks[d], sems.at[d]))
        copies[-1].start()

    def speeds(row, _):
        for which, u_ref, c_ref in ((0, east_u, east_c), (1, north_u, north_c)):
            u = jnp.dot(tables[which], faces[row, which], preferred_element_type=jnp.float32)
            size = jnp.abs(u)
            u_ref[row] = u
            c_ref[row] = 0.5 * size * (1.0 - size)
        return 0

    lax.fori_loop(0, window.size, speeds, 0, unroll=True)

    for copy in copies:
        copy.wait()
    own = window.own(lat)

    def group(g, _):
        first = pl.multiple_of(g * GROUP, GROUP)
        here = pl.ds(first, GROUP)
        for row in window.zeros(lat):
            energy[row] = jnp.zeros((GROUP, width), jnp.float32)
            other[row] = jnp.zeros((GROUP, width), jnp.float32)
        sources = [(own, [(ref, 0) for ref in own_blocks])]
        for offset, blocks in zip(window.received(lat), lat_in):
            if head:
                sources.append((offset, [(ref, head + lon * count) for ref in blocks]))
            else:
                sources.append((offset, [(blocks[0], d * count) for d in range(n_lon)]))
        for offset, blocks in sources:
            for d, (ref, lead) in enumerate(blocks):
                for row in range(rows):
                    at = pl.ds((lead + first) * rows + row, GROUP, stride=rows)
                    sea = wet[offset + row, 0:1, d * lanes : (d + 1) * lanes]
                    energy[offset + row, :, d * lanes : (d + 1) * lanes] = ref[at, :] * sea

        for substep in range(SUBSTEPS):
            base, length = window.steps(lat, substep)
            old, new = (energy, other) if substep % 2 == 0 else (other, energy)
            prior = [old[base + i] for i in (-2, -1, 0, 1)]
            gap = [b - a for a, b in zip(prior, prior[1:])]
            slope_prior, slope_here = median_zero(gap[1], gap[0]), median_zero(gap[2], gap[1])
            south = flux(
                north_u[base - 1, here], north_c[base - 1, here], prior[1], prior[2], slope_prior, slope_here
            )

            def row_step(i, carry):
                south, this, after, gap_after, slope_this = carry
                row = base + i
                beyond = old[row + 2]
                gap_beyond = beyond - after
                slope_after = median_zero(gap_beyond, gap_after)
                north = flux(north_u[row, here], north_c[row, here], this, after, slope_this, slope_after)
                east_cell = pltpu.roll(this, width - 1, 1)
                gap_east = east_cell - this
                gap_west = pltpu.roll(gap_east, 1, 1)
                slope = median_zero(gap_east, gap_west)
                slope_east = pltpu.roll(slope, width - 1, 1)
                east = flux(east_u[row, here], east_c[row, here], this, east_cell, slope, slope_east)
                west = pltpu.roll(east, 1, 1)
                new[row] = this - (east - west) - (north - south)
                return north, after, beyond, gap_beyond, slope_after

            lax.fori_loop(0, length, row_step, (south, prior[2], prior[3], gap[2], slope_here), unroll=True)

        if split:
            share = rows // n_comp
            for r in range(n_comp):
                base = own + lax.rem(comp + r, n_comp) * share
                for d in range(n_lon):
                    for k in range(share):
                        outs[r][d, k, here, :] = energy[base + k, :, d * lanes : (d + 1) * lanes]
        else:
            for row in range(rows):
                for d in range(n_lon):
                    outs[0][row, d, here, :] = energy[own + row, :, d * lanes : (d + 1) * lanes]
        return 0

    lax.fori_loop(0, count // GROUP, group, 0)


def matrix_kernel(home, place, names, index, weight, after, out, columns):
    height = out.shape[1]

    @pl.when(pl.program_id(1) == 0)
    def _():
        columns[...] = jnp.transpose(jnp.concatenate([index[0], weight[0]], axis=0))

    base = pl.multiple_of(home(place, pl.program_id(1)) * height, GROUP)

    def step(i, _):
        at = pl.multiple_of(i * GROUP, GROUP)
        column = columns[pl.ds(base + at, GROUP), :]
        name = names[...]
        made = jnp.zeros((GROUP, name.shape[1]), jnp.float32)
        for corner in range(4):
            made = jnp.where(name == column[:, corner : corner + 1], column[:, corner + 4 : corner + 5], made)
        out[0, pl.ds(at, GROUP), :] = made.astype(jnp.bfloat16)
        return 0

    lax.fori_loop(0, height // GROUP, step, 0, unroll=True)


def transposed_kernel(home, half, half_own, place, index, weight, after, out):
    height, total = out.shape[1], out.shape[2]
    base = home(place, pl.program_id(1)) * height

    def step(i, _):
        at = pl.multiple_of(i * GROUP, GROUP)
        row = base + at + lax.broadcasted_iota(jnp.int32, (GROUP, 1), 0)
        if half != half_own:
            row = jnp.where(row % half < half_own, row // half * half_own + row % half, -1)
        row = jnp.broadcast_to(row.astype(jnp.float32), (GROUP, total))
        made = jnp.zeros((GROUP, total), jnp.float32)
        for corner in range(4):
            made = jnp.where(row == index[0, corner : corner + 1, :], weight[0, corner : corner + 1, :], made)
        out[0, pl.ds(at, GROUP), :] = made.astype(jnp.bfloat16)
        return 0

    lax.fori_loop(0, height // GROUP, step, 0, unroll=3)


def forward_kernel(sizes, n_lon, home, place, matrix, coupling, *refs):
    pieces = refs[:-4]
    energy_out, source_out, source_low_out, low = refs[-4:]
    per_chunk = len(pieces) // len(sizes)
    n_comp = per_chunk - n_lon + 1
    block = coupling.shape[0] // n_comp
    half = block // n_lon
    share, lanes = pieces[0].shape[1], pieces[0].shape[3]
    for s in range(n_comp):
        for d in range(n_lon):
            first = lax.rem(place[2] + n_lon - d, n_lon) * half
            for i, size in enumerate(sizes):
                group = pieces[i * per_chunk : (i + 1) * per_chunk]
                to = first + sum(sizes[:i])
                here = pl.ds(pl.multiple_of(s * block + to, GROUP), size)
                there = pl.ds(pl.multiple_of(home(place, s) * block + to, GROUP), size)
                for k in range(share):
                    part = group[s][0, k] if d == 0 else group[d - n_lon][s, k]
                    energy_out[here, k * lanes : (k + 1) * lanes] = part
                    low[there, k * lanes : (k + 1) * lanes] = part.astype(jnp.bfloat16)
    for s in range(n_comp):
        here = slice(s * block, (s + 1) * block)
        there = pl.ds(pl.multiple_of(home(place, s) * block, GROUP), block)
        energy = energy_out[here, :]
        plus_side = jnp.dot(matrix[0, here, :], low[...], preferred_element_type=jnp.float32)
        minus_side = jnp.dot(matrix[1, here, :], low[...], preferred_element_type=jnp.float32)
        source = coupling[there, :] * (
            energy * energy * (plus_factor * plus_side + minus_factor * minus_side)
            - cross_factor * energy * plus_side * minus_side
        )
        source_out[here, :] = source
        source_low_out[there, :] = source.astype(jnp.bfloat16)


def backward_kernel(s, matrix_t, source_low, energy, source, out):
    block, lanes = out.shape[1], out.shape[2]
    here = slice(s * block, (s + 1) * block)
    gain = (
        jnp.dot(matrix_t[0, here, :], source_low[...], preferred_element_type=jnp.float32)
        + jnp.dot(matrix_t[1, here, :], source_low[...], preferred_element_type=jnp.float32)
        - 2.0 * source[here, :]
    )
    result = energy[here, :] + gain / (1.0 + jnp.abs(gain))
    for k in range(out.shape[0]):
        out[k] = result[:, k * lanes : (k + 1) * lanes]


def gather_kernel(rows, place, *refs):
    pieces, out = refs[:-1], refs[-1]
    comp = place[1]
    n_comp = len(pieces)
    share = rows // n_comp
    for r, piece in enumerate(pieces):
        for k in range(share):
            row = lax.rem(comp + r, n_comp) * share + k
            for i in range(0, piece.shape[1], GROUP):
                out[pl.ds(i * rows + row, GROUP, stride=rows), :] = piece[k, i : i + GROUP, :]


def local(
    spectrum,
    sea_mask,
    depth_class,
    current_class,
    speed_table,
    current_table,
    coupling,
    quad_index,
    quad_weight,
):
    comps_local, rows, lanes = spectrum.shape
    n_comp, n_lat, n_lon = (lax.axis_size(a) for a in ("comp", "lat", "lon"))
    comp, lat, lon = (lax.axis_index(a) for a in ("comp", "lat", "lon"))
    place = jnp.stack([lat, comp, lon]).astype(jnp.int32)
    half_own = comps_local // n_lon
    half = -(-half_own // GROUP) * GROUP
    sizes = chunk_sizes(half)
    starts = [sum(sizes[:i]) for i in range(len(sizes))]
    window = Window(n_lat, rows)
    width = n_lon * lanes
    split = rows % n_comp == 0

    if half == half_own:
        flat = spectrum.reshape(comps_local * rows, lanes)
    else:
        flat = spectrum.reshape(n_lon, half_own, rows, lanes)
        flat = jnp.pad(flat, ((0, 0), (0, half - half_own), (0, 0), (0, 0))).reshape(-1, lanes)
    if window.pair:
        moves = [[(0, 1), (1, 0)]]
    else:
        moves = [[(i, i + 1) for i in range(n_lat - 1)], [(i + 1, i) for i in range(n_lat - 1)]]
    lengths = [n_lon * size * rows for size in sizes]


    def on_all_columns(block):
        found = [block]
        for d in range(n_lon - 1, 0, -1):
            found.append(lax.ppermute(block, "lon", [(i, (i + d) % n_lon) for i in range(n_lon)]))
        return found

    first_block, fields = pl.pallas_call(
        functools.partial(pack_raw_kernel, half, rows),
        out_shape=(
            jax.ShapeDtypeStruct((lengths[0] + 3 * rows, lanes), jnp.float32),
            jax.ShapeDtypeStruct((3 * rows, lanes), jnp.float32),
        ),
        in_specs=[anywhere] * 4,
        out_specs=(whole, whole),
        scratch_shapes=[pltpu.VMEM((3, rows, lanes), jnp.int32), pltpu.SemaphoreType.DMA((2, max(n_lon, 3)))],
        compiler_params=params(),
        cost_estimate=cost(1),
    )(*[pltpu.with_memory_space_constraint(a, pltpu.HBM) for a in (flat, sea_mask, depth_class, current_class)])
    own_in, own_fields = on_all_columns(flat), on_all_columns(fields)
    blocks = [first_block]
    if len(sizes) > 1:
        blocks += pl.pallas_call(
            functools.partial(pack_kernel, starts[1:], half, rows),
            out_shape=[jax.ShapeDtypeStruct((length, lanes), jnp.float32) for length in lengths[1:]],
            in_specs=[scalars, [anywhere] * n_lon, [anywhere] * (n_lon + 1)],
            out_specs=[whole] * len(lengths[1:]),
            scratch_shapes=[pltpu.SemaphoreType.DMA((len(lengths) - 1, n_lon))],
            compiler_params=params(),
            cost_estimate=cost(1.5),
        )(place, own_in, [first_block] + own_fields)
    lat_in = [[lax.ppermute(block, "lat", move) for move in moves] for block in blocks]

    def home_of(place, s):
        return lax.rem(place[1] + n_comp - s, n_comp) if split else s

    total = n_comp * n_lon * half
    block = n_lon * half

    def spread(array):
        if half == half_own:
            return array
        array = array.reshape(array.shape[:-1] + (n_comp * n_lon, half_own))
        array = jnp.pad(array, ((0, 0),) * (array.ndim - 1) + ((0, half - half_own),), constant_values=-1)
        return array.reshape(array.shape[:-2] + (total,))

    names = spread(jnp.arange(n_comp * comps_local, dtype=jnp.float32)[None])
    index = spread(jnp.swapaxes(quad_index, 1, 2).astype(jnp.float32))
    weight = jnp.maximum(spread(jnp.swapaxes(quad_weight, 1, 2)), 0.0)
    strength = spread(coupling[None]).reshape(total, 1)
    by_cols = pl.BlockSpec((1, 4, total), lambda s, i: (s, 0, 0))
    by_block = pl.BlockSpec((1, block, total), lambda s, i: (s, i, 0))
    matrix = pl.pallas_call(
        functools.partial(matrix_kernel, home_of),
        grid=(2, n_comp),
        out_shape=pltpu.VMEM((2, total, total), jnp.bfloat16),
        in_specs=[scalars, whole, by_cols, by_cols, anywhere],
        out_specs=by_block,
        scratch_shapes=[pltpu.VMEM((total, 8), jnp.float32)],
        compiler_params=params(),
        cost_estimate=cost(6),
    )(place, names, index, weight, blocks[-1])

    lat_in[0] = [on_all_columns(block) for block in gated(lat_in[0], [matrix])]
    lat_in[1:] = [[[block] for block in found] for found in lat_in[1:]]

    n_class = speed_table.shape[0]
    head_block = pl.BlockSpec((3 * rows, lanes), lambda i: (0, 0))
    faces, window_fields = pl.pallas_call(
        functools.partial(faces_kernel, window, n_lon),
        grid=(1,),
        out_shape=(
            jax.ShapeDtypeStruct((window.size, 2, 6 * n_class, width), jnp.bfloat16),
            jax.ShapeDtypeStruct((window.size, 3, width), jnp.float32),
        ),
        in_specs=[scalars, [whole] * n_lon, [[head_block] * n_lon] * len(moves), anywhere],
        out_specs=(whole, whole),
        compiler_params=params(),
        cost_estimate=cost(2),
    )(place, own_fields, lat_in[0], matrix)

    ids = comp * comps_local + lon * half_own + jnp.arange(half, dtype=jnp.int32)
    freq_hot = ((ids // NDIR)[:, None] == jnp.arange(speed_table.shape[1], dtype=jnp.int32)[None, :]).astype(
        jnp.float32
    )
    speed = jnp.dot(freq_hot, speed_table.T, precision=lax.Precision.HIGHEST)
    angles = 2.0 * math.pi / NDIR * (ids % NDIR).astype(jnp.float32)
    tables = []
    for which, turn in ((0, jnp.cos(angles)), (1, jnp.sin(angles))):
        currents = jnp.broadcast_to(current_table[:, which][None], (half, n_class))
        left = jnp.concatenate([speed * turn[:, None], currents], axis=1)
        levels = []
        for _ in range(3):
            level = lax.reduce_precision(left, 8, 7)
            levels.append(level)
            left = left - level
        tables.append(jnp.concatenate(levels, axis=1).astype(jnp.bfloat16))
    tables = jnp.stack(tables)

    if split:
        share, span = rows // n_comp, lanes
    else:
        groups = n_comp // rows
        share, span = 1, lanes // groups
    arrived = []
    for i, (start, size) in enumerate(zip(starts, sizes)):
        table = lax.slice_in_dim(tables, start, start + size, axis=1)
        if split:
            shapes = [jax.ShapeDtypeStruct((n_lon, share, size, lanes), jnp.float32)] * n_comp
        else:
            shapes = [jax.ShapeDtypeStruct((rows, n_lon, size, lanes), jnp.float32)]
        pieces = pl.pallas_call(
            functools.partial(
                propagate_kernel, window, n_lon, n_comp, split, start, half, 0 if i else 3
            ),
            out_shape=shapes,
            in_specs=[
                scalars,
                whole,
                whole,
                whole,
                [anywhere] * n_lon,
                [[whole] * len(found) for found in lat_in[i]],
                anywhere,
            ],
            out_specs=[whole] * len(shapes),
            scratch_shapes=propagate_scratch(window, size, lanes, n_lon),
            compiler_params=params(),
            cost_estimate=cost(1.5 + 0.11 * size),
        )(
            place,
            table,
            faces,
            window_fields,
            own_in,
            lat_in[i],
            matrix if i == 0 else pieces[0],
        )
        if split:
            sent = pieces[1:]
            if i > 0:
                sent = gated(sent, moved[1 : n_comp - 1])
            moved = [pieces[0]]
            for r in range(1, n_comp):
                pairs = [(a, (a + r) % n_comp) for a in range(n_comp)]
                moved.append(lax.ppermute(sent[r - 1], "comp", pairs))
        else:
            energy = pieces[0].reshape(rows, n_lon, size, groups, span)
            energy = jnp.transpose(energy, (0, 3, 1, 2, 4)).reshape(n_comp, n_lon, 1, size, span)
            energy = lax.all_to_all(energy, "comp", split_axis=0, concat_axis=0, tiled=True)
            moved = [energy[s] for s in range(n_comp)]
        after = []
        if i == len(sizes) - 1:
            matrix_t = pl.pallas_call(
                functools.partial(transposed_kernel, home_of, half, half_own),
                grid=(2, n_comp),
                out_shape=pltpu.VMEM((2, total, total), jnp.bfloat16),
                in_specs=[scalars, by_cols, by_cols, anywhere],
                out_specs=by_block,
                compiler_params=params(),
                cost_estimate=cost(4),
            )(place, index, weight, pieces[0])
            after = [matrix_t]
        crossed = []
        for d in range(1, n_lon):
            pairs = [(b, (b + d) % n_lon) for b in range(n_lon)]
            packed = pl.pallas_call(
                functools.partial(cross_pack_kernel, d),
                out_shape=jax.ShapeDtypeStruct((n_comp, share, size, span), jnp.float32),
                in_specs=[[anywhere] * n_comp, [anywhere] * len(after)],
                out_specs=whole,
                scratch_shapes=[pltpu.SemaphoreType.DMA((n_comp,))],
                compiler_params=params(),
                cost_estimate=cost(1),
            )(moved, after)
            crossed.append(lax.ppermute(packed, "lon", pairs))
        arrived += moved + crossed

    cells = share * span
    energy, source, source_low = pl.pallas_call(
        functools.partial(forward_kernel, sizes, n_lon, home_of),
        out_shape=(
            jax.ShapeDtypeStruct((total, cells), jnp.float32),
            jax.ShapeDtypeStruct((total, cells), jnp.float32),
            jax.ShapeDtypeStruct((total, cells), jnp.bfloat16),
        ),
        in_specs=[scalars, whole, whole] + [whole] * len(arrived),
        out_specs=(whole, whole, whole),
        scratch_shapes=[pltpu.VMEM((total, cells), jnp.bfloat16)],
        compiler_params=params(),
        cost_estimate=cost(4),
    )(place, matrix, strength, *arrived)

    back = []
    for s in range(n_comp):
        back.append(
            pl.pallas_call(
                functools.partial(backward_kernel, s),
                out_shape=jax.ShapeDtypeStruct((share, block, span), jnp.float32),
                in_specs=[whole] * 4,
                out_specs=whole,
                compiler_params=params(),
                cost_estimate=cost(0.6),
            )(matrix_t, source_low, energy, source)
        )

    if split:
        home = [back[0]]
        for r in range(1, n_comp):
            home.append(lax.ppermute(back[r], "comp", [(a, (a - r) % n_comp) for a in range(n_comp)]))
        if half == half_own:
            out = pl.pallas_call(
                functools.partial(gather_kernel, rows),
                out_shape=jax.ShapeDtypeStruct((comps_local * rows, lanes), jnp.float32),
                in_specs=[scalars] + [whole] * n_comp,
                out_specs=whole,
                compiler_params=params(),
                cost_estimate=cost(2),
            )(place, *home)
            return out.reshape(comps_local, rows, lanes)
        home = jnp.stack(home).reshape(n_comp, share, n_lon, half, lanes)[:, :, :, :half_own]
        home = jnp.roll(home, comp, 0)
        return jnp.transpose(home, (2, 3, 0, 1, 4)).reshape(comps_local, rows, lanes)
    home = lax.all_to_all(jnp.concatenate(back), "comp", split_axis=0, concat_axis=0, tiled=True)
    home = home.reshape(rows, groups, n_lon, half, span)[:, :, :, :half_own]
    return jnp.transpose(home, (2, 3, 0, 1, 4)).reshape(comps_local, rows, lanes)


def solution(mesh):
    placed = (
        P(("ens", "comp"), "lat", "lon"),
        P("lat", "lon"),
        P("lat", "lon"),
        P("lat", "lon"),
        P(),
        P(),
        P(),
        P(),
        P(),
    )
    return jax.shard_map(
        local,
        mesh=mesh,
        in_specs=placed,
        out_specs=P(("ens", "comp"), "lat", "lon"),
        check_vma=False,
    )
```

```python
import functools
import math

import jax
import jax.numpy as jnp
from jax import lax
from jax.experimental import pallas as pl
from jax.experimental.pallas import tpu as pltpu
from jax.sharding import PartitionSpec as P

NDIR = 36
SUBSTEPS = 4
RIM = 2 * SUBSTEPS
GROUP = 16
CHUNKS = 3

plus_factor = 0.4096
minus_factor = 3.160494
cross_factor = 2.007843

VMEM_LIMIT = 16 * 1024 * 1024
whole = pl.BlockSpec(memory_space=pltpu.VMEM)
anywhere = pl.BlockSpec(memory_space=pl.ANY)
scalars = pl.BlockSpec(memory_space=pltpu.SMEM)


def params():
    return pltpu.CompilerParams(vmem_limit_bytes=VMEM_LIMIT)


def cost(micros):
    return pl.CostEstimate(flops=0, bytes_accessed=int(micros * 3.5e6), transcendentals=0)


def chunk_sizes(total):
    groups = total // GROUP
    count = min(CHUNKS, groups)
    return [GROUP * (groups // count + (i < groups % count)) for i in range(count)]


class Window:
    def __init__(self, n_lat, rows):
        self.pair = n_lat == 2
        self.rows = rows
        self.size = 2 * rows + 4 if self.pair else 3 * rows

    def own(self, lat):
        return jnp.where(lat == 0, 2, 2 + self.rows) if self.pair else self.rows

    def received(self, lat):
        if self.pair:
            return [jnp.where(lat == 0, 2 + self.rows, 2)]
        return [0, 2 * self.rows]

    def zeros(self, lat):
        if not self.pair:
            return []
        first = jnp.where(lat == 0, 0, 2 + 2 * self.rows)
        return [first, first + 1]

    def steps(self, lat, substep):
        shrink = 2 * (substep + 1)
        if self.pair:
            return jnp.where(lat == 0, 2, 2 + shrink), 2 * self.rows - shrink
        return shrink, 3 * self.rows - 2 * shrink


def faces_kernel(window, n_lon, place, own, received, after, out, fields):
    lat = place[0]
    rows, lanes = window.rows, own[0].shape[1]
    for row in window.zeros(lat):
        fields[row] = jnp.zeros((3, n_lon * lanes), jnp.float32)
    for offset, blocks in [(window.own(lat), own)] + list(zip(window.received(lat), received)):
        for d, ref in enumerate(blocks):
            for f in range(3):
                for row in range(rows):
                    at = f * rows + row
                    fields[offset + row, f : f + 1, d * lanes : (d + 1) * lanes] = ref[at : at + 1, :]
    width = n_lon * lanes
    n_class = out.shape[2] // 6
    classes = lax.broadcasted_iota(jnp.int32, (n_class, width), 0).astype(jnp.float32)

    def hots(row):
        wet = fields[row, 0:1, :]
        hot_depth = (classes == fields[row, 1:2, :]).astype(jnp.float32)
        hot_current = (classes == fields[row, 2:3, :]).astype(jnp.float32)
        return wet, jnp.concatenate([hot_depth, hot_current], axis=0)

    def step(row, _):
        wet, hot = hots(row)
        wet_next, hot_next = hots(row + 1)
        east_wet = 0.5 * wet * pltpu.roll(wet, width - 1, 1)
        east = ((hot + pltpu.roll(hot, width - 1, 1)) * east_wet).astype(jnp.bfloat16)
        north = ((hot + hot_next) * (0.5 * wet * wet_next)).astype(jnp.bfloat16)
        span = 2 * n_class
        for copy in range(3):
            out[row, 0, copy * span : (copy + 1) * span, :] = east
            out[row, 1, copy * span : (copy + 1) * span, :] = north
        return 0

    lax.fori_loop(0, window.size - 1, step, 0, unroll=4)
    out[window.size - 1] = jnp.zeros(out.shape[1:], jnp.bfloat16)


def pack_raw_kernel(half, rows, flat, sea, depth, current, out, fields_out, held, sems):
    fields = [sea, depth, current]
    lead = len(fields) * rows
    parts = flat.shape[0] // (half * rows)
    length = (out.shape[0] - lead) // parts
    copies = []
    for i in range(parts):
        to = out.at[pl.ds(lead + i * length, length)]
        copies.append(pltpu.make_async_copy(flat.at[pl.ds(i * half * rows, length)], to, sems.at[0, i]))
    for i, ref in enumerate(fields):
        copies.append(pltpu.make_async_copy(ref, held.at[i], sems.at[1, i]))
    for copy in copies:
        copy.start()
    for copy in copies:
        copy.wait()
    for i in range(len(fields)):
        at = slice(i * rows, (i + 1) * rows)
        out[at, :] = held[i].astype(jnp.float32)
        fields_out[at, :] = held[i].astype(jnp.float32)


def pack_kernel(starts, half, rows, place, own_in, after, *refs):
    outs, sems = refs[:-1], refs[-1]
    copies = []
    for i, (start, out) in enumerate(zip(starts, outs)):
        length = out.shape[0] // len(own_in)
        first = pl.multiple_of((place[2] * half + start) * rows, 8)
        for d, ref in enumerate(own_in):
            there = ref.at[pl.ds(first, length)]
            copies.append(pltpu.make_async_copy(there, out.at[pl.ds(d * length, length)], sems.at[i, d]))
    for copy in copies:
        copy.start()
    for copy in copies:
        copy.wait()


def cross_pack_kernel(d, pieces, after, out, sems):
    copies = []
    for s, ref in enumerate(pieces):
        copies.append(pltpu.make_async_copy(ref.at[d], out.at[s], sems.at[s]))
        copies[-1].start()
    for copy in copies:
        copy.wait()


def gate_kernel(*refs):
    pass


def gated(arrays, after):
    return pl.pallas_call(
        gate_kernel,
        out_shape=[jax.ShapeDtypeStruct(a.shape, a.dtype) for a in arrays],
        in_specs=[anywhere] * (len(arrays) + len(after)),
        out_specs=[anywhere] * len(arrays),
        input_output_aliases={i: i for i in range(len(arrays))},
        compiler_params=params(),
        cost_estimate=cost(0.1),
    )(*arrays, *after)


def median_zero(a, b):
    return jnp.maximum(jnp.minimum(a, b), jnp.minimum(jnp.maximum(a, b), 0.0))


def flux(u, c, low, high, slope_low, slope_high):
    rising = u > 0.0
    return u * jnp.where(rising, low, high) + c * jnp.where(rising, slope_low, slope_high)


def propagate_scratch(window, size, lanes, n_lon):
    width = n_lon * lanes
    energy = pltpu.VMEM((window.size, GROUP, width), jnp.float32)
    speed = pltpu.VMEM((window.size, size, width), jnp.float32)
    block = pltpu.VMEM((size * window.rows, lanes), jnp.float32)
    return [energy, energy, speed, speed, speed, speed] + [block] * n_lon + [pltpu.SemaphoreType.DMA((n_lon,))]


def propagate_kernel(
    window, n_lon, n_comp, split, start, half, head, place, tables, faces, wet, own_in, lat_in, after, *refs
):
    outs, scratch = refs[: -7 - n_lon], refs[-7 - n_lon :]
    energy, other, east_u, east_c, north_u, north_c = scratch[:6]
    own_blocks, sems = scratch[6:-1], scratch[-1]
    lat, comp, lon = place[0], place[1], place[2]
    rows, lanes = window.rows, wet.shape[2] // n_lon
    width = n_lon * lanes
    count = east_u.shape[1]
    copies = []
    for d in range(n_lon):
        first = pl.multiple_of((lon * half + start) * rows, 8)
        copies.append(pltpu.make_async_copy(own_in[d].at[pl.ds(first, count * rows)], own_blocks[d], sems.at[d]))
        copies[-1].start()

    def speeds(row, _):
        for which, u_ref, c_ref in ((0, east_u, east_c), (1, north_u, north_c)):
            u = jnp.dot(tables[which], faces[row, which], preferred_element_type=jnp.float32)
            size = jnp.abs(u)
            u_ref[row] = u
            c_ref[row] = 0.5 * size * (1.0 - size)
        return 0

    lax.fori_loop(0, window.size, speeds, 0, unroll=True)

    for copy in copies:
        copy.wait()
    own = window.own(lat)

    def group(g, _):
        first = pl.multiple_of(g * GROUP, GROUP)
        here = pl.ds(first, GROUP)
        for row in window.zeros(lat):
            energy[row] = jnp.zeros((GROUP, width), jnp.float32)
            other[row] = jnp.zeros((GROUP, width), jnp.float32)
        sources = [(own, [(ref, 0) for ref in own_blocks])]
        for offset, blocks in zip(window.received(lat), lat_in):
            if head:
                sources.append((offset, [(ref, head + lon * count) for ref in blocks]))
            else:
                sources.append((offset, [(blocks[0], d * count) for d in range(n_lon)]))
        for offset, blocks in sources:
            for d, (ref, lead) in enumerate(blocks):
                for row in range(rows):
                    at = pl.ds((lead + first) * rows + row, GROUP, stride=rows)
                    sea = wet[offset + row, 0:1, d * lanes : (d + 1) * lanes]
                    energy[offset + row, :, d * lanes : (d + 1) * lanes] = ref[at, :] * sea

        for substep in range(SUBSTEPS):
            base, length = window.steps(lat, substep)
            old, new = (energy, other) if substep % 2 == 0 else (other, energy)
            prior = [old[base + i] for i in (-2, -1, 0, 1)]
            gap = [b - a for a, b in zip(prior, prior[1:])]
            slope_prior, slope_here = median_zero(gap[1], gap[0]), median_zero(gap[2], gap[1])
            south = flux(
                north_u[base - 1, here], north_c[base - 1, here], prior[1], prior[2], slope_prior, slope_here
            )

            def row_step(i, carry):
                south, this, after, gap_after, slope_this = carry
                row = base + i
                beyond = old[row + 2]
                gap_beyond = beyond - after
                slope_after = median_zero(gap_beyond, gap_after)
                north = flux(north_u[row, here], north_c[row, here], this, after, slope_this, slope_after)
                east_cell = pltpu.roll(this, width - 1, 1)
                gap_east = east_cell - this
                gap_west = pltpu.roll(gap_east, 1, 1)
                slope = median_zero(gap_east, gap_west)
                slope_east = pltpu.roll(slope, width - 1, 1)
                east = flux(east_u[row, here], east_c[row, here], this, east_cell, slope, slope_east)
                west = pltpu.roll(east, 1, 1)
                new[row] = this - (east - west) - (north - south)
                return north, after, beyond, gap_beyond, slope_after

            lax.fori_loop(0, length, row_step, (south, prior[2], prior[3], gap[2], slope_here), unroll=True)

        if split:
            share = rows // n_comp
            for r in range(n_comp):
                base = own + lax.rem(comp + r, n_comp) * share
                for d in range(n_lon):
                    for k in range(share):
                        outs[r][d, k, here, :] = energy[base + k, :, d * lanes : (d + 1) * lanes]
        else:
            for row in range(rows):
                for d in range(n_lon):
                    outs[0][row, d, here, :] = energy[own + row, :, d * lanes : (d + 1) * lanes]
        return 0

    lax.fori_loop(0, count // GROUP, group, 0)


def matrix_kernel(home, place, names, index, weight, after, out, columns):
    height = out.shape[1]

    @pl.when(pl.program_id(1) == 0)
    def _():
        columns[...] = jnp.transpose(jnp.concatenate([index[0], weight[0]], axis=0))

    base = pl.multiple_of(home(place, pl.program_id(1)) * height, GROUP)

    def step(i, _):
        at = pl.multiple_of(i * GROUP, GROUP)
        column = columns[pl.ds(base + at, GROUP), :]
        name = names[...]
        made = jnp.zeros((GROUP, name.shape[1]), jnp.float32)
        for corner in range(4):
            made = jnp.where(name == column[:, corner : corner + 1], column[:, corner + 4 : corner + 5], made)
        out[0, pl.ds(at, GROUP), :] = made.astype(jnp.bfloat16)
        return 0

    lax.fori_loop(0, height // GROUP, step, 0, unroll=True)


def transposed_kernel(home, half, half_own, place, index, weight, after, out):
    height, total = out.shape[1], out.shape[2]
    base = home(place, pl.program_id(1)) * height

    def step(i, _):
        at = pl.multiple_of(i * GROUP, GROUP)
        row = base + at + lax.broadcasted_iota(jnp.int32, (GROUP, 1), 0)
        if half != half_own:
            row = jnp.where(row % half < half_own, row // half * half_own + row % half, -1)
        row = jnp.broadcast_to(row.astype(jnp.float32), (GROUP, total))
        made = jnp.zeros((GROUP, total), jnp.float32)
        for corner in range(4):
            made = jnp.where(row == index[0, corner : corner + 1, :], weight[0, corner : corner + 1, :], made)
        out[0, pl.ds(at, GROUP), :] = made.astype(jnp.bfloat16)
        return 0

    lax.fori_loop(0, height // GROUP, step, 0, unroll=3)


def forward_kernel(sizes, n_lon, home, place, matrix, coupling, *refs):
    pieces = refs[:-4]
    energy_out, source_out, source_low_out, low = refs[-4:]
    per_chunk = len(pieces) // len(sizes)
    n_comp = per_chunk - n_lon + 1
    block = coupling.shape[0] // n_comp
    half = block // n_lon
    share, lanes = pieces[0].shape[1], pieces[0].shape[3]
    for s in range(n_comp):
        for d in range(n_lon):
            first = lax.rem(place[2] + n_lon - d, n_lon) * half
            for i, size in enumerate(sizes):
                group = pieces[i * per_chunk : (i + 1) * per_chunk]
                to = first + sum(sizes[:i])
                here = pl.ds(pl.multiple_of(s * block + to, GROUP), size)
                there = pl.ds(pl.multiple_of(home(place, s) * block + to, GROUP), size)
                for k in range(share):
                    part = group[s][0, k] if d == 0 else group[d - n_lon][s, k]
                    energy_out[here, k * lanes : (k + 1) * lanes] = part
                    low[there, k * lanes : (k + 1) * lanes] = part.astype(jnp.bfloat16)
    for s in range(n_comp):
        here = slice(s * block, (s + 1) * block)
        there = pl.ds(pl.multiple_of(home(place, s) * block, GROUP), block)
        energy = energy_out[here, :]
        plus_side = jnp.dot(matrix[0, here, :], low[...], preferred_element_type=jnp.float32)
        minus_side = jnp.dot(matrix[1, here, :], low[...], preferred_element_type=jnp.float32)
        source = coupling[there, :] * (
            energy * energy * (plus_factor * plus_side + minus_factor * minus_side)
            - cross_factor * energy * plus_side * minus_side
        )
        source_out[here, :] = source
        source_low_out[there, :] = source.astype(jnp.bfloat16)


def backward_kernel(s, matrix_t, source_low, energy, source, out):
    block, lanes = out.shape[1], out.shape[2]
    here = slice(s * block, (s + 1) * block)
    gain = (
        jnp.dot(matrix_t[0, here, :], source_low[...], preferred_element_type=jnp.float32)
        + jnp.dot(matrix_t[1, here, :], source_low[...], preferred_element_type=jnp.float32)
        - 2.0 * source[here, :]
    )
    result = energy[here, :] + gain / (1.0 + jnp.abs(gain))
    for k in range(out.shape[0]):
        out[k] = result[:, k * lanes : (k + 1) * lanes]


def gather_kernel(rows, order, place, *refs):
    pieces, out = refs[:-1], refs[-1]
    comp = place[1]
    n_comp = len(pieces)
    share = rows // n_comp
    for r, piece in zip(order, pieces):
        for k in range(share):
            row = lax.rem(comp + r, n_comp) * share + k
            for i in range(0, piece.shape[1], GROUP):
                out[pl.ds(i * rows + row, GROUP, stride=rows), :] = piece[k, i : i + GROUP, :]


def local(
    spectrum,
    sea_mask,
    depth_class,
    current_class,
    speed_table,
    current_table,
    coupling,
    quad_index,
    quad_weight,
):
    comps_local, rows, lanes = spectrum.shape
    n_comp, n_lat, n_lon = (lax.axis_size(a) for a in ("comp", "lat", "lon"))
    comp, lat, lon = (lax.axis_index(a) for a in ("comp", "lat", "lon"))
    place = jnp.stack([lat, comp, lon]).astype(jnp.int32)
    half_own = comps_local // n_lon
    half = -(-half_own // GROUP) * GROUP
    sizes = chunk_sizes(half)
    starts = [sum(sizes[:i]) for i in range(len(sizes))]
    window = Window(n_lat, rows)
    width = n_lon * lanes
    split = rows % n_comp == 0

    if half == half_own:
        flat = spectrum.reshape(comps_local * rows, lanes)
    else:
        flat = spectrum.reshape(n_lon, half_own, rows, lanes)
        flat = jnp.pad(flat, ((0, 0), (0, half - half_own), (0, 0), (0, 0))).reshape(-1, lanes)
    if window.pair:
        moves = [[(0, 1), (1, 0)]]
    else:
        moves = [[(i, i + 1) for i in range(n_lat - 1)], [(i + 1, i) for i in range(n_lat - 1)]]
    lengths = [n_lon * size * rows for size in sizes]


    def on_all_columns(block):
        found = [block]
        for d in range(n_lon - 1, 0, -1):
            found.append(lax.ppermute(block, "lon", [(i, (i + d) % n_lon) for i in range(n_lon)]))
        return found

    first_block, fields = pl.pallas_call(
        functools.partial(pack_raw_kernel, half, rows),
        out_shape=(
            jax.ShapeDtypeStruct((lengths[0] + 3 * rows, lanes), jnp.float32),
            jax.ShapeDtypeStruct((3 * rows, lanes), jnp.float32),
        ),
        in_specs=[anywhere] * 4,
        out_specs=(whole, whole),
        scratch_shapes=[pltpu.VMEM((3, rows, lanes), jnp.int32), pltpu.SemaphoreType.DMA((2, max(n_lon, 3)))],
        compiler_params=params(),
        cost_estimate=cost(1),
    )(*[pltpu.with_memory_space_constraint(a, pltpu.HBM) for a in (flat, sea_mask, depth_class, current_class)])
    own_in, own_fields = on_all_columns(flat), on_all_columns(fields)
    blocks = [first_block]
    if len(sizes) > 1:
        blocks += pl.pallas_call(
            functools.partial(pack_kernel, starts[1:], half, rows),
            out_shape=[jax.ShapeDtypeStruct((length, lanes), jnp.float32) for length in lengths[1:]],
            in_specs=[scalars, [anywhere] * n_lon, [anywhere] * (n_lon + 1)],
            out_specs=[whole] * len(lengths[1:]),
            scratch_shapes=[pltpu.SemaphoreType.DMA((len(lengths) - 1, n_lon))],
            compiler_params=params(),
            cost_estimate=cost(1.5),
        )(place, own_in, [first_block] + own_fields)
    lat_in = [[lax.ppermute(block, "lat", move) for move in moves] for block in blocks]

    def home_of(place, s):
        return lax.rem(place[1] + n_comp - s, n_comp) if split else s

    total = n_comp * n_lon * half
    block = n_lon * half

    def spread(array):
        if half == half_own:
            return array
        array = array.reshape(array.shape[:-1] + (n_comp * n_lon, half_own))
        array = jnp.pad(array, ((0, 0),) * (array.ndim - 1) + ((0, half - half_own),), constant_values=-1)
        return array.reshape(array.shape[:-2] + (total,))

    names = spread(jnp.arange(n_comp * comps_local, dtype=jnp.float32)[None])
    index = spread(jnp.swapaxes(quad_index, 1, 2).astype(jnp.float32))
    weight = jnp.maximum(spread(jnp.swapaxes(quad_weight, 1, 2)), 0.0)
    strength = spread(coupling[None]).reshape(total, 1)
    by_cols = pl.BlockSpec((1, 4, total), lambda s, i: (s, 0, 0))
    by_block = pl.BlockSpec((1, block, total), lambda s, i: (s, i, 0))
    matrix = pl.pallas_call(
        functools.partial(matrix_kernel, home_of),
        grid=(2, n_comp),
        out_shape=pltpu.VMEM((2, total, total), jnp.bfloat16),
        in_specs=[scalars, whole, by_cols, by_cols, anywhere],
        out_specs=by_block,
        scratch_shapes=[pltpu.VMEM((total, 8), jnp.float32)],
        compiler_params=params(),
        cost_estimate=cost(6),
    )(place, names, index, weight, blocks[-1])

    lat_in[0] = [on_all_columns(block) for block in gated(lat_in[0], [matrix])]
    lat_in[1:] = [[[block] for block in found] for found in lat_in[1:]]

    n_class = speed_table.shape[0]
    head_block = pl.BlockSpec((3 * rows, lanes), lambda i: (0, 0))
    faces, window_fields = pl.pallas_call(
        functools.partial(faces_kernel, window, n_lon),
        grid=(1,),
        out_shape=(
            jax.ShapeDtypeStruct((window.size, 2, 6 * n_class, width), jnp.bfloat16),
            jax.ShapeDtypeStruct((window.size, 3, width), jnp.float32),
        ),
        in_specs=[scalars, [whole] * n_lon, [[head_block] * n_lon] * len(moves), anywhere],
        out_specs=(whole, whole),
        compiler_params=params(),
        cost_estimate=cost(2),
    )(place, own_fields, lat_in[0], matrix)

    ids = comp * comps_local + lon * half_own + jnp.arange(half, dtype=jnp.int32)
    freq_hot = ((ids // NDIR)[:, None] == jnp.arange(speed_table.shape[1], dtype=jnp.int32)[None, :]).astype(
        jnp.float32
    )
    speed = jnp.dot(freq_hot, speed_table.T, precision=lax.Precision.HIGHEST)
    angles = 2.0 * math.pi / NDIR * (ids % NDIR).astype(jnp.float32)
    tables = []
    for which, turn in ((0, jnp.cos(angles)), (1, jnp.sin(angles))):
        currents = jnp.broadcast_to(current_table[:, which][None], (half, n_class))
        left = jnp.concatenate([speed * turn[:, None], currents], axis=1)
        levels = []
        for _ in range(3):
            level = lax.reduce_precision(left, 8, 7)
            levels.append(level)
            left = left - level
        tables.append(jnp.concatenate(levels, axis=1).astype(jnp.bfloat16))
    tables = jnp.stack(tables)

    if split:
        share, span = rows // n_comp, lanes
    else:
        groups = n_comp // rows
        share, span = 1, lanes // groups
    far_first = sorted(range(1, n_comp), key=lambda r: abs(2 * r - n_comp))
    arrived = []
    for i, (start, size) in enumerate(zip(starts, sizes)):
        table = lax.slice_in_dim(tables, start, start + size, axis=1)
        if split:
            shapes = [jax.ShapeDtypeStruct((n_lon, share, size, lanes), jnp.float32)] * n_comp
        else:
            shapes = [jax.ShapeDtypeStruct((rows, n_lon, size, lanes), jnp.float32)]
        pieces = pl.pallas_call(
            functools.partial(
                propagate_kernel, window, n_lon, n_comp, split, start, half, 0 if i else 3
            ),
            out_shape=shapes,
            in_specs=[
                scalars,
                whole,
                whole,
                whole,
                [anywhere] * n_lon,
                [[whole] * len(found) for found in lat_in[i]],
                anywhere,
            ],
            out_specs=[whole] * len(shapes),
            scratch_shapes=propagate_scratch(window, size, lanes, n_lon),
            compiler_params=params(),
            cost_estimate=cost(1.5 + 0.11 * size),
        )(
            place,
            table,
            faces,
            window_fields,
            own_in,
            lat_in[i],
            matrix if i == 0 else pieces[0],
        )
        if split:
            sent = pieces[1:]
            if i > 0:
                sent = gated(sent, [moved[r] for r in far_first[:2]])
            moved = [pieces[0]] + [None] * (n_comp - 1)
            for r in far_first:
                pairs = [(a, (a + r) % n_comp) for a in range(n_comp)]
                moved[r] = lax.ppermute(sent[r - 1], "comp", pairs)
        else:
            energy = pieces[0].reshape(rows, n_lon, size, groups, span)
            energy = jnp.transpose(energy, (0, 3, 1, 2, 4)).reshape(n_comp, n_lon, 1, size, span)
            energy = lax.all_to_all(energy, "comp", split_axis=0, concat_axis=0, tiled=True)
            moved = [energy[s] for s in range(n_comp)]
        after = []
        if i == len(sizes) - 1:
            matrix_t = pl.pallas_call(
                functools.partial(transposed_kernel, home_of, half, half_own),
                grid=(2, n_comp),
                out_shape=pltpu.VMEM((2, total, total), jnp.bfloat16),
                in_specs=[scalars, by_cols, by_cols, anywhere],
                out_specs=by_block,
                compiler_params=params(),
                cost_estimate=cost(4),
            )(place, index, weight, pieces[0])
            after = [matrix_t]
        crossed = []
        for d in range(1, n_lon):
            pairs = [(b, (b + d) % n_lon) for b in range(n_lon)]
            packed = pl.pallas_call(
                functools.partial(cross_pack_kernel, d),
                out_shape=jax.ShapeDtypeStruct((n_comp, share, size, span), jnp.float32),
                in_specs=[[anywhere] * n_comp, [anywhere] * len(after)],
                out_specs=whole,
                scratch_shapes=[pltpu.SemaphoreType.DMA((n_comp,))],
                compiler_params=params(),
                cost_estimate=cost(1),
            )(moved, after)
            crossed.append(lax.ppermute(packed, "lon", pairs))
        arrived += moved + crossed

    cells = share * span
    energy, source, source_low = pl.pallas_call(
        functools.partial(forward_kernel, sizes, n_lon, home_of),
        out_shape=(
            jax.ShapeDtypeStruct((total, cells), jnp.float32),
            jax.ShapeDtypeStruct((total, cells), jnp.float32),
            jax.ShapeDtypeStruct((total, cells), jnp.bfloat16),
        ),
        in_specs=[scalars, whole, whole] + [whole] * len(arrived),
        out_specs=(whole, whole, whole),
        scratch_shapes=[pltpu.VMEM((total, cells), jnp.bfloat16)],
        compiler_params=params(),
        cost_estimate=cost(4),
    )(place, matrix, strength, *arrived)

    back = []
    for s in range(n_comp):
        back.append(
            pl.pallas_call(
                functools.partial(backward_kernel, s),
                out_shape=jax.ShapeDtypeStruct((share, block, span), jnp.float32),
                in_specs=[whole] * 4,
                out_specs=whole,
                compiler_params=params(),
                cost_estimate=cost(0.6),
            )(matrix_t, source_low, energy, source)
        )

    if split:
        home = [back[0]] + [None] * (n_comp - 1)
        for r in far_first:
            home[r] = lax.ppermute(back[r], "comp", [(a, (a - r) % n_comp) for a in range(n_comp)])
        if half == half_own:
            out = pl.pallas_call(
                functools.partial(gather_kernel, rows, [0] + far_first),
                out_shape=jax.ShapeDtypeStruct((comps_local * rows, lanes), jnp.float32),
                in_specs=[scalars] + [whole] * n_comp,
                out_specs=whole,
                compiler_params=params(),
                cost_estimate=cost(2),
            )(place, *[home[r] for r in [0] + far_first])
            return out.reshape(comps_local, rows, lanes)
        home = jnp.stack(home).reshape(n_comp, share, n_lon, half, lanes)[:, :, :, :half_own]
        home = jnp.roll(home, comp, 0)
        return jnp.transpose(home, (2, 3, 0, 1, 4)).reshape(comps_local, rows, lanes)
    home = lax.all_to_all(jnp.concatenate(back), "comp", split_axis=0, concat_axis=0, tiled=True)
    home = home.reshape(rows, groups, n_lon, half, span)[:, :, :, :half_own]
    return jnp.transpose(home, (2, 3, 0, 1, 4)).reshape(comps_local, rows, lanes)


def solution(mesh):
    placed = (
        P(("ens", "comp"), "lat", "lon"),
        P("lat", "lon"),
        P("lat", "lon"),
        P("lat", "lon"),
        P(),
        P(),
        P(),
        P(),
        P(),
    )
    return jax.shard_map(
        local,
        mesh=mesh,
        in_specs=placed,
        out_specs=P(("ens", "comp"), "lat", "lon"),
        check_vma=False,
    )
```

```python
import functools
import math

import jax
import jax.numpy as jnp
from jax import lax
from jax.experimental import pallas as pl
from jax.experimental.pallas import tpu as pltpu
from jax.sharding import PartitionSpec as P

NDIR = 36
SUBSTEPS = 4
RIM = 2 * SUBSTEPS
GROUP = 16
CHUNKS = 3

plus_factor = 0.4096
minus_factor = 3.160494
cross_factor = 2.007843

VMEM_LIMIT = 16 * 1024 * 1024
whole = pl.BlockSpec(memory_space=pltpu.VMEM)
anywhere = pl.BlockSpec(memory_space=pl.ANY)
scalars = pl.BlockSpec(memory_space=pltpu.SMEM)


def params():
    return pltpu.CompilerParams(vmem_limit_bytes=VMEM_LIMIT)


def cost(micros):
    return pl.CostEstimate(flops=0, bytes_accessed=int(micros * 3.5e6), transcendentals=0)


def chunk_sizes(total):
    groups = total // GROUP
    count = min(CHUNKS, groups)
    return [GROUP * (groups // count + (i < groups % count)) for i in range(count)]


class Window:
    def __init__(self, n_lat, rows):
        self.pair = n_lat == 2
        self.rows = rows
        self.size = 2 * rows + 4 if self.pair else 3 * rows

    def own(self, lat):
        return jnp.where(lat == 0, 2, 2 + self.rows) if self.pair else self.rows

    def received(self, lat):
        if self.pair:
            return [jnp.where(lat == 0, 2 + self.rows, 2)]
        return [0, 2 * self.rows]

    def zeros(self, lat):
        if not self.pair:
            return []
        first = jnp.where(lat == 0, 0, 2 + 2 * self.rows)
        return [first, first + 1]

    def steps(self, lat, substep):
        shrink = 2 * (substep + 1)
        if self.pair:
            return jnp.where(lat == 0, 2, 2 + shrink), 2 * self.rows - shrink
        return shrink, 3 * self.rows - 2 * shrink


def faces_kernel(window, n_lon, place, own, received, after, out, fields):
    lat = place[0]
    rows, lanes = window.rows, own[0].shape[1]
    for row in window.zeros(lat):
        fields[row] = jnp.zeros((3, n_lon * lanes), jnp.float32)
    for offset, blocks in [(window.own(lat), own)] + list(zip(window.received(lat), received)):
        for d, ref in enumerate(blocks):
            for f in range(3):
                for row in range(rows):
                    at = f * rows + row
                    fields[offset + row, f : f + 1, d * lanes : (d + 1) * lanes] = ref[at : at + 1, :]
    width = n_lon * lanes
    n_class = out.shape[2] // 6
    classes = lax.broadcasted_iota(jnp.int32, (n_class, width), 0).astype(jnp.float32)

    def hots(row):
        wet = fields[row, 0:1, :]
        hot_depth = (classes == fields[row, 1:2, :]).astype(jnp.float32)
        hot_current = (classes == fields[row, 2:3, :]).astype(jnp.float32)
        return wet, jnp.concatenate([hot_depth, hot_current], axis=0)

    def step(row, _):
        wet, hot = hots(row)
        wet_next, hot_next = hots(row + 1)
        east_wet = 0.5 * wet * pltpu.roll(wet, width - 1, 1)
        east = ((hot + pltpu.roll(hot, width - 1, 1)) * east_wet).astype(jnp.bfloat16)
        north = ((hot + hot_next) * (0.5 * wet * wet_next)).astype(jnp.bfloat16)
        span = 2 * n_class
        for copy in range(3):
            out[row, 0, copy * span : (copy + 1) * span, :] = east
            out[row, 1, copy * span : (copy + 1) * span, :] = north
        return 0

    lax.fori_loop(0, window.size - 1, step, 0, unroll=4)
    out[window.size - 1] = jnp.zeros(out.shape[1:], jnp.bfloat16)


def pack_raw_kernel(half, rows, flat, sea, depth, current, out, fields_out, held, sems):
    fields = [sea, depth, current]
    lead = len(fields) * rows
    parts = flat.shape[0] // (half * rows)
    length = (out.shape[0] - lead) // parts
    copies = []
    for i in range(parts):
        to = out.at[pl.ds(lead + i * length, length)]
        copies.append(pltpu.make_async_copy(flat.at[pl.ds(i * half * rows, length)], to, sems.at[0, i]))
    for i, ref in enumerate(fields):
        copies.append(pltpu.make_async_copy(ref, held.at[i], sems.at[1, i]))
    for copy in copies:
        copy.start()
    for copy in copies:
        copy.wait()
    for i in range(len(fields)):
        at = slice(i * rows, (i + 1) * rows)
        out[at, :] = held[i].astype(jnp.float32)
        fields_out[at, :] = held[i].astype(jnp.float32)


def pack_kernel(starts, half, rows, place, own_in, after, *refs):
    outs, sems = refs[:-1], refs[-1]
    copies = []
    for i, (start, out) in enumerate(zip(starts, outs)):
        length = out.shape[0] // len(own_in)
        first = pl.multiple_of((place[2] * half + start) * rows, 8)
        for d, ref in enumerate(own_in):
            there = ref.at[pl.ds(first, length)]
            copies.append(pltpu.make_async_copy(there, out.at[pl.ds(d * length, length)], sems.at[i, d]))
    for copy in copies:
        copy.start()
    for copy in copies:
        copy.wait()


def cross_pack_kernel(d, pieces, after, out, sems):
    copies = []
    for s, ref in enumerate(pieces):
        copies.append(pltpu.make_async_copy(ref.at[d], out.at[s], sems.at[s]))
        copies[-1].start()
    for copy in copies:
        copy.wait()


def gate_kernel(*refs):
    pass


def gated(arrays, after):
    return pl.pallas_call(
        gate_kernel,
        out_shape=[jax.ShapeDtypeStruct(a.shape, a.dtype) for a in arrays],
        in_specs=[anywhere] * (len(arrays) + len(after)),
        out_specs=[anywhere] * len(arrays),
        input_output_aliases={i: i for i in range(len(arrays))},
        compiler_params=params(),
        cost_estimate=cost(0.1),
    )(*arrays, *after)


def median_zero(a, b):
    return jnp.maximum(jnp.minimum(a, b), jnp.minimum(jnp.maximum(a, b), 0.0))


def flux(u, c, low, high, slope_low, slope_high):
    rising = u > 0.0
    return u * jnp.where(rising, low, high) + c * jnp.where(rising, slope_low, slope_high)


def propagate_scratch(window, size, lanes, n_lon):
    width = n_lon * lanes
    energy = pltpu.VMEM((window.size, GROUP, width), jnp.float32)
    speed = pltpu.VMEM((window.size, size, width), jnp.float32)
    block = pltpu.VMEM((size * window.rows, lanes), jnp.float32)
    return [energy, energy, speed, speed, speed, speed] + [block] * n_lon + [pltpu.SemaphoreType.DMA((n_lon,))]


def propagate_kernel(
    window, n_lon, n_comp, split, start, half, head, place, tables, faces, wet, own_in, lat_in, after, *refs
):
    outs, scratch = refs[: -7 - n_lon], refs[-7 - n_lon :]
    energy, other, east_u, east_c, north_u, north_c = scratch[:6]
    own_blocks, sems = scratch[6:-1], scratch[-1]
    lat, comp, lon = place[0], place[1], place[2]
    rows, lanes = window.rows, wet.shape[2] // n_lon
    width = n_lon * lanes
    count = east_u.shape[1]
    copies = []
    for d in range(n_lon):
        first = pl.multiple_of((lon * half + start) * rows, 8)
        copies.append(pltpu.make_async_copy(own_in[d].at[pl.ds(first, count * rows)], own_blocks[d], sems.at[d]))
        copies[-1].start()

    def speeds(row, _):
        for which, u_ref, c_ref in ((0, east_u, east_c), (1, north_u, north_c)):
            u = jnp.dot(tables[which], faces[row, which], preferred_element_type=jnp.float32)
            size = jnp.abs(u)
            u_ref[row] = u
            c_ref[row] = 0.5 * size * (1.0 - size)
        return 0

    lax.fori_loop(0, window.size, speeds, 0, unroll=True)

    for copy in copies:
        copy.wait()
    own = window.own(lat)

    def group(g, _):
        first = pl.multiple_of(g * GROUP, GROUP)
        here = pl.ds(first, GROUP)
        for row in window.zeros(lat):
            energy[row] = jnp.zeros((GROUP, width), jnp.float32)
            other[row] = jnp.zeros((GROUP, width), jnp.float32)
        sources = [(own, [(ref, 0) for ref in own_blocks])]
        for offset, blocks in zip(window.received(lat), lat_in):
            if head:
                sources.append((offset, [(ref, head + lon * count) for ref in blocks]))
            else:
                sources.append((offset, [(blocks[0], d * count) for d in range(n_lon)]))
        for offset, blocks in sources:
            for d, (ref, lead) in enumerate(blocks):
                for row in range(rows):
                    at = pl.ds((lead + first) * rows + row, GROUP, stride=rows)
                    sea = wet[offset + row, 0:1, d * lanes : (d + 1) * lanes]
                    energy[offset + row, :, d * lanes : (d + 1) * lanes] = ref[at, :] * sea

        for substep in range(SUBSTEPS):
            base, length = window.steps(lat, substep)
            old, new = (energy, other) if substep % 2 == 0 else (other, energy)
            prior = [old[base + i] for i in (-2, -1, 0, 1)]
            gap = [b - a for a, b in zip(prior, prior[1:])]
            slope_prior, slope_here = median_zero(gap[1], gap[0]), median_zero(gap[2], gap[1])
            south = flux(
                north_u[base - 1, here], north_c[base - 1, here], prior[1], prior[2], slope_prior, slope_here
            )

            def row_step(i, carry):
                south, this, after, gap_after, slope_this = carry
                row = base + i
                beyond = old[row + 2]
                gap_beyond = beyond - after
                slope_after = median_zero(gap_beyond, gap_after)
                north = flux(north_u[row, here], north_c[row, here], this, after, slope_this, slope_after)
                east_cell = pltpu.roll(this, width - 1, 1)
                gap_east = east_cell - this
                gap_west = pltpu.roll(gap_east, 1, 1)
                slope = median_zero(gap_east, gap_west)
                slope_east = pltpu.roll(slope, width - 1, 1)
                east = flux(east_u[row, here], east_c[row, here], this, east_cell, slope, slope_east)
                west = pltpu.roll(east, 1, 1)
                new[row] = this - (east - west) - (north - south)
                return north, after, beyond, gap_beyond, slope_after

            lax.fori_loop(0, length, row_step, (south, prior[2], prior[3], gap[2], slope_here), unroll=True)

        if split:
            share = rows // n_comp
            for r in range(n_comp):
                base = own + lax.rem(comp + r, n_comp) * share
                for d in range(n_lon):
                    for k in range(share):
                        outs[r][d, k, here, :] = energy[base + k, :, d * lanes : (d + 1) * lanes]
        else:
            for row in range(rows):
                for d in range(n_lon):
                    outs[0][row, d, here, :] = energy[own + row, :, d * lanes : (d + 1) * lanes]
        return 0

    lax.fori_loop(0, count // GROUP, group, 0)


def matrix_kernel(home, place, names, index, weight, after, out, columns):
    height = out.shape[1]

    @pl.when(pl.program_id(1) == 0)
    def _():
        columns[...] = jnp.transpose(jnp.concatenate([index[0], weight[0]], axis=0))

    base = pl.multiple_of(home(place, pl.program_id(1)) * height, GROUP)

    def step(i, _):
        at = pl.multiple_of(i * GROUP, GROUP)
        column = columns[pl.ds(base + at, GROUP), :]
        name = names[...]
        made = jnp.zeros((GROUP, name.shape[1]), jnp.float32)
        for corner in range(4):
            made = jnp.where(name == column[:, corner : corner + 1], column[:, corner + 4 : corner + 5], made)
        out[0, pl.ds(at, GROUP), :] = made.astype(jnp.bfloat16)
        return 0

    lax.fori_loop(0, height // GROUP, step, 0, unroll=True)


def transposed_kernel(home, half, half_own, place, index, weight, after, out):
    height, total = out.shape[1], out.shape[2]
    base = home(place, pl.program_id(1)) * height

    def step(i, _):
        at = pl.multiple_of(i * GROUP, GROUP)
        row = base + at + lax.broadcasted_iota(jnp.int32, (GROUP, 128), 0)
        if half != half_own:
            row = jnp.where(row % half < half_own, row // half * half_own + row % half, -1)
        row = jnp.concatenate([row.astype(jnp.float32)] * (-(-total // 128)), axis=1)[:, :total]
        made = jnp.zeros((GROUP, total), jnp.float32)
        for corner in range(4):
            made = jnp.where(row == index[0, corner : corner + 1, :], weight[0, corner : corner + 1, :], made)
        out[0, pl.ds(at, GROUP), :] = made.astype(jnp.bfloat16)
        return 0

    lax.fori_loop(0, height // GROUP, step, 0, unroll=3)


def forward_kernel(sizes, n_lon, home, place, matrix, coupling, *refs):
    pieces = refs[:-4]
    energy_out, source_out, source_low_out, low = refs[-4:]
    per_chunk = len(pieces) // len(sizes)
    n_comp = per_chunk - n_lon + 1
    block = coupling.shape[0] // n_comp
    half = block // n_lon
    share, lanes = pieces[0].shape[1], pieces[0].shape[3]
    for s in range(n_comp):
        for d in range(n_lon):
            first = lax.rem(place[2] + n_lon - d, n_lon) * half
            for i, size in enumerate(sizes):
                group = pieces[i * per_chunk : (i + 1) * per_chunk]
                to = first + sum(sizes[:i])
                here = pl.ds(pl.multiple_of(s * block + to, GROUP), size)
                there = pl.ds(pl.multiple_of(home(place, s) * block + to, GROUP), size)
                for k in range(share):
                    part = group[s][0, k] if d == 0 else group[d - n_lon][s, k]
                    energy_out[here, k * lanes : (k + 1) * lanes] = part
                    low[there, k * lanes : (k + 1) * lanes] = part.astype(jnp.bfloat16)
    for s in range(n_comp):
        here = slice(s * block, (s + 1) * block)
        there = pl.ds(pl.multiple_of(home(place, s) * block, GROUP), block)
        energy = energy_out[here, :]
        plus_side = jnp.dot(matrix[0, here, :], low[...], preferred_element_type=jnp.float32)
        minus_side = jnp.dot(matrix[1, here, :], low[...], preferred_element_type=jnp.float32)
        source = coupling[there, :] * (
            energy * energy * (plus_factor * plus_side + minus_factor * minus_side)
            - cross_factor * energy * plus_side * minus_side
        )
        source_out[here, :] = source
        source_low_out[there, :] = source.astype(jnp.bfloat16)


def backward_kernel(s, matrix_t, source_low, energy, source, out):
    block, lanes = out.shape[1], out.shape[2]
    here = slice(s * block, (s + 1) * block)
    gain = (
        jnp.dot(matrix_t[0, here, :], source_low[...], preferred_element_type=jnp.float32)
        + jnp.dot(matrix_t[1, here, :], source_low[...], preferred_element_type=jnp.float32)
        - 2.0 * source[here, :]
    )
    result = energy[here, :] + gain / (1.0 + jnp.abs(gain))
    for k in range(out.shape[0]):
        out[k] = result[:, k * lanes : (k + 1) * lanes]


def gather_kernel(rows, n_comp, order, place, held, *refs):
    pieces, out = refs[:-1], refs[-1]
    share = rows // n_comp
    for ref in held:
        out[...] = ref[...]
    for r, piece in zip(order, pieces):
        for k in range(share):
            row = lax.rem(place[1] + r, n_comp) * share + k
            for i in range(0, piece.shape[1], GROUP):
                out[pl.ds(i * rows + row, GROUP, stride=rows), :] = piece[k, i : i + GROUP, :]


def local(
    spectrum,
    sea_mask,
    depth_class,
    current_class,
    speed_table,
    current_table,
    coupling,
    quad_index,
    quad_weight,
):
    comps_local, rows, lanes = spectrum.shape
    n_comp, n_lat, n_lon = (lax.axis_size(a) for a in ("comp", "lat", "lon"))
    comp, lat, lon = (lax.axis_index(a) for a in ("comp", "lat", "lon"))
    place = jnp.stack([lat, comp, lon]).astype(jnp.int32)
    half_own = comps_local // n_lon
    half = -(-half_own // GROUP) * GROUP
    sizes = chunk_sizes(half)
    starts = [sum(sizes[:i]) for i in range(len(sizes))]
    window = Window(n_lat, rows)
    width = n_lon * lanes
    split = rows % n_comp == 0

    if half == half_own:
        flat = spectrum.reshape(comps_local * rows, lanes)
    else:
        flat = spectrum.reshape(n_lon, half_own, rows, lanes)
        flat = jnp.pad(flat, ((0, 0), (0, half - half_own), (0, 0), (0, 0))).reshape(-1, lanes)
    if window.pair:
        moves = [[(0, 1), (1, 0)]]
    else:
        moves = [[(i, i + 1) for i in range(n_lat - 1)], [(i + 1, i) for i in range(n_lat - 1)]]
    lengths = [n_lon * size * rows for size in sizes]


    def on_all_columns(block):
        found = [block]
        for d in range(n_lon - 1, 0, -1):
            found.append(lax.ppermute(block, "lon", [(i, (i + d) % n_lon) for i in range(n_lon)]))
        return found

    first_block, fields = pl.pallas_call(
        functools.partial(pack_raw_kernel, half, rows),
        out_shape=(
            jax.ShapeDtypeStruct((lengths[0] + 3 * rows, lanes), jnp.float32),
            jax.ShapeDtypeStruct((3 * rows, lanes), jnp.float32),
        ),
        in_specs=[anywhere] * 4,
        out_specs=(whole, whole),
        scratch_shapes=[pltpu.VMEM((3, rows, lanes), jnp.int32), pltpu.SemaphoreType.DMA((2, max(n_lon, 3)))],
        compiler_params=params(),
        cost_estimate=cost(1),
    )(*[pltpu.with_memory_space_constraint(a, pltpu.HBM) for a in (flat, sea_mask, depth_class, current_class)])
    own_in, own_fields = on_all_columns(flat), on_all_columns(fields)
    blocks = [first_block]
    if len(sizes) > 1:
        blocks += pl.pallas_call(
            functools.partial(pack_kernel, starts[1:], half, rows),
            out_shape=[jax.ShapeDtypeStruct((length, lanes), jnp.float32) for length in lengths[1:]],
            in_specs=[scalars, [anywhere] * n_lon, [anywhere] * (n_lon + 1)],
            out_specs=[whole] * len(lengths[1:]),
            scratch_shapes=[pltpu.SemaphoreType.DMA((len(lengths) - 1, n_lon))],
            compiler_params=params(),
            cost_estimate=cost(1.5),
        )(place, own_in, [first_block] + own_fields)
    lat_in = [[lax.ppermute(block, "lat", move) for move in moves] for block in blocks]

    def home_of(place, s):
        return lax.rem(place[1] + n_comp - s, n_comp) if split else s

    total = n_comp * n_lon * half
    block = n_lon * half

    def spread(array):
        if half == half_own:
            return array
        array = array.reshape(array.shape[:-1] + (n_comp * n_lon, half_own))
        array = jnp.pad(array, ((0, 0),) * (array.ndim - 1) + ((0, half - half_own),), constant_values=-1)
        return array.reshape(array.shape[:-2] + (total,))

    names = spread(jnp.arange(n_comp * comps_local, dtype=jnp.float32)[None])
    index = spread(jnp.swapaxes(quad_index, 1, 2).astype(jnp.float32))
    weight = jnp.maximum(spread(jnp.swapaxes(quad_weight, 1, 2)), 0.0)
    strength = spread(coupling[None]).reshape(total, 1)
    by_cols = pl.BlockSpec((1, 4, total), lambda s, i: (s, 0, 0))
    by_block = pl.BlockSpec((1, block, total), lambda s, i: (s, i, 0))
    matrix = pl.pallas_call(
        functools.partial(matrix_kernel, home_of),
        grid=(2, n_comp),
        out_shape=pltpu.VMEM((2, total, total), jnp.bfloat16),
        in_specs=[scalars, whole, by_cols, by_cols, [anywhere] * 2],
        out_specs=by_block,
        scratch_shapes=[pltpu.VMEM((total, 8), jnp.float32)],
        compiler_params=params(),
        cost_estimate=cost(6),
    )(place, names, index, weight, [blocks[-1], strength])

    lat_in[0] = [on_all_columns(block) for block in gated(lat_in[0], [matrix])]
    lat_in[1:] = [[[block] for block in found] for found in lat_in[1:]]

    n_class = speed_table.shape[0]
    head_block = pl.BlockSpec((3 * rows, lanes), lambda i: (0, 0))
    faces, window_fields = pl.pallas_call(
        functools.partial(faces_kernel, window, n_lon),
        grid=(1,),
        out_shape=(
            jax.ShapeDtypeStruct((window.size, 2, 6 * n_class, width), jnp.bfloat16),
            jax.ShapeDtypeStruct((window.size, 3, width), jnp.float32),
        ),
        in_specs=[scalars, [whole] * n_lon, [[head_block] * n_lon] * len(moves), anywhere],
        out_specs=(whole, whole),
        compiler_params=params(),
        cost_estimate=cost(2),
    )(place, own_fields, lat_in[0], matrix)

    ids = comp * comps_local + lon * half_own + jnp.arange(half, dtype=jnp.int32)
    freq_hot = ((ids // NDIR)[:, None] == jnp.arange(speed_table.shape[1], dtype=jnp.int32)[None, :]).astype(
        jnp.float32
    )
    speed = jnp.dot(freq_hot, speed_table.T, precision=lax.Precision.HIGHEST)
    angles = 2.0 * math.pi / NDIR * (ids % NDIR).astype(jnp.float32)
    tables = []
    for which, turn in ((0, jnp.cos(angles)), (1, jnp.sin(angles))):
        currents = jnp.broadcast_to(current_table[:, which][None], (half, n_class))
        left = jnp.concatenate([speed * turn[:, None], currents], axis=1)
        levels = []
        for _ in range(3):
            level = lax.reduce_precision(left, 8, 7)
            levels.append(level)
            left = left - level
        tables.append(jnp.concatenate(levels, axis=1).astype(jnp.bfloat16))
    tables = jnp.stack(tables)

    if split:
        share, span = rows // n_comp, lanes
    else:
        groups = n_comp // rows
        share, span = 1, lanes // groups
    far_first = sorted(range(1, n_comp), key=lambda r: abs(2 * r - n_comp))
    order = [0] + far_first
    arrived = []
    for i, (start, size) in enumerate(zip(starts, sizes)):
        table = lax.slice_in_dim(tables, start, start + size, axis=1)
        if split:
            shapes = [jax.ShapeDtypeStruct((n_lon, share, size, lanes), jnp.float32)] * n_comp
        else:
            shapes = [jax.ShapeDtypeStruct((rows, n_lon, size, lanes), jnp.float32)]
        pieces = pl.pallas_call(
            functools.partial(
                propagate_kernel, window, n_lon, n_comp, split, start, half, 0 if i else 3
            ),
            out_shape=shapes,
            in_specs=[
                scalars,
                whole,
                whole,
                whole,
                [anywhere] * n_lon,
                [[whole] * len(found) for found in lat_in[i]],
                anywhere,
            ],
            out_specs=[whole] * len(shapes),
            scratch_shapes=propagate_scratch(window, size, lanes, n_lon),
            compiler_params=params(),
            cost_estimate=cost(1.5 + 0.11 * size),
        )(
            place,
            table,
            faces,
            window_fields,
            own_in,
            lat_in[i],
            matrix if i == 0 else pieces[0],
        )
        if split:
            sent = pieces[1:]
            if i > 0:
                sent = gated(sent, [moved[r] for r in far_first[:2]])
            moved = [pieces[0]] + [None] * (n_comp - 1)
            for r in far_first:
                pairs = [(a, (a + r) % n_comp) for a in range(n_comp)]
                moved[r] = lax.ppermute(sent[r - 1], "comp", pairs)
        else:
            energy = pieces[0].reshape(rows, n_lon, size, groups, span)
            energy = jnp.transpose(energy, (0, 3, 1, 2, 4)).reshape(n_comp, n_lon, 1, size, span)
            energy = lax.all_to_all(energy, "comp", split_axis=0, concat_axis=0, tiled=True)
            moved = [energy[s] for s in range(n_comp)]
        after = []
        if i == len(sizes) - 1:
            matrix_t = pl.pallas_call(
                functools.partial(transposed_kernel, home_of, half, half_own),
                grid=(2, n_comp),
                out_shape=pltpu.VMEM((2, total, total), jnp.bfloat16),
                in_specs=[scalars, by_cols, by_cols, anywhere],
                out_specs=by_block,
                compiler_params=params(),
                cost_estimate=cost(4),
            )(place, index, weight, pieces[0])
            after = [matrix_t]
        crossed = []
        for d in range(1, n_lon):
            pairs = [(b, (b + d) % n_lon) for b in range(n_lon)]
            packed = pl.pallas_call(
                functools.partial(cross_pack_kernel, d),
                out_shape=jax.ShapeDtypeStruct((n_comp, share, size, span), jnp.float32),
                in_specs=[[anywhere] * n_comp, [anywhere] * len(after)],
                out_specs=whole,
                scratch_shapes=[pltpu.SemaphoreType.DMA((n_comp,))],
                compiler_params=params(),
                cost_estimate=cost(1),
            )(moved, after)
            crossed.append(lax.ppermute(packed, "lon", pairs))
        arrived += moved + crossed

    cells = share * span
    energy, source, source_low = pl.pallas_call(
        functools.partial(forward_kernel, sizes, n_lon, home_of),
        out_shape=(
            jax.ShapeDtypeStruct((total, cells), jnp.float32),
            jax.ShapeDtypeStruct((total, cells), jnp.float32),
            jax.ShapeDtypeStruct((total, cells), jnp.bfloat16),
        ),
        in_specs=[scalars, whole, whole] + [whole] * len(arrived),
        out_specs=(whole, whole, whole),
        scratch_shapes=[pltpu.VMEM((total, cells), jnp.bfloat16)],
        compiler_params=params(),
        cost_estimate=cost(4),
    )(place, matrix, strength, *arrived)

    back = []
    for s in range(n_comp):
        back.append(
            pl.pallas_call(
                functools.partial(backward_kernel, s),
                out_shape=jax.ShapeDtypeStruct((share, block, span), jnp.float32),
                in_specs=[whole] * 4,
                out_specs=whole,
                compiler_params=params(),
                cost_estimate=cost(0.6),
            )(matrix_t, source_low, energy, source)
        )

    if split:
        home = [back[0]] + [None] * (n_comp - 1)
        for r in far_first:
            home[r] = lax.ppermute(back[r], "comp", [(a, (a - r) % n_comp) for a in range(n_comp)])
        if half == half_own:
            held = []
            for some in (order[:2], order[2:]):
                held = [
                    pl.pallas_call(
                        functools.partial(gather_kernel, rows, n_comp, some),
                        out_shape=jax.ShapeDtypeStruct((comps_local * rows, lanes), jnp.float32),
                        in_specs=[scalars, [whole] * len(held)] + [whole] * len(some),
                        out_specs=whole,
                        compiler_params=params(),
                        cost_estimate=cost(1),
                    )(place, held, *[home[r] for r in some])
                ]
            out = held[0]
            return out.reshape(comps_local, rows, lanes)
        home = jnp.stack(home).reshape(n_comp, share, n_lon, half, lanes)[:, :, :, :half_own]
        home = jnp.roll(home, comp, 0)
        return jnp.transpose(home, (2, 3, 0, 1, 4)).reshape(comps_local, rows, lanes)
    home = lax.all_to_all(jnp.concatenate(back), "comp", split_axis=0, concat_axis=0, tiled=True)
    home = home.reshape(rows, groups, n_lon, half, span)[:, :, :, :half_own]
    return jnp.transpose(home, (2, 3, 0, 1, 4)).reshape(comps_local, rows, lanes)


def solution(mesh):
    placed = (
        P(("ens", "comp"), "lat", "lon"),
        P("lat", "lon"),
        P("lat", "lon"),
        P("lat", "lon"),
        P(),
        P(),
        P(),
        P(),
        P(),
    )
    return jax.shard_map(
        local,
        mesh=mesh,
        in_specs=placed,
        out_specs=P(("ens", "comp"), "lat", "lon"),
        check_vma=False,
    )
```

```python
import functools
import math

import jax
import jax.numpy as jnp
from jax import lax
from jax.experimental import pallas as pl
from jax.experimental.pallas import tpu as pltpu
from jax.sharding import PartitionSpec as P

NDIR = 36
SUBSTEPS = 4
RIM = 2 * SUBSTEPS
GROUP = 16
CHUNKS = 3

plus_factor = 0.4096
minus_factor = 3.160494
cross_factor = 2.007843

VMEM_LIMIT = 16 * 1024 * 1024
whole = pl.BlockSpec(memory_space=pltpu.VMEM)
anywhere = pl.BlockSpec(memory_space=pl.ANY)
scalars = pl.BlockSpec(memory_space=pltpu.SMEM)


def params():
    return pltpu.CompilerParams(vmem_limit_bytes=VMEM_LIMIT)


def cost(micros):
    return pl.CostEstimate(flops=0, bytes_accessed=int(micros * 3.5e6), transcendentals=0)


def chunk_sizes(total):
    groups = total // GROUP
    count = min(CHUNKS, groups)
    return [GROUP * (groups // count + (i < groups % count)) for i in range(count)]


class Window:
    def __init__(self, n_lat, rows):
        self.pair = n_lat == 2
        self.rows = rows
        self.size = 2 * rows + 4 if self.pair else 3 * rows

    def own(self, lat):
        return jnp.where(lat == 0, 2, 2 + self.rows) if self.pair else self.rows

    def received(self, lat):
        if self.pair:
            return [jnp.where(lat == 0, 2 + self.rows, 2)]
        return [0, 2 * self.rows]

    def zeros(self, lat):
        if not self.pair:
            return []
        first = jnp.where(lat == 0, 0, 2 + 2 * self.rows)
        return [first, first + 1]

    def steps(self, lat, substep):
        shrink = 2 * (substep + 1)
        if self.pair:
            return jnp.where(lat == 0, 2, 2 + shrink), 2 * self.rows - shrink
        return shrink, 3 * self.rows - 2 * shrink


def faces_kernel(window, n_lon, place, own, received, after, out, fields):
    lat = place[0]
    rows, lanes = window.rows, own[0].shape[1]
    for row in window.zeros(lat):
        fields[row] = jnp.zeros((3, n_lon * lanes), jnp.float32)
    for offset, blocks in [(window.own(lat), own)] + list(zip(window.received(lat), received)):
        for d, ref in enumerate(blocks):
            for f in range(3):
                for row in range(rows):
                    at = f * rows + row
                    fields[offset + row, f : f + 1, d * lanes : (d + 1) * lanes] = ref[at : at + 1, :]
    width = n_lon * lanes
    n_class = out.shape[2] // 6
    classes = lax.broadcasted_iota(jnp.int32, (n_class, width), 0).astype(jnp.float32)

    def hots(row):
        wet = fields[row, 0:1, :]
        hot_depth = (classes == fields[row, 1:2, :]).astype(jnp.float32)
        hot_current = (classes == fields[row, 2:3, :]).astype(jnp.float32)
        return wet, jnp.concatenate([hot_depth, hot_current], axis=0)

    def step(row, _):
        wet, hot = hots(row)
        wet_next, hot_next = hots(row + 1)
        east_wet = 0.5 * wet * pltpu.roll(wet, width - 1, 1)
        east = ((hot + pltpu.roll(hot, width - 1, 1)) * east_wet).astype(jnp.bfloat16)
        north = ((hot + hot_next) * (0.5 * wet * wet_next)).astype(jnp.bfloat16)
        span = 2 * n_class
        for copy in range(3):
            out[row, 0, copy * span : (copy + 1) * span, :] = east
            out[row, 1, copy * span : (copy + 1) * span, :] = north
        return 0

    lax.fori_loop(0, window.size - 1, step, 0, unroll=True)
    out[window.size - 1] = jnp.zeros(out.shape[1:], jnp.bfloat16)


def pack_raw_kernel(half, rows, flat, sea, depth, current, out, fields_out, held, sems):
    fields = [sea, depth, current]
    lead = len(fields) * rows
    parts = flat.shape[0] // (half * rows)
    length = (out.shape[0] - lead) // parts
    copies = []
    for i in range(parts):
        to = out.at[pl.ds(lead + i * length, length)]
        copies.append(pltpu.make_async_copy(flat.at[pl.ds(i * half * rows, length)], to, sems.at[0, i]))
    for i, ref in enumerate(fields):
        copies.append(pltpu.make_async_copy(ref, held.at[i], sems.at[1, i]))
    for copy in copies:
        copy.start()
    for copy in copies:
        copy.wait()
    for i in range(len(fields)):
        at = slice(i * rows, (i + 1) * rows)
        out[at, :] = held[i].astype(jnp.float32)
        fields_out[at, :] = held[i].astype(jnp.float32)


def pack_kernel(starts, half, rows, place, own_in, after, *refs):
    outs, sems = refs[:-1], refs[-1]
    copies = []
    for i, (start, out) in enumerate(zip(starts, outs)):
        length = out.shape[0] // len(own_in)
        first = pl.multiple_of((place[2] * half + start) * rows, 8)
        for d, ref in enumerate(own_in):
            there = ref.at[pl.ds(first, length)]
            copies.append(pltpu.make_async_copy(there, out.at[pl.ds(d * length, length)], sems.at[i, d]))
    for copy in copies:
        copy.start()
    for copy in copies:
        copy.wait()


def cross_pack_kernel(d, pieces, after, out, sems):
    copies = []
    for s, ref in enumerate(pieces):
        copies.append(pltpu.make_async_copy(ref.at[d], out.at[s], sems.at[s]))
        copies[-1].start()
    for copy in copies:
        copy.wait()


def gate_kernel(*refs):
    pass


def gated(arrays, after):
    return pl.pallas_call(
        gate_kernel,
        out_shape=[jax.ShapeDtypeStruct(a.shape, a.dtype) for a in arrays],
        in_specs=[anywhere] * (len(arrays) + len(after)),
        out_specs=[anywhere] * len(arrays),
        input_output_aliases={i: i for i in range(len(arrays))},
        compiler_params=params(),
        cost_estimate=cost(0.1),
    )(*arrays, *after)


def median_zero(a, b):
    return jnp.maximum(jnp.minimum(a, b), jnp.minimum(jnp.maximum(a, b), 0.0))


def flux(u, c, low, high, slope_low, slope_high):
    rising = u > 0.0
    return u * jnp.where(rising, low, high) + c * jnp.where(rising, slope_low, slope_high)


def propagate_scratch(window, size, lanes, n_lon):
    width = n_lon * lanes
    energy = pltpu.VMEM((window.size, GROUP, width), jnp.float32)
    speed = pltpu.VMEM((window.size, size, width), jnp.float32)
    block = pltpu.VMEM((size * window.rows, lanes), jnp.float32)
    return [energy, energy, speed, speed, speed, speed] + [block] * n_lon + [pltpu.SemaphoreType.DMA((n_lon,))]


def propagate_kernel(
    window, n_lon, n_comp, split, start, half, head, place, tables, faces, wet, own_in, lat_in, after, *refs
):
    outs, scratch = refs[: -7 - n_lon], refs[-7 - n_lon :]
    energy, other, east_u, east_c, north_u, north_c = scratch[:6]
    own_blocks, sems = scratch[6:-1], scratch[-1]
    lat, comp, lon = place[0], place[1], place[2]
    rows, lanes = window.rows, wet.shape[2] // n_lon
    width = n_lon * lanes
    count = east_u.shape[1]
    copies = []
    for d in range(n_lon):
        first = pl.multiple_of((lon * half + start) * rows, 8)
        copies.append(pltpu.make_async_copy(own_in[d].at[pl.ds(first, count * rows)], own_blocks[d], sems.at[d]))
        copies[-1].start()

    def speeds(row, _):
        for which, u_ref, c_ref in ((0, east_u, east_c), (1, north_u, north_c)):
            u = jnp.dot(tables[which], faces[row, which], preferred_element_type=jnp.float32)
            size = jnp.abs(u)
            u_ref[row] = u
            c_ref[row] = 0.5 * size * (1.0 - size)
        return 0

    lax.fori_loop(0, window.size, speeds, 0, unroll=True)

    for copy in copies:
        copy.wait()
    own = window.own(lat)

    def group(g, _):
        first = pl.multiple_of(g * GROUP, GROUP)
        here = pl.ds(first, GROUP)
        for row in window.zeros(lat):
            energy[row] = jnp.zeros((GROUP, width), jnp.float32)
            other[row] = jnp.zeros((GROUP, width), jnp.float32)
        sources = [(own, [(ref, 0) for ref in own_blocks])]
        for offset, blocks in zip(window.received(lat), lat_in):
            if head:
                sources.append((offset, [(ref, head + lon * count) for ref in blocks]))
            else:
                sources.append((offset, [(blocks[0], d * count) for d in range(n_lon)]))
        for offset, blocks in sources:
            for d, (ref, lead) in enumerate(blocks):
                for row in range(rows):
                    at = pl.ds((lead + first) * rows + row, GROUP, stride=rows)
                    sea = wet[offset + row, 0:1, d * lanes : (d + 1) * lanes]
                    energy[offset + row, :, d * lanes : (d + 1) * lanes] = ref[at, :] * sea

        for substep in range(SUBSTEPS):
            base, length = window.steps(lat, substep)
            old, new = (energy, other) if substep % 2 == 0 else (other, energy)
            prior = [old[base + i] for i in (-2, -1, 0, 1)]
            gap = [b - a for a, b in zip(prior, prior[1:])]
            slope_prior, slope_here = median_zero(gap[1], gap[0]), median_zero(gap[2], gap[1])
            south = flux(
                north_u[base - 1, here], north_c[base - 1, here], prior[1], prior[2], slope_prior, slope_here
            )

            def row_step(i, carry):
                south, this, after, gap_after, slope_this = carry
                row = base + i
                beyond = old[row + 2]
                gap_beyond = beyond - after
                slope_after = median_zero(gap_beyond, gap_after)
                north = flux(north_u[row, here], north_c[row, here], this, after, slope_this, slope_after)
                east_cell = pltpu.roll(this, width - 1, 1)
                gap_east = east_cell - this
                gap_west = pltpu.roll(gap_east, 1, 1)
                slope = median_zero(gap_east, gap_west)
                slope_east = pltpu.roll(slope, width - 1, 1)
                east = flux(east_u[row, here], east_c[row, here], this, east_cell, slope, slope_east)
                west = pltpu.roll(east, 1, 1)
                new[row] = this - (east - west) - (north - south)
                return north, after, beyond, gap_beyond, slope_after

            lax.fori_loop(0, length, row_step, (south, prior[2], prior[3], gap[2], slope_here), unroll=True)

        if split:
            share = rows // n_comp
            for r in range(n_comp):
                base = own + lax.rem(comp + r, n_comp) * share
                for d in range(n_lon):
                    for k in range(share):
                        outs[r][d, k, here, :] = energy[base + k, :, d * lanes : (d + 1) * lanes]
        else:
            for row in range(rows):
                for d in range(n_lon):
                    outs[0][row, d, here, :] = energy[own + row, :, d * lanes : (d + 1) * lanes]
        return 0

    lax.fori_loop(0, count // GROUP, group, 0)


def matrix_kernel(home, place, names, index, weight, after, out, columns):
    height = out.shape[1]

    @pl.when(pl.program_id(1) == 0)
    def _():
        columns[...] = jnp.transpose(jnp.concatenate([index[0], weight[0]], axis=0))

    base = pl.multiple_of(home(place, pl.program_id(1)) * height, GROUP)

    def step(i, _):
        at = pl.multiple_of(i * GROUP, GROUP)
        column = columns[pl.ds(base + at, GROUP), :]
        name = names[...]
        made = jnp.zeros((GROUP, name.shape[1]), jnp.float32)
        for corner in range(4):
            made = jnp.where(name == column[:, corner : corner + 1], column[:, corner + 4 : corner + 5], made)
        out[0, pl.ds(at, GROUP), :] = made.astype(jnp.bfloat16)
        return 0

    lax.fori_loop(0, height // GROUP, step, 0, unroll=True)


def transposed_kernel(home, half, half_own, place, index, weight, after, out):
    height, total = out.shape[1], out.shape[2]
    base = home(place, pl.program_id(1)) * height

    def step(i, _):
        at = pl.multiple_of(i * GROUP, GROUP)
        row = base + at + lax.broadcasted_iota(jnp.int32, (GROUP, 128), 0)
        if half != half_own:
            row = jnp.where(row % half < half_own, row // half * half_own + row % half, -1)
        row = jnp.concatenate([row.astype(jnp.float32)] * (-(-total // 128)), axis=1)[:, :total]
        made = jnp.zeros((GROUP, total), jnp.float32)
        for corner in range(4):
            made = jnp.where(row == index[0, corner : corner + 1, :], weight[0, corner : corner + 1, :], made)
        out[0, pl.ds(at, GROUP), :] = made.astype(jnp.bfloat16)
        return 0

    lax.fori_loop(0, height // GROUP, step, 0, unroll=3)


def forward_kernel(sizes, n_lon, home, place, matrix, coupling, *refs):
    pieces = refs[:-4]
    energy_out, source_out, source_low_out, low = refs[-4:]
    per_chunk = len(pieces) // len(sizes)
    n_comp = per_chunk - n_lon + 1
    block = coupling.shape[0] // n_comp
    half = block // n_lon
    share, lanes = pieces[0].shape[1], pieces[0].shape[3]
    for s in range(n_comp):
        for d in range(n_lon):
            first = lax.rem(place[2] + n_lon - d, n_lon) * half
            for i, size in enumerate(sizes):
                group = pieces[i * per_chunk : (i + 1) * per_chunk]
                to = first + sum(sizes[:i])
                here = pl.ds(pl.multiple_of(s * block + to, GROUP), size)
                there = pl.ds(pl.multiple_of(home(place, s) * block + to, GROUP), size)
                for k in range(share):
                    part = group[s][0, k] if d == 0 else group[d - n_lon][s, k]
                    energy_out[here, k * lanes : (k + 1) * lanes] = part
                    low[there, k * lanes : (k + 1) * lanes] = part.astype(jnp.bfloat16)
    for s in range(n_comp):
        here = slice(s * block, (s + 1) * block)
        there = pl.ds(pl.multiple_of(home(place, s) * block, GROUP), block)
        energy = energy_out[here, :]
        plus_side = jnp.dot(matrix[0, here, :], low[...], preferred_element_type=jnp.float32)
        minus_side = jnp.dot(matrix[1, here, :], low[...], preferred_element_type=jnp.float32)
        source = coupling[there, :] * (
            energy * energy * (plus_factor * plus_side + minus_factor * minus_side)
            - cross_factor * energy * plus_side * minus_side
        )
        source_out[here, :] = source
        source_low_out[there, :] = source.astype(jnp.bfloat16)


def backward_kernel(s, matrix_t, source_low, energy, source, out):
    block, lanes = out.shape[1], out.shape[2]
    here = slice(s * block, (s + 1) * block)
    gain = (
        jnp.dot(matrix_t[0, here, :], source_low[...], preferred_element_type=jnp.float32)
        + jnp.dot(matrix_t[1, here, :], source_low[...], preferred_element_type=jnp.float32)
        - 2.0 * source[here, :]
    )
    result = energy[here, :] + gain / (1.0 + jnp.abs(gain))
    for k in range(out.shape[0]):
        out[k] = result[:, k * lanes : (k + 1) * lanes]


def gather_kernel(rows, n_comp, order, place, held, *refs):
    pieces, out = refs[:-1], refs[-1]
    share = rows // n_comp
    for ref in held:
        out[...] = ref[...]
    for r, piece in zip(order, pieces):
        for k in range(share):
            row = lax.rem(place[1] + r, n_comp) * share + k
            for i in range(0, piece.shape[1], GROUP):
                out[pl.ds(i * rows + row, GROUP, stride=rows), :] = piece[k, i : i + GROUP, :]


def local(
    spectrum,
    sea_mask,
    depth_class,
    current_class,
    speed_table,
    current_table,
    coupling,
    quad_index,
    quad_weight,
):
    comps_local, rows, lanes = spectrum.shape
    n_comp, n_lat, n_lon = (lax.axis_size(a) for a in ("comp", "lat", "lon"))
    comp, lat, lon = (lax.axis_index(a) for a in ("comp", "lat", "lon"))
    place = jnp.stack([lat, comp, lon]).astype(jnp.int32)
    half_own = comps_local // n_lon
    half = -(-half_own // GROUP) * GROUP
    sizes = chunk_sizes(half)
    starts = [sum(sizes[:i]) for i in range(len(sizes))]
    window = Window(n_lat, rows)
    width = n_lon * lanes
    split = rows % n_comp == 0

    if half == half_own:
        flat = spectrum.reshape(comps_local * rows, lanes)
    else:
        flat = spectrum.reshape(n_lon, half_own, rows, lanes)
        flat = jnp.pad(flat, ((0, 0), (0, half - half_own), (0, 0), (0, 0))).reshape(-1, lanes)
    if window.pair:
        moves = [[(0, 1), (1, 0)]]
    else:
        moves = [[(i, i + 1) for i in range(n_lat - 1)], [(i + 1, i) for i in range(n_lat - 1)]]
    lengths = [n_lon * size * rows for size in sizes]


    def on_all_columns(block):
        found = [block]
        for d in range(n_lon - 1, 0, -1):
            found.append(lax.ppermute(block, "lon", [(i, (i + d) % n_lon) for i in range(n_lon)]))
        return found

    first_block, fields = pl.pallas_call(
        functools.partial(pack_raw_kernel, half, rows),
        out_shape=(
            jax.ShapeDtypeStruct((lengths[0] + 3 * rows, lanes), jnp.float32),
            jax.ShapeDtypeStruct((3 * rows, lanes), jnp.float32),
        ),
        in_specs=[anywhere] * 4,
        out_specs=(whole, whole),
        scratch_shapes=[pltpu.VMEM((3, rows, lanes), jnp.int32), pltpu.SemaphoreType.DMA((2, max(n_lon, 3)))],
        compiler_params=params(),
        cost_estimate=cost(1),
    )(*[pltpu.with_memory_space_constraint(a, pltpu.HBM) for a in (flat, sea_mask, depth_class, current_class)])
    own_in, own_fields = on_all_columns(flat), on_all_columns(fields)
    blocks = [first_block]
    if len(sizes) > 1:
        blocks += pl.pallas_call(
            functools.partial(pack_kernel, starts[1:], half, rows),
            out_shape=[jax.ShapeDtypeStruct((length, lanes), jnp.float32) for length in lengths[1:]],
            in_specs=[scalars, [anywhere] * n_lon, [anywhere] * (n_lon + 1)],
            out_specs=[whole] * len(lengths[1:]),
            scratch_shapes=[pltpu.SemaphoreType.DMA((len(lengths) - 1, n_lon))],
            compiler_params=params(),
            cost_estimate=cost(1.5),
        )(place, own_in, [first_block] + own_fields)
    lat_in = [[lax.ppermute(block, "lat", move) for move in moves] for block in blocks]

    def home_of(place, s):
        return lax.rem(place[1] + n_comp - s, n_comp) if split else s

    total = n_comp * n_lon * half
    block = n_lon * half

    def spread(array):
        if half == half_own:
            return array
        array = array.reshape(array.shape[:-1] + (n_comp * n_lon, half_own))
        array = jnp.pad(array, ((0, 0),) * (array.ndim - 1) + ((0, half - half_own),), constant_values=-1)
        return array.reshape(array.shape[:-2] + (total,))

    names = spread(jnp.arange(n_comp * comps_local, dtype=jnp.float32)[None])
    index = spread(jnp.swapaxes(quad_index, 1, 2).astype(jnp.float32))
    weight = jnp.maximum(spread(jnp.swapaxes(quad_weight, 1, 2)), 0.0)
    strength = spread(coupling[None]).reshape(total, 1)
    by_cols = pl.BlockSpec((1, 4, total), lambda s, i: (s, 0, 0))
    by_block = pl.BlockSpec((1, block, total), lambda s, i: (s, i, 0))
    matrix = pl.pallas_call(
        functools.partial(matrix_kernel, home_of),
        grid=(2, n_comp),
        out_shape=pltpu.VMEM((2, total, total), jnp.bfloat16),
        in_specs=[scalars, whole, by_cols, by_cols, [anywhere] * 2],
        out_specs=by_block,
        scratch_shapes=[pltpu.VMEM((total, 8), jnp.float32)],
        compiler_params=params(),
        cost_estimate=cost(6),
    )(place, names, index, weight, [blocks[-1], strength])

    lat_in[0] = [on_all_columns(block) for block in gated(lat_in[0], [matrix])]
    lat_in[1:] = [[[block] for block in found] for found in lat_in[1:]]

    n_class = speed_table.shape[0]
    head_block = pl.BlockSpec((3 * rows, lanes), lambda i: (0, 0))
    faces, window_fields = pl.pallas_call(
        functools.partial(faces_kernel, window, n_lon),
        grid=(1,),
        out_shape=(
            jax.ShapeDtypeStruct((window.size, 2, 6 * n_class, width), jnp.bfloat16),
            jax.ShapeDtypeStruct((window.size, 3, width), jnp.float32),
        ),
        in_specs=[scalars, [whole] * n_lon, [[head_block] * n_lon] * len(moves), anywhere],
        out_specs=(whole, whole),
        compiler_params=params(),
        cost_estimate=cost(2),
    )(place, own_fields, lat_in[0], matrix)

    ids = comp * comps_local + lon * half_own + jnp.arange(half, dtype=jnp.int32)
    freq_hot = ((ids // NDIR)[:, None] == jnp.arange(speed_table.shape[1], dtype=jnp.int32)[None, :]).astype(
        jnp.float32
    )
    speed = jnp.dot(freq_hot, speed_table.T, precision=lax.Precision.HIGHEST)
    angles = 2.0 * math.pi / NDIR * (ids % NDIR).astype(jnp.float32)
    tables = []
    for which, turn in ((0, jnp.cos(angles)), (1, jnp.sin(angles))):
        currents = jnp.broadcast_to(current_table[:, which][None], (half, n_class))
        left = jnp.concatenate([speed * turn[:, None], currents], axis=1)
        levels = []
        for _ in range(3):
            level = lax.reduce_precision(left, 8, 7)
            levels.append(level)
            left = left - level
        tables.append(jnp.concatenate(levels, axis=1).astype(jnp.bfloat16))
    tables = jnp.stack(tables)

    if split:
        share, span = rows // n_comp, lanes
    else:
        groups = n_comp // rows
        share, span = 1, lanes // groups
    far_first = sorted(range(1, n_comp), key=lambda r: abs(2 * r - n_comp))
    order = [0] + far_first
    arrived = []
    for i, (start, size) in enumerate(zip(starts, sizes)):
        table = lax.slice_in_dim(tables, start, start + size, axis=1)
        if split:
            shapes = [jax.ShapeDtypeStruct((n_lon, share, size, lanes), jnp.float32)] * n_comp
        else:
            shapes = [jax.ShapeDtypeStruct((rows, n_lon, size, lanes), jnp.float32)]
        pieces = pl.pallas_call(
            functools.partial(
                propagate_kernel, window, n_lon, n_comp, split, start, half, 0 if i else 3
            ),
            out_shape=shapes,
            in_specs=[
                scalars,
                whole,
                whole,
                whole,
                [anywhere] * n_lon,
                [[whole] * len(found) for found in lat_in[i]],
                anywhere,
            ],
            out_specs=[whole] * len(shapes),
            scratch_shapes=propagate_scratch(window, size, lanes, n_lon),
            compiler_params=params(),
            cost_estimate=cost(1.5 + 0.11 * size),
        )(
            place,
            table,
            faces,
            window_fields,
            own_in,
            lat_in[i],
            matrix if i == 0 else pieces[0],
        )
        if split:
            sent = pieces[1:]
            if i > 0:
                sent = gated(sent, [moved[r] for r in far_first[:2]])
            moved = [pieces[0]] + [None] * (n_comp - 1)
            for r in far_first:
                pairs = [(a, (a + r) % n_comp) for a in range(n_comp)]
                moved[r] = lax.ppermute(sent[r - 1], "comp", pairs)
        else:
            energy = pieces[0].reshape(rows, n_lon, size, groups, span)
            energy = jnp.transpose(energy, (0, 3, 1, 2, 4)).reshape(n_comp, n_lon, 1, size, span)
            energy = lax.all_to_all(energy, "comp", split_axis=0, concat_axis=0, tiled=True)
            moved = [energy[s] for s in range(n_comp)]
        after = []
        if i == len(sizes) - 1:
            matrix_t = pl.pallas_call(
                functools.partial(transposed_kernel, home_of, half, half_own),
                grid=(2, n_comp),
                out_shape=pltpu.VMEM((2, total, total), jnp.bfloat16),
                in_specs=[scalars, by_cols, by_cols, anywhere],
                out_specs=by_block,
                compiler_params=params(),
                cost_estimate=cost(4),
            )(place, index, weight, pieces[0])
            after = [matrix_t]
        crossed = []
        for d in range(1, n_lon):
            pairs = [(b, (b + d) % n_lon) for b in range(n_lon)]
            packed = pl.pallas_call(
                functools.partial(cross_pack_kernel, d),
                out_shape=jax.ShapeDtypeStruct((n_comp, share, size, span), jnp.float32),
                in_specs=[[anywhere] * n_comp, [anywhere] * len(after)],
                out_specs=whole,
                scratch_shapes=[pltpu.SemaphoreType.DMA((n_comp,))],
                compiler_params=params(),
                cost_estimate=cost(1),
            )(moved, after)
            crossed.append(lax.ppermute(packed, "lon", pairs))
        arrived += moved + crossed

    cells = share * span
    energy, source, source_low = pl.pallas_call(
        functools.partial(forward_kernel, sizes, n_lon, home_of),
        out_shape=(
            jax.ShapeDtypeStruct((total, cells), jnp.float32),
            jax.ShapeDtypeStruct((total, cells), jnp.float32),
            jax.ShapeDtypeStruct((total, cells), jnp.bfloat16),
        ),
        in_specs=[scalars, whole, whole] + [whole] * len(arrived),
        out_specs=(whole, whole, whole),
        scratch_shapes=[pltpu.VMEM((total, cells), jnp.bfloat16)],
        compiler_params=params(),
        cost_estimate=cost(4),
    )(place, matrix, strength, *arrived)

    back = []
    for s in range(n_comp):
        back.append(
            pl.pallas_call(
                functools.partial(backward_kernel, s),
                out_shape=jax.ShapeDtypeStruct((share, block, span), jnp.float32),
                in_specs=[whole] * 4,
                out_specs=whole,
                compiler_params=params(),
                cost_estimate=cost(0.6),
            )(matrix_t, source_low, energy, source)
        )

    if split:
        home = [back[0]] + [None] * (n_comp - 1)
        for r in far_first:
            home[r] = lax.ppermute(back[r], "comp", [(a, (a - r) % n_comp) for a in range(n_comp)])
        if half == half_own:
            held = []
            for some in (order[:2], order[2:]):
                held = [
                    pl.pallas_call(
                        functools.partial(gather_kernel, rows, n_comp, some),
                        out_shape=jax.ShapeDtypeStruct((comps_local * rows, lanes), jnp.float32),
                        in_specs=[scalars, [whole] * len(held)] + [whole] * len(some),
                        out_specs=whole,
                        compiler_params=params(),
                        cost_estimate=cost(1),
                    )(place, held, *[home[r] for r in some])
                ]
            out = held[0]
            return out.reshape(comps_local, rows, lanes)
        home = jnp.stack(home).reshape(n_comp, share, n_lon, half, lanes)[:, :, :, :half_own]
        home = jnp.roll(home, comp, 0)
        return jnp.transpose(home, (2, 3, 0, 1, 4)).reshape(comps_local, rows, lanes)
    home = lax.all_to_all(jnp.concatenate(back), "comp", split_axis=0, concat_axis=0, tiled=True)
    home = home.reshape(rows, groups, n_lon, half, span)[:, :, :, :half_own]
    return jnp.transpose(home, (2, 3, 0, 1, 4)).reshape(comps_local, rows, lanes)


def solution(mesh):
    placed = (
        P(("ens", "comp"), "lat", "lon"),
        P("lat", "lon"),
        P("lat", "lon"),
        P("lat", "lon"),
        P(),
        P(),
        P(),
        P(),
        P(),
    )
    return jax.shard_map(
        local,
        mesh=mesh,
        in_specs=placed,
        out_specs=P(("ens", "comp"), "lat", "lon"),
        check_vma=False,
    )
```

```python
import functools
import math

import jax
import jax.numpy as jnp
from jax import lax
from jax.experimental import pallas as pl
from jax.experimental.pallas import tpu as pltpu
from jax.sharding import PartitionSpec as P

NDIR = 36
SUBSTEPS = 4
RIM = 2 * SUBSTEPS
GROUP = 16
CHUNKS = 3

plus_factor = 0.4096
minus_factor = 3.160494
cross_factor = 2.007843

VMEM_LIMIT = 16 * 1024 * 1024
whole = pl.BlockSpec(memory_space=pltpu.VMEM)
anywhere = pl.BlockSpec(memory_space=pl.ANY)
scalars = pl.BlockSpec(memory_space=pltpu.SMEM)


def params():
    return pltpu.CompilerParams(vmem_limit_bytes=VMEM_LIMIT)


def cost(micros):
    return pl.CostEstimate(flops=0, bytes_accessed=int(micros * 3.5e6), transcendentals=0)


def chunk_sizes(total):
    groups = total // GROUP
    count = min(CHUNKS, groups)
    return [GROUP * (groups // count + (i < groups % count)) for i in range(count)]


class Window:
    def __init__(self, n_lat, rows):
        self.pair = n_lat == 2
        self.rows = rows
        self.size = 2 * rows + 4 if self.pair else 3 * rows

    def own(self, lat):
        return jnp.where(lat == 0, 2, 2 + self.rows) if self.pair else self.rows

    def received(self, lat):
        if self.pair:
            return [jnp.where(lat == 0, 2 + self.rows, 2)]
        return [0, 2 * self.rows]

    def zeros(self, lat):
        if not self.pair:
            return []
        first = jnp.where(lat == 0, 0, 2 + 2 * self.rows)
        return [first, first + 1]

    def steps(self, lat, substep):
        shrink = 2 * (substep + 1)
        if self.pair:
            return jnp.where(lat == 0, 2, 2 + shrink), 2 * self.rows - shrink
        return shrink, 3 * self.rows - 2 * shrink


def faces_kernel(window, n_lon, place, own, received, after, out, fields):
    lat = place[0]
    rows, lanes = window.rows, own[0].shape[1]
    for row in window.zeros(lat):
        fields[row] = jnp.zeros((3, n_lon * lanes), jnp.float32)
    for offset, blocks in [(window.own(lat), own)] + list(zip(window.received(lat), received)):
        for d, ref in enumerate(blocks):
            for f in range(3):
                for row in range(rows):
                    at = f * rows + row
                    fields[offset + row, f : f + 1, d * lanes : (d + 1) * lanes] = ref[at : at + 1, :]
    width = n_lon * lanes
    n_class = out.shape[2] // 6
    classes = lax.broadcasted_iota(jnp.int32, (n_class, width), 0).astype(jnp.float32)

    def hots(row):
        wet = fields[row, 0:1, :]
        hot_depth = (classes == fields[row, 1:2, :]).astype(jnp.float32)
        hot_current = (classes == fields[row, 2:3, :]).astype(jnp.float32)
        return wet, jnp.concatenate([hot_depth, hot_current], axis=0)

    def step(row, _):
        wet, hot = hots(row)
        wet_next, hot_next = hots(row + 1)
        east_wet = 0.5 * wet * pltpu.roll(wet, width - 1, 1)
        east = ((hot + pltpu.roll(hot, width - 1, 1)) * east_wet).astype(jnp.bfloat16)
        north = ((hot + hot_next) * (0.5 * wet * wet_next)).astype(jnp.bfloat16)
        span = 2 * n_class
        for copy in range(3):
            out[row, 0, copy * span : (copy + 1) * span, :] = east
            out[row, 1, copy * span : (copy + 1) * span, :] = north
        return 0

    lax.fori_loop(0, window.size - 1, step, 0, unroll=True)
    out[window.size - 1] = jnp.zeros(out.shape[1:], jnp.bfloat16)


def pack_raw_kernel(half, rows, flat, sea, depth, current, out, fields_out, held, sems):
    fields = [sea, depth, current]
    lead = len(fields) * rows
    parts = flat.shape[0] // (half * rows)
    length = (out.shape[0] - lead) // parts
    copies = []
    for i in range(parts):
        to = out.at[pl.ds(lead + i * length, length)]
        copies.append(pltpu.make_async_copy(flat.at[pl.ds(i * half * rows, length)], to, sems.at[0, i]))
    for i, ref in enumerate(fields):
        copies.append(pltpu.make_async_copy(ref, held.at[i], sems.at[1, i]))
    for copy in copies:
        copy.start()
    for copy in copies:
        copy.wait()
    for i in range(len(fields)):
        at = slice(i * rows, (i + 1) * rows)
        out[at, :] = held[i].astype(jnp.float32)
        fields_out[at, :] = held[i].astype(jnp.float32)


def pack_kernel(starts, half, rows, place, own_in, after, *refs):
    outs, sems = refs[:-1], refs[-1]
    copies = []
    for i, (start, out) in enumerate(zip(starts, outs)):
        length = out.shape[0] // len(own_in)
        first = pl.multiple_of((place[2] * half + start) * rows, 8)
        for d, ref in enumerate(own_in):
            there = ref.at[pl.ds(first, length)]
            copies.append(pltpu.make_async_copy(there, out.at[pl.ds(d * length, length)], sems.at[i, d]))
    for copy in copies:
        copy.start()
    for copy in copies:
        copy.wait()


def cross_pack_kernel(d, pieces, after, out, sems):
    copies = []
    for s, ref in enumerate(pieces):
        copies.append(pltpu.make_async_copy(ref.at[d], out.at[s], sems.at[s]))
        copies[-1].start()
    for copy in copies:
        copy.wait()


def gate_kernel(*refs):
    pass


def gated(arrays, after):
    return pl.pallas_call(
        gate_kernel,
        out_shape=[jax.ShapeDtypeStruct(a.shape, a.dtype) for a in arrays],
        in_specs=[anywhere] * (len(arrays) + len(after)),
        out_specs=[anywhere] * len(arrays),
        input_output_aliases={i: i for i in range(len(arrays))},
        compiler_params=params(),
        cost_estimate=cost(0.1),
    )(*arrays, *after)


def median_zero(a, b):
    return jnp.maximum(jnp.minimum(a, b), jnp.minimum(jnp.maximum(a, b), 0.0))


def flux(u, c, low, high, slope_low, slope_high):
    rising = u > 0.0
    return u * jnp.where(rising, low, high) + c * jnp.where(rising, slope_low, slope_high)


def propagate_scratch(window, size, lanes, n_lon):
    width = n_lon * lanes
    energy = pltpu.VMEM((window.size, GROUP, width), jnp.float32)
    speed = pltpu.VMEM((window.size, size, width), jnp.float32)
    return [energy, energy, speed, speed, speed, speed]


def propagate_kernel(
    window, n_lon, n_comp, split, start, half, head, place, tables, faces, wet, own_in, lat_in, after, *refs
):
    outs = refs[:-6]
    energy, other, east_u, east_c, north_u, north_c = refs[-6:]
    lat, comp, lon = place[0], place[1], place[2]
    rows, lanes = window.rows, wet.shape[2] // n_lon
    width = n_lon * lanes
    count = east_u.shape[1]
    def speeds(row, _):
        for which, u_ref, c_ref in ((0, east_u, east_c), (1, north_u, north_c)):
            u = jnp.dot(tables[which], faces[row, which], preferred_element_type=jnp.float32)
            size = jnp.abs(u)
            u_ref[row] = u
            c_ref[row] = 0.5 * size * (1.0 - size)
        return 0

    lax.fori_loop(0, window.size, speeds, 0, unroll=True)

    own = window.own(lat)

    def group(g, _):
        first = pl.multiple_of(g * GROUP, GROUP)
        here = pl.ds(first, GROUP)
        for row in window.zeros(lat):
            energy[row] = jnp.zeros((GROUP, width), jnp.float32)
            other[row] = jnp.zeros((GROUP, width), jnp.float32)
        sources = [(own, [(ref, lon * half + start) for ref in own_in])]
        for offset, blocks in zip(window.received(lat), lat_in):
            if head:
                sources.append((offset, [(ref, head + lon * count) for ref in blocks]))
            else:
                sources.append((offset, [(blocks[0], d * count) for d in range(n_lon)]))
        for offset, blocks in sources:
            for d, (ref, lead) in enumerate(blocks):
                for row in range(rows):
                    at = pl.ds((lead + first) * rows + row, GROUP, stride=rows)
                    sea = wet[offset + row, 0:1, d * lanes : (d + 1) * lanes]
                    energy[offset + row, :, d * lanes : (d + 1) * lanes] = ref[at, :] * sea

        for substep in range(SUBSTEPS):
            base, length = window.steps(lat, substep)
            old, new = (energy, other) if substep % 2 == 0 else (other, energy)
            prior = [old[base + i] for i in (-2, -1, 0, 1)]
            gap = [b - a for a, b in zip(prior, prior[1:])]
            slope_prior, slope_here = median_zero(gap[1], gap[0]), median_zero(gap[2], gap[1])
            south = flux(
                north_u[base - 1, here], north_c[base - 1, here], prior[1], prior[2], slope_prior, slope_here
            )

            def row_step(i, carry):
                south, this, after, gap_after, slope_this = carry
                row = base + i
                beyond = old[row + 2]
                gap_beyond = beyond - after
                slope_after = median_zero(gap_beyond, gap_after)
                north = flux(north_u[row, here], north_c[row, here], this, after, slope_this, slope_after)
                east_cell = pltpu.roll(this, width - 1, 1)
                gap_east = east_cell - this
                gap_west = pltpu.roll(gap_east, 1, 1)
                slope = median_zero(gap_east, gap_west)
                slope_east = pltpu.roll(slope, width - 1, 1)
                east = flux(east_u[row, here], east_c[row, here], this, east_cell, slope, slope_east)
                west = pltpu.roll(east, 1, 1)
                new[row] = this - (east - west) - (north - south)
                return north, after, beyond, gap_beyond, slope_after

            lax.fori_loop(0, length, row_step, (south, prior[2], prior[3], gap[2], slope_here), unroll=True)

        if split:
            share = rows // n_comp
            for r in range(n_comp):
                base = own + lax.rem(comp + r, n_comp) * share
                for d in range(n_lon):
                    for k in range(share):
                        outs[r][d, k, here, :] = energy[base + k, :, d * lanes : (d + 1) * lanes]
        else:
            for row in range(rows):
                for d in range(n_lon):
                    outs[0][row, d, here, :] = energy[own + row, :, d * lanes : (d + 1) * lanes]
        return 0

    lax.fori_loop(0, count // GROUP, group, 0)


def matrix_kernel(home, place, names, index, weight, after, out, columns):
    height = out.shape[1]

    @pl.when(pl.program_id(1) == 0)
    def _():
        columns[...] = jnp.transpose(jnp.concatenate([index[0], weight[0]], axis=0))

    base = pl.multiple_of(home(place, pl.program_id(1)) * height, GROUP)

    def step(i, _):
        at = pl.multiple_of(i * GROUP, GROUP)
        column = columns[pl.ds(base + at, GROUP), :]
        name = names[...]
        made = jnp.zeros((GROUP, name.shape[1]), jnp.float32)
        for corner in range(4):
            made = jnp.where(name == column[:, corner : corner + 1], column[:, corner + 4 : corner + 5], made)
        out[0, pl.ds(at, GROUP), :] = made.astype(jnp.bfloat16)
        return 0

    lax.fori_loop(0, height // GROUP, step, 0, unroll=True)


def transposed_kernel(home, half, half_own, place, index, weight, after, out):
    height, total = out.shape[1], out.shape[2]
    base = home(place, pl.program_id(1)) * height

    def step(i, _):
        at = pl.multiple_of(i * GROUP, GROUP)
        row = base + at + lax.broadcasted_iota(jnp.int32, (GROUP, 128), 0)
        if half != half_own:
            row = jnp.where(row % half < half_own, row // half * half_own + row % half, -1)
        row = jnp.concatenate([row.astype(jnp.float32)] * (-(-total // 128)), axis=1)[:, :total]
        made = jnp.zeros((GROUP, total), jnp.float32)
        for corner in range(4):
            made = jnp.where(row == index[0, corner : corner + 1, :], weight[0, corner : corner + 1, :], made)
        out[0, pl.ds(at, GROUP), :] = made.astype(jnp.bfloat16)
        return 0

    lax.fori_loop(0, height // GROUP, step, 0, unroll=3)


def forward_kernel(sizes, n_lon, home, place, matrix, coupling, *refs):
    pieces = refs[:-4]
    energy_out, source_out, source_low_out, low = refs[-4:]
    per_chunk = len(pieces) // len(sizes)
    n_comp = per_chunk - n_lon + 1
    block = coupling.shape[0] // n_comp
    half = block // n_lon
    share, lanes = pieces[0].shape[1], pieces[0].shape[3]
    for s in range(n_comp):
        for d in range(n_lon):
            first = lax.rem(place[2] + n_lon - d, n_lon) * half
            for i, size in enumerate(sizes):
                group = pieces[i * per_chunk : (i + 1) * per_chunk]
                to = first + sum(sizes[:i])
                here = pl.ds(pl.multiple_of(s * block + to, GROUP), size)
                there = pl.ds(pl.multiple_of(home(place, s) * block + to, GROUP), size)
                for k in range(share):
                    part = group[s][0, k] if d == 0 else group[d - n_lon][s, k]
                    energy_out[here, k * lanes : (k + 1) * lanes] = part
                    low[there, k * lanes : (k + 1) * lanes] = part.astype(jnp.bfloat16)
    for s in range(n_comp):
        here = slice(s * block, (s + 1) * block)
        there = pl.ds(pl.multiple_of(home(place, s) * block, GROUP), block)
        energy = energy_out[here, :]
        plus_side = jnp.dot(matrix[0, here, :], low[...], preferred_element_type=jnp.float32)
        minus_side = jnp.dot(matrix[1, here, :], low[...], preferred_element_type=jnp.float32)
        source = coupling[there, :] * (
            energy * energy * (plus_factor * plus_side + minus_factor * minus_side)
            - cross_factor * energy * plus_side * minus_side
        )
        source_out[here, :] = source
        source_low_out[there, :] = source.astype(jnp.bfloat16)


def backward_kernel(s, matrix_t, source_low, energy, source, out):
    block, lanes = out.shape[1], out.shape[2]
    here = slice(s * block, (s + 1) * block)
    gain = (
        jnp.dot(matrix_t[0, here, :], source_low[...], preferred_element_type=jnp.float32)
        + jnp.dot(matrix_t[1, here, :], source_low[...], preferred_element_type=jnp.float32)
        - 2.0 * source[here, :]
    )
    result = energy[here, :] + gain / (1.0 + jnp.abs(gain))
    for k in range(out.shape[0]):
        out[k] = result[:, k * lanes : (k + 1) * lanes]


def gather_kernel(rows, n_comp, order, place, held, *refs):
    pieces, out = refs[:-1], refs[-1]
    share = rows // n_comp
    for ref in held:
        out[...] = ref[...]
    for r, piece in zip(order, pieces):
        for k in range(share):
            row = lax.rem(place[1] + r, n_comp) * share + k
            for i in range(0, piece.shape[1], GROUP):
                out[pl.ds(i * rows + row, GROUP, stride=rows), :] = piece[k, i : i + GROUP, :]


def local(
    spectrum,
    sea_mask,
    depth_class,
    current_class,
    speed_table,
    current_table,
    coupling,
    quad_index,
    quad_weight,
):
    comps_local, rows, lanes = spectrum.shape
    n_comp, n_lat, n_lon = (lax.axis_size(a) for a in ("comp", "lat", "lon"))
    comp, lat, lon = (lax.axis_index(a) for a in ("comp", "lat", "lon"))
    place = jnp.stack([lat, comp, lon]).astype(jnp.int32)
    half_own = comps_local // n_lon
    half = -(-half_own // GROUP) * GROUP
    sizes = chunk_sizes(half)
    starts = [sum(sizes[:i]) for i in range(len(sizes))]
    window = Window(n_lat, rows)
    width = n_lon * lanes
    split = rows % n_comp == 0

    if half == half_own:
        flat = spectrum.reshape(comps_local * rows, lanes)
    else:
        flat = spectrum.reshape(n_lon, half_own, rows, lanes)
        flat = jnp.pad(flat, ((0, 0), (0, half - half_own), (0, 0), (0, 0))).reshape(-1, lanes)
    if window.pair:
        moves = [[(0, 1), (1, 0)]]
    else:
        moves = [[(i, i + 1) for i in range(n_lat - 1)], [(i + 1, i) for i in range(n_lat - 1)]]
    lengths = [n_lon * size * rows for size in sizes]


    def on_all_columns(block):
        found = [block]
        for d in range(n_lon - 1, 0, -1):
            found.append(lax.ppermute(block, "lon", [(i, (i + d) % n_lon) for i in range(n_lon)]))
        return found

    first_block, fields = pl.pallas_call(
        functools.partial(pack_raw_kernel, half, rows),
        out_shape=(
            jax.ShapeDtypeStruct((lengths[0] + 3 * rows, lanes), jnp.float32),
            jax.ShapeDtypeStruct((3 * rows, lanes), jnp.float32),
        ),
        in_specs=[anywhere] * 4,
        out_specs=(whole, whole),
        scratch_shapes=[pltpu.VMEM((3, rows, lanes), jnp.int32), pltpu.SemaphoreType.DMA((2, max(n_lon, 3)))],
        compiler_params=params(),
        cost_estimate=cost(1),
    )(*[pltpu.with_memory_space_constraint(a, pltpu.HBM) for a in (flat, sea_mask, depth_class, current_class)])
    own_in, own_fields = on_all_columns(flat), on_all_columns(fields)
    blocks = [first_block]
    if len(sizes) > 1:
        blocks += pl.pallas_call(
            functools.partial(pack_kernel, starts[1:], half, rows),
            out_shape=[jax.ShapeDtypeStruct((length, lanes), jnp.float32) for length in lengths[1:]],
            in_specs=[scalars, [anywhere] * n_lon, [anywhere] * (n_lon + 1)],
            out_specs=[whole] * len(lengths[1:]),
            scratch_shapes=[pltpu.SemaphoreType.DMA((len(lengths) - 1, n_lon))],
            compiler_params=params(),
            cost_estimate=cost(1.5),
        )(place, own_in, [first_block] + own_fields)
    lat_in = [[lax.ppermute(block, "lat", move) for move in moves] for block in blocks]

    def home_of(place, s):
        return lax.rem(place[1] + n_comp - s, n_comp) if split else s

    total = n_comp * n_lon * half
    block = n_lon * half

    def spread(array):
        if half == half_own:
            return array
        array = array.reshape(array.shape[:-1] + (n_comp * n_lon, half_own))
        array = jnp.pad(array, ((0, 0),) * (array.ndim - 1) + ((0, half - half_own),), constant_values=-1)
        return array.reshape(array.shape[:-2] + (total,))

    names = spread(jnp.arange(n_comp * comps_local, dtype=jnp.float32)[None])
    index = spread(jnp.swapaxes(quad_index, 1, 2).astype(jnp.float32))
    weight = jnp.maximum(spread(jnp.swapaxes(quad_weight, 1, 2)), 0.0)
    strength = spread(coupling[None]).reshape(total, 1)
    by_cols = pl.BlockSpec((1, 4, total), lambda s, i: (s, 0, 0))
    by_block = pl.BlockSpec((1, block, total), lambda s, i: (s, i, 0))
    matrix = pl.pallas_call(
        functools.partial(matrix_kernel, home_of),
        grid=(2, n_comp),
        out_shape=pltpu.VMEM((2, total, total), jnp.bfloat16),
        in_specs=[scalars, whole, by_cols, by_cols, [anywhere] * 2],
        out_specs=by_block,
        scratch_shapes=[pltpu.VMEM((total, 8), jnp.float32)],
        compiler_params=params(),
        cost_estimate=cost(6),
    )(place, names, index, weight, [blocks[-1], strength])

    lat_in[0] = [on_all_columns(block) for block in gated(lat_in[0], [matrix])]
    lat_in[1:] = [[[block] for block in found] for found in lat_in[1:]]

    n_class = speed_table.shape[0]
    head_block = pl.BlockSpec((3 * rows, lanes), lambda i: (0, 0))
    faces, window_fields = pl.pallas_call(
        functools.partial(faces_kernel, window, n_lon),
        grid=(1,),
        out_shape=(
            jax.ShapeDtypeStruct((window.size, 2, 6 * n_class, width), jnp.bfloat16),
            jax.ShapeDtypeStruct((window.size, 3, width), jnp.float32),
        ),
        in_specs=[scalars, [whole] * n_lon, [[head_block] * n_lon] * len(moves), anywhere],
        out_specs=(whole, whole),
        compiler_params=params(),
        cost_estimate=cost(2),
    )(place, own_fields, lat_in[0], matrix)

    ids = comp * comps_local + lon * half_own + jnp.arange(half, dtype=jnp.int32)
    freq_hot = ((ids // NDIR)[:, None] == jnp.arange(speed_table.shape[1], dtype=jnp.int32)[None, :]).astype(
        jnp.float32
    )
    speed = jnp.dot(freq_hot, speed_table.T, precision=lax.Precision.HIGHEST)
    angles = 2.0 * math.pi / NDIR * (ids % NDIR).astype(jnp.float32)
    tables = []
    for which, turn in ((0, jnp.cos(angles)), (1, jnp.sin(angles))):
        currents = jnp.broadcast_to(current_table[:, which][None], (half, n_class))
        left = jnp.concatenate([speed * turn[:, None], currents], axis=1)
        levels = []
        for _ in range(3):
            level = lax.reduce_precision(left, 8, 7)
            levels.append(level)
            left = left - level
        tables.append(jnp.concatenate(levels, axis=1).astype(jnp.bfloat16))
    tables = jnp.stack(tables)

    if split:
        share, span = rows // n_comp, lanes
    else:
        groups = n_comp // rows
        share, span = 1, lanes // groups
    far_first = sorted(range(1, n_comp), key=lambda r: abs(2 * r - n_comp))
    order = [0] + far_first
    arrived = []
    for i, (start, size) in enumerate(zip(starts, sizes)):
        table = lax.slice_in_dim(tables, start, start + size, axis=1)
        if split:
            shapes = [jax.ShapeDtypeStruct((n_lon, share, size, lanes), jnp.float32)] * n_comp
        else:
            shapes = [jax.ShapeDtypeStruct((rows, n_lon, size, lanes), jnp.float32)]
        pieces = pl.pallas_call(
            functools.partial(
                propagate_kernel, window, n_lon, n_comp, split, start, half, 0 if i else 3
            ),
            out_shape=shapes,
            in_specs=[
                scalars,
                whole,
                whole,
                whole,
                [whole] * n_lon,
                [[whole] * len(found) for found in lat_in[i]],
                anywhere,
            ],
            out_specs=[whole] * len(shapes),
            scratch_shapes=propagate_scratch(window, size, lanes, n_lon),
            compiler_params=params(),
            cost_estimate=cost(1.5 + 0.11 * size),
        )(
            place,
            table,
            faces,
            window_fields,
            own_in,
            lat_in[i],
            matrix if i == 0 else pieces[0],
        )
        if split:
            sent = pieces[1:]
            if i > 0:
                sent = gated(sent, [moved[r] for r in far_first[:2]])
            moved = [pieces[0]] + [None] * (n_comp - 1)
            for r in far_first:
                pairs = [(a, (a + r) % n_comp) for a in range(n_comp)]
                moved[r] = lax.ppermute(sent[r - 1], "comp", pairs)
        else:
            energy = pieces[0].reshape(rows, n_lon, size, groups, span)
            energy = jnp.transpose(energy, (0, 3, 1, 2, 4)).reshape(n_comp, n_lon, 1, size, span)
            energy = lax.all_to_all(energy, "comp", split_axis=0, concat_axis=0, tiled=True)
            moved = [energy[s] for s in range(n_comp)]
        after = []
        if i == len(sizes) - 1:
            matrix_t = pl.pallas_call(
                functools.partial(transposed_kernel, home_of, half, half_own),
                grid=(2, n_comp),
                out_shape=pltpu.VMEM((2, total, total), jnp.bfloat16),
                in_specs=[scalars, by_cols, by_cols, anywhere],
                out_specs=by_block,
                compiler_params=params(),
                cost_estimate=cost(4),
            )(place, index, weight, pieces[0])
            after = [matrix_t]
        crossed = []
        for d in range(1, n_lon):
            pairs = [(b, (b + d) % n_lon) for b in range(n_lon)]
            packed = pl.pallas_call(
                functools.partial(cross_pack_kernel, d),
                out_shape=jax.ShapeDtypeStruct((n_comp, share, size, span), jnp.float32),
                in_specs=[[anywhere] * n_comp, [anywhere] * len(after)],
                out_specs=whole,
                scratch_shapes=[pltpu.SemaphoreType.DMA((n_comp,))],
                compiler_params=params(),
                cost_estimate=cost(1),
            )(moved, after)
            crossed.append(lax.ppermute(packed, "lon", pairs))
        arrived += moved + crossed

    cells = share * span
    energy, source, source_low = pl.pallas_call(
        functools.partial(forward_kernel, sizes, n_lon, home_of),
        out_shape=(
            jax.ShapeDtypeStruct((total, cells), jnp.float32),
            jax.ShapeDtypeStruct((total, cells), jnp.float32),
            jax.ShapeDtypeStruct((total, cells), jnp.bfloat16),
        ),
        in_specs=[scalars, whole, whole] + [whole] * len(arrived),
        out_specs=(whole, whole, whole),
        scratch_shapes=[pltpu.VMEM((total, cells), jnp.bfloat16)],
        compiler_params=params(),
        cost_estimate=cost(4),
    )(place, matrix, strength, *arrived)

    back = []
    for s in range(n_comp):
        back.append(
            pl.pallas_call(
                functools.partial(backward_kernel, s),
                out_shape=jax.ShapeDtypeStruct((share, block, span), jnp.float32),
                in_specs=[whole] * 4,
                out_specs=whole,
                compiler_params=params(),
                cost_estimate=cost(0.6),
            )(matrix_t, source_low, energy, source)
        )

    if split:
        home = [back[0]] + [None] * (n_comp - 1)
        for r in far_first:
            home[r] = lax.ppermute(back[r], "comp", [(a, (a - r) % n_comp) for a in range(n_comp)])
        if half == half_own:
            held = []
            for some in (order[:2], order[2:]):
                held = [
                    pl.pallas_call(
                        functools.partial(gather_kernel, rows, n_comp, some),
                        out_shape=jax.ShapeDtypeStruct((comps_local * rows, lanes), jnp.float32),
                        in_specs=[scalars, [whole] * len(held)] + [whole] * len(some),
                        out_specs=whole,
                        compiler_params=params(),
                        cost_estimate=cost(1),
                    )(place, held, *[home[r] for r in some])
                ]
            out = held[0]
            return out.reshape(comps_local, rows, lanes)
        home = jnp.stack(home).reshape(n_comp, share, n_lon, half, lanes)[:, :, :, :half_own]
        home = jnp.roll(home, comp, 0)
        return jnp.transpose(home, (2, 3, 0, 1, 4)).reshape(comps_local, rows, lanes)
    home = lax.all_to_all(jnp.concatenate(back), "comp", split_axis=0, concat_axis=0, tiled=True)
    home = home.reshape(rows, groups, n_lon, half, span)[:, :, :, :half_own]
    return jnp.transpose(home, (2, 3, 0, 1, 4)).reshape(comps_local, rows, lanes)


def solution(mesh):
    placed = (
        P(("ens", "comp"), "lat", "lon"),
        P("lat", "lon"),
        P("lat", "lon"),
        P("lat", "lon"),
        P(),
        P(),
        P(),
        P(),
        P(),
    )
    return jax.shard_map(
        local,
        mesh=mesh,
        in_specs=placed,
        out_specs=P(("ens", "comp"), "lat", "lon"),
        check_vma=False,
    )
```
